128 devices in a mesh: member: 2 (over x_hi), space: 64 (over y, z, x_lo, core).
Axes of the slice: x: 4 (x_hi: 2, x_lo: 2; x = x_hi * 2 + x_lo), y: 4, z: 4, core: 2. Of those that a mesh axis runs over, the one named last changes fastest.
Arguments:
- mesh_latent: bfloat16 [8192, 512], P('space'), may hold values from -6 to 6
- grid_embed: bfloat16 [65536, 512], P('space'), may hold values from -6 to 6
- weather_state: float32 [84, 65536], P(None, 'space'), may hold values from -6 to 6
- target: float32 [84, 65536], P(None, 'space'), may hold values from -6 to 6
- cell_area: float32 [65536], P('space'), may hold values from 0.2 to 2
- member_noise: float32 [2, 32], P('member'), may hold values from -5 to 5
- mesh_nbrs: int32 [16, 8192], P(None, 'space'), may hold values from 0 to 8191, as said below
- mesh_bias: float32 [16, 8192], P(None, 'space'), may hold values from -2 to 300
- grid_nbrs: int32 [3, 65536], P(None, 'space'), may hold values from 0 to 8191, as said below
- grid_bias: float32 [3, 65536], P(None, 'space'), may hold values from -2 to 300
- grid_counts: int32 [64], P('space'), may hold values from 512 to 1024, as said below
- cond_scale: float32 [32, 512], replicated, may hold values from -0.5 to 0.5
- cond_shift: float32 [32, 512], replicated, may hold values from -0.5 to 0.5
- attn_qkv: bfloat16 [512, 1536], replicated, may hold values from -0.25 to 0.25
- attn_out: bfloat16 [512, 512], replicated, may hold values from -0.25 to 0.25
- dec_query: bfloat16 [512, 512], replicated, may hold values from -0.25 to 0.25
- dec_kv: bfloat16 [512, 1024], replicated, may hold values from -0.25 to 0.25
- dec_out: bfloat16 [512, 512], replicated, may hold values from -0.25 to 0.25
- head_out: bfloat16 [84, 512], replicated, may hold values from -0.25 to 0.25
Outputs:
- prediction: float32 [2, 84, 65536], P('member', None, 'space')
- grad_cond_scale: float32 [32, 512], replicated
- grad_cond_shift: float32 [32, 512], replicated
- grad_attn_qkv: float32 [512, 1536], replicated
- grad_attn_out: float32 [512, 512], replicated
- grad_dec_query: float32 [512, 512], replicated
- grad_dec_kv: float32 [512, 1024], replicated
- grad_dec_out: float32 [512, 512], replicated
- grad_head_out: float32 [84, 512], replicated
- loss: float32 [], replicated
The draws below stay inside these ranges and needn't reach their ends.
Inputs may be any that keep to these rules, and one draw needn't show every extreme that they name: `mesh_nbrs`: row 0 of column i is i itself. For the mesh nodes of the k-th aligned block of 128, every entry lies in the cyclic window of mesh nodes from k * 128 - 64 to (k + 1) * 128 + 63, modulo 8192. `grid_nbrs`: for the grid slots of the k-th aligned block of 1024, every entry lies in the cyclic window of mesh nodes from k * 128 - 64 to (k + 1) * 128 + 63, modulo 8192. `grid_counts`: entry k counts the live slots of the k-th aligned block of 1024 grid slots, which are its first ones; some entry equals 1024.
All inputs are finite; a program needn't handle non-finite values.
Results may differ from the reference program's by a relative error of at most 0.033.
Values may be sent and summed in bfloat16 or wider, within the bound.
No kernel may reach another device: no remote copies, remote signals or barrier semaphores. Data moves between devices by JAX's collectives and lax.ppermute only.
A program may use at most 128 MiB of HBM per device.

```python
import math
import jax
import jax.numpy as jnp
from jax import lax

D = 512
HEAD = 128
C = 84
NZ = 32
KNB = 16
DEC = 3
M_DEV = 128
G_DEV = 1024
HALO = 64
MESH = 8192
GRID = 65536
PARTS_SIZE = 64


def draw_mesh_nbrs(key, part):
    key = jax.random.fold_in(key, 11)
    node_ids = jnp.arange(MESH, dtype=jnp.int32)
    window_start = node_ids // M_DEV * M_DEV - HALO
    offsets = jax.random.randint(key, (KNB, MESH), 0, M_DEV + 2 * HALO, dtype=jnp.int32)
    listed = (window_start[None, :] + offsets) % MESH
    first_row = jnp.arange(KNB, dtype=jnp.int32)[:, None] == 0
    return jnp.where(first_row, node_ids[None, :], listed).astype(jnp.int32)


def draw_grid_nbrs(key, part):
    key = jax.random.fold_in(key, 12)
    slot_ids = jnp.arange(GRID, dtype=jnp.int32)
    window_start = slot_ids // G_DEV * M_DEV - HALO
    offsets = jax.random.randint(key, (DEC, GRID), 0, M_DEV + 2 * HALO, dtype=jnp.int32)
    return ((window_start[None, :] + offsets) % MESH).astype(jnp.int32)


def draw_grid_counts(key, part):
    key = jax.random.fold_in(key, 13)
    subkeys = jax.random.split(key, 2)
    counts = jax.random.randint(subkeys[0], (PARTS_SIZE,), G_DEV // 2, G_DEV + 1, dtype=jnp.int32)
    chosen = jax.random.randint(subkeys[1], (), 0, PARTS_SIZE, dtype=jnp.int32)
    return jnp.where(jnp.arange(PARTS_SIZE, dtype=jnp.int32) == chosen, G_DEV, counts).astype(jnp.int32)


def draw_mesh_bias(key, part):
    key = jax.random.fold_in(key, 14)
    subkeys = jax.random.split(key, 1)
    drawn = jax.random.uniform(subkeys[0], (KNB, MESH), jnp.float32, -2.0, 2.0)
    return drawn


def draw_grid_bias(key, part):
    key = jax.random.fold_in(key, 15)
    subkeys = jax.random.split(key, 1)
    drawn = jax.random.uniform(subkeys[0], (DEC, GRID), jnp.float32, -2.0, 2.0)
    return drawn


def levels(rng, extent, cuts, low, high):
    def one(dim, blocks):
        steps = jax.random.uniform(jax.random.fold_in(jax.random.fold_in(rng, 6), dim), (blocks,), jnp.float32, low / len(cuts), high / len(cuts))
        return jnp.repeat(jnp.exp(steps), extent[dim] // blocks).reshape((-1,) + (1,) * (len(extent) - dim - 1))

    factor_of = one(*cuts[0])
    for cut in cuts[1:]:
        factor_of = factor_of * one(*cut)
    return factor_of


def gaussian(stream_key, dims, scale, limit, cuts=(), kind=jnp.bfloat16):
    factor_of = levels(stream_key, dims, cuts, -0.22, 0.18) if cuts else 1.0
    values = jax.random.normal(stream_key, dims, jnp.float32) * scale * factor_of
    return jnp.minimum(jnp.maximum(values, -limit), limit).astype(kind)


def setup_inputs(seed: int = 0) -> dict:
    arg_keys = jax.random.split(jax.random.key(seed), 20)
    mesh_latent = gaussian(arg_keys[0], (MESH, D), 1.0, 6.0, ((0, 64),))
    grid_embed = gaussian(arg_keys[1], (GRID, D), 1.0, 6.0, ((0, 64),))
    weather_state = gaussian(arg_keys[2], (C, GRID), 1.0, 6.0, ((1, 64),), jnp.float32)
    target = gaussian(arg_keys[3], (C, GRID), 1.0, 6.0, ((1, 64),), jnp.float32)
    cell_area = jnp.clip(jnp.exp(math.log(2.0) - 2.3025851 * jax.random.uniform(arg_keys[4], (GRID,), jnp.float32) ** levels(arg_keys[4], (GRID,), ((0, 64),), -0.2, 0.2)), 0.2, 2.0)
    member_noise = gaussian(arg_keys[5], (2, NZ), 1.0, 5.0, ((0, 2),), jnp.float32)
    mesh_nbrs = draw_mesh_nbrs(jax.random.fold_in(arg_keys[19], 71), 0)
    mesh_bias = draw_mesh_bias(jax.random.fold_in(arg_keys[19], 71), 0)
    grid_nbrs = draw_grid_nbrs(jax.random.fold_in(arg_keys[19], 71), 0)
    grid_bias = draw_grid_bias(jax.random.fold_in(arg_keys[19], 71), 0)
    grid_counts = draw_grid_counts(jax.random.fold_in(arg_keys[19], 71), 0)
    cond_scale = gaussian(arg_keys[11], (NZ, D), (4 * NZ) ** -0.5, 0.5, (), jnp.float32)
    cond_shift = gaussian(arg_keys[12], (NZ, D), (4 * NZ) ** -0.5, 0.5, (), jnp.float32)
    attn_qkv = gaussian(arg_keys[13], (D, 3 * D), D ** -0.5, 0.25)
    attn_out = gaussian(arg_keys[14], (D, D), D ** -0.5, 0.25)
    dec_query = gaussian(arg_keys[15], (D, D), D ** -0.5, 0.25)
    dec_kv = gaussian(arg_keys[16], (D, 2 * D), D ** -0.5, 0.25)
    dec_out = gaussian(arg_keys[17], (D, D), D ** -0.5, 0.25)
    head_out = gaussian(arg_keys[18], (C, D), D ** -0.5, 0.25)
    return {"mesh_latent": mesh_latent, "grid_embed": grid_embed, "weather_state": weather_state, "target": target, "cell_area": cell_area, "member_noise": member_noise, "mesh_nbrs": mesh_nbrs, "mesh_bias": mesh_bias, "grid_nbrs": grid_nbrs, "grid_bias": grid_bias, "grid_counts": grid_counts, "cond_scale": cond_scale, "cond_shift": cond_shift, "attn_qkv": attn_qkv, "attn_out": attn_out, "dec_query": dec_query, "dec_kv": dec_kv, "dec_out": dec_out, "head_out": head_out}


EPSILON = 1e-05
LOSS_SCALE = 65536.0
SMOOTHING = 0.0625

def smooth_size(values):
    return jnp.sqrt(values * values + SMOOTHING)

def smooth_slope(values):
    return values / jnp.sqrt(values * values + SMOOTHING)

def normalize(values):
    values = values.astype(jnp.float32)
    center = values - lax.optimization_barrier(jnp.mean(values, axis=-1, keepdims=True))
    spread = lax.optimization_barrier(jnp.mean(center * center, axis=-1, keepdims=True))
    return center * lax.rsqrt(spread + EPSILON)

def normalize_back(values, grad_out):
    return jax.vjp(normalize, values.astype(jnp.float32))[1](grad_out)[0]

def left_product(first, second):
    return lax.dot_general(first, second, (((0,), (0,)), ((), ())), preferred_element_type=jnp.float32)

def right_product(first, second):
    return lax.dot_general(first, second, (((1,), (1,)), ((), ())), preferred_element_type=jnp.float32)

def split_heads(queries, gathered):
    row_count, feature_dim = queries.shape
    nbr_count = gathered.shape[0]
    head_count = feature_dim // HEAD
    query_heads = queries.reshape(row_count, head_count, HEAD).astype(jnp.float32)
    key_heads = gathered[:, :, :feature_dim].reshape(nbr_count, row_count, head_count, HEAD).astype(jnp.float32)
    value_heads = gathered[:, :, feature_dim:].reshape(nbr_count, row_count, head_count, HEAD).astype(jnp.float32)
    return (query_heads, key_heads, value_heads)

def attend(queries, gathered, bias_rows):
    row_count, feature_dim = queries.shape
    query_heads, key_heads, value_heads = split_heads(queries, gathered)
    scores = jnp.einsum('rhe,jrhe->jrh', query_heads, key_heads) / math.sqrt(HEAD) + bias_rows[:, :, None]
    row_max = lax.optimization_barrier(jnp.max(scores, axis=0, keepdims=True))
    exp_terms = jnp.exp(scores - row_max)
    attn_probs = exp_terms / lax.optimization_barrier(jnp.sum(exp_terms, axis=0, keepdims=True))
    attn_weights = attn_probs.astype(jnp.bfloat16)
    mixed_rows = jnp.einsum('jrh,jrhe->rhe', attn_weights.astype(jnp.float32), value_heads)
    return (mixed_rows.astype(jnp.bfloat16).reshape(row_count, feature_dim), attn_probs, attn_weights)

def attend_back(queries, gathered, attn_probs, attn_weights, grad_mixed):
    row_count, feature_dim = queries.shape
    nbr_count = gathered.shape[0]
    head_count = feature_dim // HEAD
    query_heads, key_heads, value_heads = split_heads(queries, gathered)
    grad_heads = grad_mixed.reshape(row_count, head_count, HEAD).astype(jnp.float32)
    grad_weights = jnp.einsum('rhe,jrhe->jrh', grad_heads, value_heads)
    grad_values = jnp.einsum('jrh,rhe->jrhe', attn_weights.astype(jnp.float32), grad_heads)
    grad_scores = attn_probs * (grad_weights - lax.optimization_barrier(jnp.sum(attn_probs * grad_weights, axis=0, keepdims=True))) / math.sqrt(HEAD)
    grad_scores = grad_scores.astype(jnp.bfloat16).astype(jnp.float32)
    grad_queries = jnp.einsum('jrh,jrhe->rhe', grad_scores, key_heads).reshape(row_count, feature_dim)
    grad_keys = jnp.einsum('jrh,rhe->jrhe', grad_scores, query_heads)
    grad_gathered = jnp.concatenate([grad_keys.reshape(nbr_count, row_count, feature_dim), grad_values.reshape(nbr_count, row_count, feature_dim)], axis=2)
    return (grad_queries, grad_gathered)

def block_attend(query_blocks, table, index_blocks, bias_blocks):

    def block_step(block):
        return attend(block[0], table[block[1]], block[2])[0]
    return lax.map(block_step, (query_blocks, index_blocks, bias_blocks))

def block_attend_back(query_blocks, table, index_blocks, bias_blocks, grad_blocks):

    def block_step(table_grad, block):
        query_block, index_block, bias_block, grad_block = block
        gathered = table[index_block]
        _, attn_probs, attn_weights = attend(query_block, gathered, bias_block)
        grad_query, grad_gathered = attend_back(query_block, gathered, attn_probs, attn_weights, grad_block)
        table_grad = table_grad.at[index_block.reshape(-1)].add(grad_gathered.reshape(-1, grad_gathered.shape[2]))
        return (table_grad, grad_query)
    return lax.scan(block_step, jnp.zeros(table.shape, jnp.float32), (query_blocks, index_blocks, bias_blocks, grad_blocks))

def reference(mesh_latent, grid_embed, weather_state, target, cell_area, member_noise, mesh_nbrs, mesh_bias, grid_nbrs, grid_bias, grid_counts, cond_scale, cond_shift, attn_qkv, attn_out, dec_query, dec_kv, dec_out, head_out):
    highest = lax.Precision.HIGHEST
    mesh_blocks = MESH // M_DEV
    grid_blocks = GRID // G_DEV
    slot_ids = jnp.arange(GRID, dtype=jnp.int32)
    live_slots = (slot_ids % G_DEV < grid_counts[(slot_ids // G_DEV).astype(jnp.int32)]).astype(jnp.float32)
    weighting = cell_area * live_slots
    scale_den = 2.0 * C * GRID
    mesh_index = mesh_nbrs.reshape(KNB, mesh_blocks, M_DEV).transpose(1, 0, 2)
    mesh_bias_blocks = mesh_bias.reshape(KNB, mesh_blocks, M_DEV).transpose(1, 0, 2)
    grid_index = grid_nbrs.reshape(DEC, grid_blocks, G_DEV).transpose(1, 0, 2)
    grid_bias_blocks = grid_bias.reshape(DEC, grid_blocks, G_DEV).transpose(1, 0, 2)
    latent_norm = normalize(mesh_latent)
    grid_norm = normalize(grid_embed).astype(jnp.bfloat16)
    grid_query = jnp.dot(grid_norm, dec_query, preferred_element_type=jnp.float32).astype(jnp.bfloat16)
    grid_query_blocks = grid_query.reshape(grid_blocks, G_DEV, D)
    saved = []
    for member in range(2):
        noise_row = member_noise[member]
        gain_row = 1.0 + jnp.dot(noise_row, cond_scale, precision=highest)
        shift_row = jnp.dot(noise_row, cond_shift, precision=highest)
        activation = (latent_norm * gain_row + shift_row).astype(jnp.bfloat16)
        qkv_rows = jnp.dot(activation, attn_qkv, preferred_element_type=jnp.float32).astype(jnp.bfloat16)
        query_rows = qkv_rows[:, :D]
        kv_table = qkv_rows[:, D:]
        mesh_mixed = block_attend(query_rows.reshape(mesh_blocks, M_DEV, D), kv_table, mesh_index, mesh_bias_blocks).reshape(MESH, D)
        mesh_out = (mesh_latent.astype(jnp.float32) + jnp.dot(mesh_mixed, attn_out, preferred_element_type=jnp.float32)).astype(jnp.bfloat16)
        mesh_norm = normalize(mesh_out).astype(jnp.bfloat16)
        dec_table = jnp.dot(mesh_norm, dec_kv, preferred_element_type=jnp.float32).astype(jnp.bfloat16)
        grid_mixed = block_attend(grid_query_blocks, dec_table, grid_index, grid_bias_blocks).reshape(GRID, D)
        grid_out = (grid_embed.astype(jnp.float32) + jnp.dot(grid_mixed, dec_out, preferred_element_type=jnp.float32)).astype(jnp.bfloat16)
        grid_final = normalize(grid_out).astype(jnp.bfloat16)
        change = right_product(head_out, grid_final)
        prediction = weather_state + live_slots * change
        saved.append((noise_row, activation, query_rows, kv_table, mesh_mixed, mesh_out, mesh_norm, dec_table, grid_mixed, grid_out, grid_final, prediction))
    grad_cond_scale = jnp.zeros((NZ, D), jnp.float32)
    grad_cond_shift = jnp.zeros((NZ, D), jnp.float32)
    grad_attn_qkv = jnp.zeros((D, 3 * D), jnp.float32)
    grad_attn_out = jnp.zeros((D, D), jnp.float32)
    grad_dec_query = jnp.zeros((D, D), jnp.float32)
    grad_dec_kv = jnp.zeros((D, 2 * D), jnp.float32)
    grad_dec_out = jnp.zeros((D, D), jnp.float32)
    grad_head_out = jnp.zeros((C, D), jnp.float32)
    loss = jnp.zeros((), jnp.float32)
    for member in range(2):
        noise_row, activation, query_rows, kv_table, mesh_mixed, mesh_out, mesh_norm, dec_table, grid_mixed, grid_out, grid_final, prediction = saved[member]
        partner_pred = saved[1 - member][11]
        loss = loss + jnp.sum(weighting * (smooth_size(prediction - target) - 0.5 * smooth_size(prediction - partner_pred))) / scale_den
        grad_change = (LOSS_SCALE * weighting * (smooth_slope(prediction - target) - smooth_slope(prediction - partner_pred)) / scale_den).astype(jnp.bfloat16)
        grad_head_out = grad_head_out + jnp.dot(grad_change, grid_final, preferred_element_type=jnp.float32)
        grad_final = left_product(grad_change, head_out)
        grad_grid_out = normalize_back(grid_out, grad_final).astype(jnp.bfloat16)
        grad_dec_out = grad_dec_out + left_product(grid_mixed, grad_grid_out)
        grad_grid_mixed = right_product(grad_grid_out, dec_out).astype(jnp.bfloat16)
        grad_dec_table, grad_query_blocks = block_attend_back(grid_query_blocks, dec_table, grid_index, grid_bias_blocks, grad_grid_mixed.reshape(grid_blocks, G_DEV, D))
        grad_dec_query = grad_dec_query + left_product(grid_norm, grad_query_blocks.reshape(GRID, D).astype(jnp.bfloat16))
        grad_dec_keys = grad_dec_table.astype(jnp.bfloat16)
        grad_dec_kv = grad_dec_kv + left_product(mesh_norm, grad_dec_keys)
        grad_mesh_norm = right_product(grad_dec_keys, dec_kv)
        grad_mesh_out = normalize_back(mesh_out, grad_mesh_norm).astype(jnp.bfloat16)
        grad_attn_out = grad_attn_out + left_product(mesh_mixed, grad_mesh_out)
        grad_mesh_mixed = right_product(grad_mesh_out, attn_out).astype(jnp.bfloat16)
        grad_kv_table, grad_mesh_queries = block_attend_back(query_rows.reshape(mesh_blocks, M_DEV, D), kv_table, mesh_index, mesh_bias_blocks, grad_mesh_mixed.reshape(mesh_blocks, M_DEV, D))
        grad_qkv = jnp.concatenate([grad_mesh_queries.reshape(MESH, D), grad_kv_table], axis=1).astype(jnp.bfloat16)
        grad_attn_qkv = grad_attn_qkv + left_product(activation, grad_qkv)
        grad_act = right_product(grad_qkv, attn_qkv)
        grad_gain = lax.optimization_barrier(jnp.sum(grad_act * latent_norm, axis=0))
        grad_shift = lax.optimization_barrier(jnp.sum(grad_act, axis=0))
        grad_cond_scale = grad_cond_scale + noise_row[:, None] * grad_gain[None, :]
        grad_cond_shift = grad_cond_shift + noise_row[:, None] * grad_shift[None, :]
    predictions = jnp.stack([saved[0][11], saved[1][11]], axis=0)
    return (predictions, grad_cond_scale, grad_cond_shift, grad_attn_qkv, grad_attn_out, grad_dec_query, grad_dec_kv, grad_dec_out, grad_head_out, loss)
```

```python
import math

import jax
import jax.numpy as jnp
from jax import lax
from jax.experimental import pallas as pl
from jax.experimental.pallas import tpu as pltpu
from jax.sharding import PartitionSpec as P

HEAD = 128
EPSILON = 1e-05
LOSS_SCALE = 65536.0
SMOOTHING = 0.0625
FAR = -1e30

F32 = jnp.float32
BF16 = jnp.bfloat16


def nn(first, second):
    return lax.dot_general(first, second, (((1,), (0,)), ((), ())), preferred_element_type=F32)


def nt(first, second):
    return lax.dot_general(first, second, (((1,), (1,)), ((), ())), preferred_element_type=F32)


def tn(first, second):
    return lax.dot_general(first, second, (((0,), (0,)), ((), ())), preferred_element_type=F32)


def normalize(values, axis):
    center = values - jnp.mean(values, axis=axis, keepdims=True)
    spread = jnp.mean(center * center, axis=axis, keepdims=True)
    scale = lax.rsqrt(spread + EPSILON)
    return center * scale, scale


def normalize_back(values, grad_out, axis):
    unit, scale = normalize(values, axis)
    mean_grad = jnp.mean(grad_out, axis=axis, keepdims=True)
    mean_unit = jnp.mean(grad_out * unit, axis=axis, keepdims=True)
    return scale * (grad_out - mean_grad - unit * mean_unit)


def spread_bias(slots, bias, rows):
    entries, width = slots.shape
    row_ids = lax.broadcasted_iota(jnp.int32, (rows, width), 0)
    logits = jnp.full((rows, width), FAR, F32)
    for entry in range(entries):
        same = slots == slots[entry : entry + 1]
        top = jnp.max(jnp.where(same, bias, FAR), axis=0, keepdims=True)
        terms = jnp.sum(jnp.where(same, jnp.exp(bias - top), 0.0), axis=0, keepdims=True)
        logits = jnp.where(row_ids == slots[entry : entry + 1], top + jnp.log(terms), logits)
    return logits


def softmax_rows(scores):
    terms = jnp.exp(scores - jnp.max(scores, axis=0, keepdims=True))
    return terms * (1.0 / jnp.sum(terms, axis=0, keepdims=True))


def score_back(probs, grad_probs):
    probs = probs.astype(F32)
    inner = jnp.sum(probs * grad_probs, axis=0, keepdims=True)
    return (probs * (grad_probs - inner) * (1.0 / math.sqrt(HEAD))).astype(BF16)


def prepare_kernel(
    place, embed, nbrs, bias, dec_query, embed_t, norm_t, query_t, logits, *, rows, halo, total
):
    values = embed[...].T
    embed_t[...] = values
    norm = normalize(values.astype(F32), 0)[0].astype(BF16)
    norm_t[...] = norm
    query_t[...] = tn(dec_query[...], norm).astype(BF16)
    local = (nbrs[...] - place[1]) & (total - 1)
    slots = jnp.where(local < halo, local + rows, jnp.where(local < halo + rows, local - halo, local))
    logits[...] = spread_bias(slots, bias[...], rows + 2 * halo)


def window_order(values, rows, halo):
    first = 2 * halo + halo
    return jnp.concatenate(
        [
            values[first : first + rows],
            values[first - halo : first],
            values[first + rows : first + rows + halo],
        ],
        axis=0,
    )


def step_kernel(
    place,
    own,
    before,
    after,
    before2,
    after2,
    edges,
    edges_before,
    edges_after,
    noise,
    embed_t,
    norm_t,
    query_t,
    grid_logits,
    weather,
    target,
    area,
    cond_scale,
    cond_shift,
    attn_qkv,
    attn_out,
    dec_kv,
    dec_out,
    head_out,
    pred_own,
    pred_other,
    grads,
    latent,
    unit_t,
    unit_q_t,
    mesh_logits,
    mesh_query,
    mesh_kv,
    mesh_probs,
    mesh_mixed,
    mesh_out,
    mesh_norm,
    dec_keys,
    grid_probs,
    grid_mixed,
    grid_out,
    grid_final,
    change,
    grad_change,
    head_pad,
    grad_dec,
    grad_kv,
    *,
    total,
    scale_den,
):
    rows, dim = own.shape
    halo = rows // 2
    window = rows + 2 * halo
    heads = dim // HEAD
    members = 2
    channels = weather.shape[0]
    slots = embed_t.shape[1]
    inv_sqrt = 1.0 / math.sqrt(HEAD)

    latent[0:halo] = before2[...]
    latent[halo : halo + rows] = before[...]
    latent[halo + rows : halo + 2 * rows] = own[...]
    latent[halo + 2 * rows : halo + 3 * rows] = after[...]
    latent[halo + 3 * rows :] = after2[...]
    unit = normalize(latent[...].astype(F32), 1)[0]
    unit_t[...] = unit.astype(BF16).T
    unit_q_t[...] = window_order(unit, rows, halo).astype(BF16).T

    lane = lax.broadcasted_iota(jnp.int32, edges.shape, 1)
    ends = pltpu.roll(jnp.where(lane >= halo, edges_before[...], edges_after[...]), halo, 1)
    entries = edges.shape[0] // 2
    lane = lane[:entries]
    own_slots = (edges[:entries].astype(jnp.int32) - place[1]) & (total - 1)
    end_start = place[1] + jnp.where(lane < halo, -rows, rows)
    end_slots = (ends[:entries].astype(jnp.int32) - end_start) & (total - 1)
    mesh_logits[...] = spread_bias(
        jnp.concatenate([own_slots, end_slots], axis=1),
        jnp.concatenate([edges[entries:], ends[entries:]], axis=1),
        window,
    )
    is_before = lax.broadcasted_iota(jnp.int32, (window, rows), 1) < halo

    def split_ends(values):
        values = values.astype(F32)
        return jnp.concatenate(
            [jnp.where(is_before, values, 0.0), jnp.where(is_before, 0.0, values)], axis=0
        ).astype(BF16)

    def window_scores(keys, queries):
        mid = nn(keys[rows : rows + window], queries[:, :rows])
        ends = nn(keys, queries[:, rows:])
        return jnp.concatenate([mid, jnp.where(is_before, ends[:window], ends[window:])], axis=1)

    gains = []
    shifts = []
    for m in range(members):
        noise_col = noise[:, m : m + 1]
        gains.append(1.0 + jnp.sum(noise_col * cond_scale[...], axis=0, keepdims=True))
        shifts.append(jnp.sum(noise_col * cond_shift[...], axis=0, keepdims=True))

    for m in range(members):
        act = (unit * gains[m] + shifts[m]).astype(BF16)
        mesh_kv[m] = nn(act, attn_qkv[:, dim:]).astype(BF16)
        act_q = window_order(act, rows, halo)
        mesh_query[m] = nn(act_q, attn_qkv[:, :dim]).astype(BF16).T
        for h in range(heads):
            cols = slice(h * HEAD, (h + 1) * HEAD)
            value_cols = slice(dim + h * HEAD, dim + (h + 1) * HEAD)
            scores = window_scores(mesh_kv[m, :, cols], mesh_query[m, cols, :])
            probs = softmax_rows(scores * inv_sqrt + mesh_logits[...]).astype(BF16)
            mesh_probs[m, h] = probs
            values = mesh_kv[m, :, value_cols]
            mid = tn(values[rows : rows + window], probs[:, :rows])
            ends = tn(values, split_ends(probs[:, rows:]))
            mesh_mixed[m, cols, :] = jnp.concatenate([mid, ends], axis=1).astype(BF16)
        residual = window_order(latent[...].astype(F32), rows, halo)
        out = (residual + nn(mesh_mixed[m].T, attn_out[...])).astype(BF16)
        mesh_out[m] = out
        norm = normalize(out.astype(F32), 1)[0].astype(BF16)
        mesh_norm[m] = norm
        dec_keys[m] = nn(norm, dec_kv[...]).astype(BF16)

    head_pad[...] = jnp.zeros_like(head_pad)
    head_pad[:channels] = head_out[...]
    for m in range(members):
        for h in range(heads):
            cols = slice(h * HEAD, (h + 1) * HEAD)
            value_cols = slice(dim + h * HEAD, dim + (h + 1) * HEAD)
            scores = nn(dec_keys[m, :, cols], query_t[cols, :])
            probs = softmax_rows(scores * inv_sqrt + grid_logits[...]).astype(BF16)
            grid_probs[m, h] = probs
            grid_mixed[m, cols, :] = tn(dec_keys[m, :, value_cols], probs).astype(BF16)
        out = (embed_t[...].astype(F32) + tn(dec_out[...], grid_mixed[m])).astype(BF16)
        grid_out[m] = out
        final = normalize(out.astype(F32), 0)[0].astype(BF16)
        grid_final[m] = final
        change[m] = nn(head_pad[...], final)

    slot = lax.broadcasted_iota(jnp.int32, (1, slots), 1) + place[0] * slots
    live = jnp.where(slot < place[2], 1.0, 0.0)
    weighting = live * area[...]
    first = weather[...] + live * change[0, :channels]
    second = weather[...] + live * change[1, :channels]
    pred_own[...] = first
    pred_other[...] = second

    def smooth(values):
        square = values * values + SMOOTHING
        inverse = lax.rsqrt(square)
        return square * inverse, values * inverse

    size_first, slope_first = smooth(first - target[...])
    size_second, slope_second = smooth(second - target[...])
    size_pair, slope_pair = smooth(first - second)
    loss = jnp.sum(weighting * (size_first + size_second - size_pair)) / scale_den
    factor = weighting * (LOSS_SCALE / scale_den)
    grad_change[...] = jnp.zeros_like(grad_change)
    grad_change[0, :channels] = (factor * (slope_first - slope_pair)).astype(BF16)
    grad_change[1, :channels] = (factor * (slope_second + slope_pair)).astype(BF16)

    grad_head = None
    grad_dec_out = None
    grad_query = None
    for m in range(members):
        g_change = grad_change[m]
        term = nt(g_change, grid_final[m])
        grad_head = term if m == 0 else grad_head + term
        g_final = tn(head_pad[...], g_change)
        g_out = normalize_back(grid_out[m].astype(F32), g_final, 0).astype(BF16)
        term = nt(grid_mixed[m], g_out)
        grad_dec_out = term if m == 0 else grad_dec_out + term
        g_mixed = nn(dec_out[...], g_out).astype(BF16)
        terms = []
        for h in range(heads):
            cols = slice(h * HEAD, (h + 1) * HEAD)
            value_cols = slice(dim + h * HEAD, dim + (h + 1) * HEAD)
            g_head = g_mixed[cols, :]
            probs = grid_probs[m, h]
            g_scores = score_back(probs, nn(dec_keys[m, :, value_cols], g_head))
            terms.append(tn(dec_keys[m, :, cols], g_scores))
            grad_dec[m, :, cols] = nt(g_scores, query_t[cols, :]).astype(BF16)
            grad_dec[m, :, value_cols] = nt(probs, g_head).astype(BF16)
        term = jnp.concatenate(terms, axis=0)
        grad_query = term if m == 0 else grad_query + term
    grad_dec_query = nt(norm_t[...], grad_query.astype(BF16))

    grad_dec_kv = None
    grad_attn_out = None
    grad_qkv = None
    grad_scale = None
    grad_shift = None
    for m in range(members):
        g_dec = grad_dec[m]
        term = tn(mesh_norm[m], g_dec)
        grad_dec_kv = term if m == 0 else grad_dec_kv + term
        g_norm = nt(g_dec, dec_kv[...])
        g_out = normalize_back(mesh_out[m].astype(F32), g_norm, 1).astype(BF16)
        term = nn(mesh_mixed[m], g_out)
        grad_attn_out = term if m == 0 else grad_attn_out + term
        g_mixed = nt(attn_out[...], g_out).astype(BF16)
        g_queries = []
        for h in range(heads):
            cols = slice(h * HEAD, (h + 1) * HEAD)
            value_cols = slice(dim + h * HEAD, dim + (h + 1) * HEAD)
            g_head = g_mixed[cols, :]
            probs = mesh_probs[m, h]
            keys = mesh_kv[m, :, cols]
            g_scores = score_back(probs, window_scores(mesh_kv[m, :, value_cols], g_head))
            g_ends = split_ends(g_scores[:, rows:])
            mid = tn(keys[rows : rows + window], g_scores[:, :rows])
            ends = tn(keys, g_ends)
            g_queries.append(jnp.concatenate([mid, ends], axis=1))
            queries = mesh_query[m, cols, :]
            grad_kv[:, cols] = nt(g_ends, queries[:, rows:])
            grad_kv[rows : rows + window, cols] += nt(g_scores[:, :rows], queries[:, :rows])
            grad_kv[:, value_cols] = nt(split_ends(probs[:, rows:]), g_head[:, rows:])
            grad_kv[rows : rows + window, value_cols] += nt(probs[:, :rows], g_head[:, :rows])
        g_kv = grad_kv[...].astype(BF16)
        g_query = jnp.concatenate(g_queries, axis=0).astype(BF16).T
        moment = jnp.concatenate([nn(unit_q_t[...], g_query), nn(unit_t[...], g_kv)], axis=1)
        col_sum = jnp.concatenate(
            [
                jnp.sum(g_query.astype(F32), axis=0, keepdims=True),
                jnp.sum(g_kv.astype(F32), axis=0, keepdims=True),
            ],
            axis=1,
        )
        gain_col = jnp.broadcast_to(gains[m], (HEAD, dim)).T[:, :1]
        shift_col = jnp.broadcast_to(shifts[m], (HEAD, dim)).T[:, :1]
        term = gain_col * moment + shift_col * col_sum
        grad_qkv = term if m == 0 else grad_qkv + term
        weight = attn_qkv[...].astype(F32)
        g_gain = jnp.sum(weight * moment, axis=1, keepdims=True)
        g_shift = jnp.sum(weight * col_sum, axis=1, keepdims=True)
        noise_col = noise[:, m : m + 1]
        spread = noise.shape[0]
        term = noise_col * jnp.broadcast_to(g_gain, (dim, HEAD)).T[:spread]
        grad_scale = term if m == 0 else grad_scale + term
        term = noise_col * jnp.broadcast_to(g_shift, (dim, HEAD)).T[:spread]
        grad_shift = term if m == 0 else grad_shift + term

    row = 0
    for block in (
        grad_qkv[:, :dim],
        grad_qkv[:, dim : 2 * dim],
        grad_qkv[:, 2 * dim :],
        grad_attn_out,
        grad_dec_query,
        grad_dec_kv[:, :dim],
        grad_dec_kv[:, dim:],
        grad_dec_out,
        grad_scale,
        grad_shift,
        grad_head,
    ):
        grads[row : row + block.shape[0]] = block.astype(grads.dtype)
        row += block.shape[0]
    rest = grads.shape[0] - row
    tail_row = lax.broadcasted_iota(jnp.int32, (rest, dim), 0)
    grads[row:] = jnp.where(tail_row == 0, loss, 0.0).astype(grads.dtype)


def whole(shape):
    return pl.BlockSpec(shape, lambda *_: (0,) * len(shape))


def per_device(
    mesh_latent,
    grid_embed,
    weather_state,
    target,
    cell_area,
    member_noise,
    mesh_nbrs,
    mesh_bias,
    grid_nbrs,
    grid_bias,
    grid_counts,
    cond_scale,
    cond_shift,
    attn_qkv,
    attn_out,
    dec_query,
    dec_kv,
    dec_out,
    head_out,
):
    rows, dim = mesh_latent.shape
    halo = rows // 2
    window = rows + 2 * halo
    outer = 2 * window
    size = lax.axis_size("space")
    grid_slots = grid_embed.shape[0]
    slots = grid_slots // 2
    channels = weather_state.shape[0]
    total = rows * size
    heads = dim // HEAD
    noise_size = member_noise.shape[1]
    entries = grid_nbrs.shape[0]
    scale_den = 2.0 * channels * grid_slots * size

    member = lax.axis_index("member")
    start = lax.axis_index("space") * rows - halo
    place = jnp.stack([member, start, grid_counts[0]]).astype(jnp.int32)

    def shift(value, hops):
        pairs = [(i, (i + hops) % size) for i in range(size)]
        return lax.ppermute(value, "space", pairs)

    swap = [(0, 1), (1, 0)]
    edges = jnp.concatenate([mesh_nbrs.astype(F32), mesh_bias], axis=0)
    before = shift(mesh_latent, 1)
    after = shift(mesh_latent, -1)
    before2 = shift(mesh_latent[halo:], 2)
    after2 = shift(mesh_latent[:halo], -2)
    edges_before = shift(edges, 1)
    edges_after = shift(edges, -1)
    other_noise = lax.ppermute(member_noise, "member", swap)
    noise = jnp.concatenate([member_noise, other_noise], axis=0).T

    part = pl.BlockSpec((slots, dim), lambda i, place: (place[0], 0))
    lists = pl.BlockSpec((entries, slots), lambda i, place: (0, place[0]))
    square = (dim, slots)
    embed_t, norm_t, query_t, grid_logits = pl.pallas_call(
        lambda *refs: prepare_kernel(*refs, rows=rows, halo=halo, total=total),
        grid_spec=pltpu.PrefetchScalarGridSpec(
            num_scalar_prefetch=1,
            grid=(1,),
            in_specs=[part, lists, lists, whole((dim, dim))],
            out_specs=[whole(square), whole(square), whole(square), whole((window, slots))],
        ),
        out_shape=[
            jax.ShapeDtypeStruct(square, BF16),
            jax.ShapeDtypeStruct(square, BF16),
            jax.ShapeDtypeStruct(square, BF16),
            jax.ShapeDtypeStruct((window, slots), F32),
        ],
        compiler_params=pltpu.CompilerParams(vmem_limit_bytes=40 * 2**20),
        cost_estimate=pl.CostEstimate(
            flops=2 * dim * dim * slots, bytes_accessed=3 * 2**20, transcendentals=0
        ),
        name="prepare",
    )(place, grid_embed, grid_nbrs, grid_bias, dec_query)

    channel_pad = -(-channels // 32) * 32
    grad_rows = 8 * dim + 2 * noise_size + channel_pad + 16
    grad_rows = -(-grad_rows // 256) * 256
    fields = pl.BlockSpec((channels, slots), lambda i, place: (0, place[0]))
    operands = (
        mesh_latent,
        before,
        after,
        before2,
        after2,
        edges,
        edges_before,
        edges_after,
        noise,
        embed_t,
        norm_t,
        query_t,
        grid_logits,
        weather_state,
        target,
        cell_area[None, :],
        cond_scale,
        cond_shift,
        attn_qkv,
        attn_out,
        dec_kv,
        dec_out,
        head_out,
    )
    specs = [whole(value.shape) for value in operands]
    specs[13] = fields
    specs[14] = fields
    specs[15] = pl.BlockSpec((1, slots), lambda i, place: (0, place[0]))
    pred_own, pred_other, grads = pl.pallas_call(
        lambda *refs: step_kernel(*refs, total=total, scale_den=scale_den),
        grid_spec=pltpu.PrefetchScalarGridSpec(
            num_scalar_prefetch=1,
            grid=(1,),
            in_specs=specs,
            out_specs=[
                whole((channels, slots)),
                whole((channels, slots)),
                whole((grad_rows, dim)),
            ],
            scratch_shapes=[
                pltpu.VMEM((outer, dim), BF16),
                pltpu.VMEM((dim, outer), BF16),
                pltpu.VMEM((dim, window), BF16),
                pltpu.VMEM((window, window), F32),
                pltpu.VMEM((2, dim, window), BF16),
                pltpu.VMEM((2, outer, 2 * dim), BF16),
                pltpu.VMEM((2, heads, window, window), BF16),
                pltpu.VMEM((2, dim, window), BF16),
                pltpu.VMEM((2, window, dim), BF16),
                pltpu.VMEM((2, window, dim), BF16),
                pltpu.VMEM((2, window, 2 * dim), BF16),
                pltpu.VMEM((2, heads, window, slots), BF16),
                pltpu.VMEM((2, dim, slots), BF16),
                pltpu.VMEM((2, dim, slots), BF16),
                pltpu.VMEM((2, dim, slots), BF16),
                pltpu.VMEM((2, channel_pad, slots), F32),
                pltpu.VMEM((2, channel_pad, slots), BF16),
                pltpu.VMEM((channel_pad, dim), BF16),
                pltpu.VMEM((2, window, 2 * dim), BF16),
                pltpu.VMEM((outer, 2 * dim), F32),
            ],
        ),
        out_shape=[
            jax.ShapeDtypeStruct((channels, slots), F32),
            jax.ShapeDtypeStruct((channels, slots), F32),
            jax.ShapeDtypeStruct((grad_rows, dim), BF16),
        ],
        compiler_params=pltpu.CompilerParams(vmem_limit_bytes=56 * 2**20),
        cost_estimate=pl.CostEstimate(
            flops=10**10, bytes_accessed=12 * 2**20, transcendentals=2**21
        ),
        name="step",
    )(place, *operands)

    arrived = lax.ppermute(pred_other, "member", swap)
    lower = jnp.where(member == 0, pred_own, arrived)
    upper = jnp.where(member == 0, arrived, pred_own)
    prediction = jnp.concatenate([lower, upper], axis=1)[None]

    axes = ("member", "space")
    summed = lax.psum(grads, axes).astype(F32)
    blocks = [summed[i * dim : (i + 1) * dim] for i in range(8)]
    row = 8 * dim
    scale_grad = summed[row : row + noise_size]
    shift_grad = summed[row + noise_size : row + 2 * noise_size]
    row += 2 * noise_size
    head_grad = summed[row : row + channels]
    loss = summed[row + channel_pad, 0]
    return (
        prediction,
        scale_grad,
        shift_grad,
        jnp.concatenate(blocks[:3], axis=1),
        blocks[3],
        blocks[4],
        jnp.concatenate(blocks[5:7], axis=1),
        blocks[7],
        head_grad,
        loss,
    )


def solution(mesh):
    in_specs = (
        P("space", None),
        P("space", None),
        P(None, "space"),
        P(None, "space"),
        P("space"),
        P("member", None),
        P(None, "space"),
        P(None, "space"),
        P(None, "space"),
        P(None, "space"),
        P("space"),
        P(),
        P(),
        P(),
        P(),
        P(),
        P(),
        P(),
        P(),
    )
    out_specs = (P("member", None, "space"), P(), P(), P(), P(), P(), P(), P(), P(), P())
    return jax.shard_map(
        per_device, mesh=mesh, in_specs=in_specs, out_specs=out_specs, check_vma=False
    )
```

```python
import math

import jax
import jax.numpy as jnp
from jax import lax
from jax.experimental import pallas as pl
from jax.experimental.pallas import tpu as pltpu
from jax.sharding import PartitionSpec as P

HEAD = 128
EPSILON = 1e-05
LOSS_SCALE = 65536.0
SMOOTHING = 0.0625
FAR = -1e30

F32 = jnp.float32
BF16 = jnp.bfloat16


def nn(first, second):
    return lax.dot_general(first, second, (((1,), (0,)), ((), ())), preferred_element_type=F32)


def nt(first, second):
    return lax.dot_general(first, second, (((1,), (1,)), ((), ())), preferred_element_type=F32)


def tn(first, second):
    return lax.dot_general(first, second, (((0,), (0,)), ((), ())), preferred_element_type=F32)


def normalize(values, axis):
    center = values - jnp.mean(values, axis=axis, keepdims=True)
    spread = jnp.mean(center * center, axis=axis, keepdims=True)
    scale = lax.rsqrt(spread + EPSILON)
    return center * scale, scale


def normalize_back(values, grad_out, axis):
    unit, scale = normalize(values, axis)
    mean_grad = jnp.mean(grad_out, axis=axis, keepdims=True)
    mean_unit = jnp.mean(grad_out * unit, axis=axis, keepdims=True)
    return scale * (grad_out - mean_grad - unit * mean_unit)


def spread_bias(slots, bias, rows):
    entries, width = slots.shape
    row_ids = lax.broadcasted_iota(jnp.int32, (rows, width), 0)
    logits = jnp.full((rows, width), FAR, F32)
    for entry in range(entries):
        same = slots == slots[entry : entry + 1]
        top = jnp.max(jnp.where(same, bias, FAR), axis=0, keepdims=True)
        terms = jnp.sum(jnp.where(same, jnp.exp(bias - top), 0.0), axis=0, keepdims=True)
        logits = jnp.where(row_ids == slots[entry : entry + 1], top + jnp.log(terms), logits)
    return logits


def softmax_rows(scores):
    terms = jnp.exp(scores - jnp.max(scores, axis=0, keepdims=True))
    return terms * (1.0 / jnp.sum(terms, axis=0, keepdims=True))


def score_back(probs, grad_probs):
    probs = probs.astype(F32)
    inner = jnp.sum(probs * grad_probs, axis=0, keepdims=True)
    return (probs * (grad_probs - inner) * (1.0 / math.sqrt(HEAD))).astype(BF16)


def split_terms(values):
    high = values.astype(BF16)
    rest = values - high.astype(F32)
    middle = rest.astype(BF16)
    low = (rest - middle.astype(F32)).astype(BF16)
    return high, middle, low


def joined_terms(high, middle, low):
    return high.astype(F32) + (middle.astype(F32) + low.astype(F32))


def pack_kernel(place, latent, nbrs, bias, noise, packet, upward, *, total):
    rows = latent.shape[0]
    halo = rows // 2
    packet[:rows] = latent[...]
    slots = ((nbrs[...] - place[1]) & (total - 1)).astype(F32).astype(BF16)
    packet[rows:] = jnp.concatenate([slots, *split_terms(bias[...])], axis=1)
    upward[:halo] = latent[halo:]
    spare = jnp.zeros((1, rows - noise.shape[1]), F32)
    padded = jnp.concatenate([noise[...], spare], axis=1)
    padded = jnp.broadcast_to(padded, (upward.shape[0] - halo, rows))
    terms = split_terms(padded)
    upward[halo:] = jnp.concatenate([*terms, jnp.zeros_like(terms[0])], axis=1)


def prepare_kernel(
    place, embed, nbrs, bias, dec_query, embed_t, norm_t, query_t, logits, *, rows, halo, total
):
    values = embed[...].T
    embed_t[...] = values
    norm = normalize(values.astype(F32), 0)[0].astype(BF16)
    norm_t[...] = norm
    query_t[...] = tn(dec_query[...], norm).astype(BF16)
    local = (nbrs[...] - place[1]) & (total - 1)
    slots = jnp.where(local < halo, local + rows, jnp.where(local < halo + rows, local - halo, local))
    logits[...] = spread_bias(slots, bias[...], rows + 2 * halo)


def window_order(values, rows, halo):
    first = 2 * halo + halo
    return jnp.concatenate(
        [
            values[first : first + rows],
            values[first - halo : first],
            values[first + rows : first + rows + halo],
        ],
        axis=0,
    )


def step_kernel(
    place,
    own,
    edges,
    twin,
    beside,
    below,
    above,
    noise_own,
    embed_hbm,
    norm_hbm,
    query_hbm,
    logits_hbm,
    weather_hbm,
    target_hbm,
    area_hbm,
    scale_hbm,
    shift_hbm,
    qkv_hbm,
    attn_out_hbm,
    dec_kv_hbm,
    dec_out_hbm,
    head_hbm,
    pred_own_hbm,
    pred_other_hbm,
    keep_hbm,
    send_hbm,
    noise_out,
    embed_t,
    norm_t,
    query_t,
    grid_logits,
    weather,
    target,
    area,
    cond_scale,
    cond_shift,
    attn_qkv,
    attn_out,
    dec_kv,
    dec_out,
    head_out,
    pred,
    grads,
    latent,
    unit_t,
    unit_q_t,
    mesh_logits,
    mesh_query,
    mesh_kv,
    mesh_probs,
    mesh_mixed,
    mesh_out,
    mesh_norm,
    dec_keys,
    grid_probs,
    grid_mixed,
    grid_out,
    grid_final,
    change,
    grad_change,
    head_pad,
    grad_dec,
    grad_kv,
    load_sems,
    store_sems,
    *,
    scale_den,
):
    rows, dim = own.shape
    halo = rows // 2
    window = rows + 2 * halo
    heads = dim // HEAD
    members = 2
    channels = weather.shape[0]
    slots = embed_t.shape[1]
    inv_sqrt = 1.0 / math.sqrt(HEAD)
    member = place[0]
    core = place[3]
    here = pl.ds(pl.multiple_of(member * slots, slots), slots)

    loads = {}

    def load(name, source, target_ref):
        loads[name] = pltpu.make_async_copy(source, target_ref, load_sems.at[len(loads)])
        loads[name].start()

    load("scale", scale_hbm, cond_scale)
    load("shift", shift_hbm, cond_shift)
    load("qkv", qkv_hbm, attn_qkv)
    load("attn_out", attn_out_hbm, attn_out)
    load("dec_kv", dec_kv_hbm, dec_kv)
    load("query", query_hbm, query_t)
    load("logits", logits_hbm, grid_logits)
    load("embed", embed_hbm, embed_t)
    load("dec_out", dec_out_hbm, dec_out)
    load("head", head_hbm, head_out)
    load("weather", weather_hbm.at[:, here], weather)
    load("target", target_hbm.at[:, here], target)
    load("area", area_hbm.at[:, here], area)
    load("norm", norm_hbm, norm_t)

    odd = core == 1
    latent[0:halo] = below[:halo]
    latent[halo : halo + rows] = jnp.where(odd, twin[:rows], beside[:rows])
    latent[halo + rows : halo + 2 * rows] = own[...]
    latent[halo + 2 * rows : halo + 3 * rows] = jnp.where(odd, beside[:rows], twin[:rows])
    latent[halo + 3 * rows :] = above[...]
    unit = normalize(latent[...].astype(F32), 1)[0]
    unit_t[...] = unit.astype(BF16).T
    unit_q_t[...] = window_order(unit, rows, halo).astype(BF16).T

    lane = lax.broadcasted_iota(jnp.int32, (edges.shape[0], rows), 1)
    late = (lane >= halo) == odd
    ends = jnp.where(
        jnp.concatenate([late] * 4, axis=1), twin[rows:].astype(F32), beside[rows:].astype(F32)
    )
    lists = edges[...].astype(F32)

    def listed(part):
        return [
            lists[:, part * rows : (part + 1) * rows],
            pltpu.roll(ends[:, part * rows : (part + 1) * rows], halo, 1),
        ]

    mesh_logits[...] = spread_bias(
        jnp.concatenate(listed(0), axis=1).astype(jnp.int32),
        joined_terms(*(jnp.concatenate(listed(part), axis=1) for part in (1, 2, 3))),
        window,
    )
    noise_row = joined_terms(*(below[halo:, part * rows : (part + 1) * rows] for part in (0, 1, 2)))
    spread = cond_scale.shape[0]
    noise_other = jnp.broadcast_to(noise_row[:1], (rows, rows)).T[:spread, :1]
    noise = [noise_own[...], noise_other]
    noise_out[...] = noise_other
    is_before = lax.broadcasted_iota(jnp.int32, (window, rows), 1) < halo

    def split_ends(values):
        values = values.astype(F32)
        return jnp.concatenate(
            [jnp.where(is_before, values, 0.0), jnp.where(is_before, 0.0, values)], axis=0
        ).astype(BF16)

    def window_scores(keys, queries):
        mid = nn(keys[rows : rows + window], queries[:, :rows])
        ends = nn(keys, queries[:, rows:])
        return jnp.concatenate([mid, jnp.where(is_before, ends[:window], ends[window:])], axis=1)

    loads["scale"].wait()
    loads["shift"].wait()
    gains = []
    shifts = []
    for m in range(members):
        gains.append(1.0 + jnp.sum(noise[m] * cond_scale[...], axis=0, keepdims=True))
        shifts.append(jnp.sum(noise[m] * cond_shift[...], axis=0, keepdims=True))

    loads["qkv"].wait()
    for m in range(members):
        act = (unit * gains[m] + shifts[m]).astype(BF16)
        mesh_kv[m] = nn(act, attn_qkv[:, dim:]).astype(BF16)
        act_q = window_order(act, rows, halo)
        mesh_query[m] = nn(act_q, attn_qkv[:, :dim]).astype(BF16).T
        for h in range(heads):
            cols = slice(h * HEAD, (h + 1) * HEAD)
            value_cols = slice(dim + h * HEAD, dim + (h + 1) * HEAD)
            scores = window_scores(mesh_kv[m, :, cols], mesh_query[m, cols, :])
            probs = softmax_rows(scores * inv_sqrt + mesh_logits[...]).astype(BF16)
            mesh_probs[m, h] = probs
            values = mesh_kv[m, :, value_cols]
            mid = tn(values[rows : rows + window], probs[:, :rows])
            ends = tn(values, split_ends(probs[:, rows:]))
            mesh_mixed[m, cols, :] = jnp.concatenate([mid, ends], axis=1).astype(BF16)
        if m == 0:
            loads["attn_out"].wait()
            loads["dec_kv"].wait()
        residual = window_order(latent[...].astype(F32), rows, halo)
        out = (residual + nn(mesh_mixed[m].T, attn_out[...])).astype(BF16)
        mesh_out[m] = out
        norm = normalize(out.astype(F32), 1)[0].astype(BF16)
        mesh_norm[m] = norm
        dec_keys[m] = nn(norm, dec_kv[...]).astype(BF16)

    for name in ("query", "logits", "embed", "dec_out", "head"):
        loads[name].wait()
    head_pad[...] = jnp.zeros_like(head_pad)
    head_pad[:channels] = head_out[...]
    for m in range(members):
        for h in range(heads):
            cols = slice(h * HEAD, (h + 1) * HEAD)
            value_cols = slice(dim + h * HEAD, dim + (h + 1) * HEAD)
            scores = nn(dec_keys[m, :, cols], query_t[cols, :])
            probs = softmax_rows(scores * inv_sqrt + grid_logits[...]).astype(BF16)
            grid_probs[m, h] = probs
            grid_mixed[m, cols, :] = tn(dec_keys[m, :, value_cols], probs).astype(BF16)
        out = (embed_t[...].astype(F32) + tn(dec_out[...], grid_mixed[m])).astype(BF16)
        grid_out[m] = out
        final = normalize(out.astype(F32), 0)[0].astype(BF16)
        grid_final[m] = final
        change[m] = nn(head_pad[...], final)

    for name in ("weather", "target", "area", "norm"):
        loads[name].wait()
    slot = lax.broadcasted_iota(jnp.int32, (1, slots), 1) + place[0] * slots
    live = jnp.where(slot < place[2], 1.0, 0.0)
    weighting = live * area[...]
    first = weather[...] + live * change[0, :channels]
    second = weather[...] + live * change[1, :channels]
    pred[0] = first
    pred[1] = second
    stores = [
        pltpu.make_async_copy(pred.at[0], pred_own_hbm, store_sems.at[0]),
        pltpu.make_async_copy(pred.at[1], pred_other_hbm, store_sems.at[1]),
    ]
    for store in stores:
        store.start()

    def smooth(values):
        square = values * values + SMOOTHING
        inverse = lax.rsqrt(square)
        return square * inverse, values * inverse

    size_first, slope_first = smooth(first - target[...])
    size_second, slope_second = smooth(second - target[...])
    size_pair, slope_pair = smooth(first - second)
    loss = jnp.sum(weighting * (size_first + size_second - size_pair)) / scale_den
    factor = weighting * (LOSS_SCALE / scale_den)
    grad_change[...] = jnp.zeros_like(grad_change)
    grad_change[0, :channels] = (factor * (slope_first - slope_pair)).astype(BF16)
    grad_change[1, :channels] = (factor * (slope_second + slope_pair)).astype(BF16)

    grad_head = None
    grad_dec_out = None
    grad_query = None
    for m in range(members):
        g_change = grad_change[m]
        term = nt(g_change, grid_final[m])
        grad_head = term if m == 0 else grad_head + term
        g_final = tn(head_pad[...], g_change)
        g_out = normalize_back(grid_out[m].astype(F32), g_final, 0).astype(BF16)
        term = nt(grid_mixed[m], g_out)
        grad_dec_out = term if m == 0 else grad_dec_out + term
        g_mixed = nn(dec_out[...], g_out).astype(BF16)
        terms = []
        for h in range(heads):
            cols = slice(h * HEAD, (h + 1) * HEAD)
            value_cols = slice(dim + h * HEAD, dim + (h + 1) * HEAD)
            g_head = g_mixed[cols, :]
            probs = grid_probs[m, h]
            g_scores = score_back(probs, nn(dec_keys[m, :, value_cols], g_head))
            terms.append(tn(dec_keys[m, :, cols], g_scores))
            grad_dec[m, :, cols] = nt(g_scores, query_t[cols, :]).astype(BF16)
            grad_dec[m, :, value_cols] = nt(probs, g_head).astype(BF16)
        term = jnp.concatenate(terms, axis=0)
        grad_query = term if m == 0 else grad_query + term
    grad_dec_query = nt(norm_t[...], grad_query.astype(BF16))

    grad_dec_kv = None
    grad_attn_out = None
    grad_qkv = None
    grad_cond = None
    for m in range(members):
        g_dec = grad_dec[m]
        term = tn(mesh_norm[m], g_dec)
        grad_dec_kv = term if m == 0 else grad_dec_kv + term
        g_norm = nt(g_dec, dec_kv[...])
        g_out = normalize_back(mesh_out[m].astype(F32), g_norm, 1).astype(BF16)
        term = nn(mesh_mixed[m], g_out)
        grad_attn_out = term if m == 0 else grad_attn_out + term
        g_mixed = nt(attn_out[...], g_out).astype(BF16)
        g_queries = []
        for h in range(heads):
            cols = slice(h * HEAD, (h + 1) * HEAD)
            value_cols = slice(dim + h * HEAD, dim + (h + 1) * HEAD)
            g_head = g_mixed[cols, :]
            probs = mesh_probs[m, h]
            keys = mesh_kv[m, :, cols]
            g_scores = score_back(probs, window_scores(mesh_kv[m, :, value_cols], g_head))
            g_ends = split_ends(g_scores[:, rows:])
            mid = tn(keys[rows : rows + window], g_scores[:, :rows])
            ends = tn(keys, g_ends)
            g_queries.append(jnp.concatenate([mid, ends], axis=1))
            queries = mesh_query[m, cols, :]
            grad_kv[:, cols] = nt(g_ends, queries[:, rows:])
            grad_kv[rows : rows + window, cols] += nt(g_scores[:, :rows], queries[:, :rows])
            grad_kv[:, value_cols] = nt(split_ends(probs[:, rows:]), g_head[:, rows:])
            grad_kv[rows : rows + window, value_cols] += nt(probs[:, :rows], g_head[:, :rows])
        g_kv = grad_kv[...].astype(BF16)
        g_query = jnp.concatenate(g_queries, axis=0).astype(BF16).T
        moment = jnp.concatenate([nn(unit_q_t[...], g_query), nn(unit_t[...], g_kv)], axis=1)
        col_sum = jnp.concatenate(
            [
                jnp.sum(g_query.astype(F32), axis=0, keepdims=True),
                jnp.sum(g_kv.astype(F32), axis=0, keepdims=True),
            ],
            axis=1,
        )
        gain_col = jnp.broadcast_to(gains[m], (HEAD, dim)).T[:, :1]
        shift_col = jnp.broadcast_to(shifts[m], (HEAD, dim)).T[:, :1]
        term = gain_col * moment + shift_col * col_sum
        grad_qkv = term if m == 0 else grad_qkv + term
        weight = attn_qkv[...].astype(F32)
        g_gain = jnp.sum(weight * moment, axis=1, keepdims=True)
        g_shift = jnp.sum(weight * col_sum, axis=1, keepdims=True)
        mine = member if m == 0 else 1 - member
        row_id = lax.broadcasted_iota(jnp.int32, (16, dim), 0)
        term = jnp.where(row_id == mine, jnp.broadcast_to(g_gain, (dim, HEAD)).T[:16], 0.0)
        term += jnp.where(row_id == mine + 2, jnp.broadcast_to(g_shift, (dim, HEAD)).T[:16], 0.0)
        grad_cond = term if m == 0 else grad_cond + term

    row_id = lax.broadcasted_iota(jnp.int32, (16, dim), 0)
    grad_cond += jnp.where(row_id == 4, loss, 0.0)
    grads[:, :, HEAD:, :] = jnp.zeros((2, 64, 16, HEAD), BF16)
    blocks = (
        grad_qkv[:, :dim],
        grad_qkv[:, dim : 2 * dim],
        grad_qkv[:, 2 * dim :],
        grad_attn_out,
        grad_dec_query,
        grad_dec_kv[:, :dim],
        grad_dec_kv[:, dim:],
        grad_dec_out,
    )
    tall = HEAD * HEAD // dim
    for i, block in enumerate(blocks):
        first_chunk = i % 4 * (dim // tall)
        for c in range(dim // tall):
            for t in range(heads):
                grads[i // 4, first_chunk + c, t * tall : (t + 1) * tall, :] = block[
                    c * tall : (c + 1) * tall, t * HEAD : (t + 1) * HEAD
                ].astype(BF16)
    extras = jnp.concatenate([grad_head, grad_cond], axis=0)
    for i in range(extras.shape[0] // 16):
        for t in range(heads):
            grads[0, i * heads + t, HEAD:, :] = extras[
                i * 16 : (i + 1) * 16, t * HEAD : (t + 1) * HEAD
            ].astype(BF16)
    keep = pltpu.make_async_copy(grads.at[core], keep_hbm, store_sems.at[2])
    send = pltpu.make_async_copy(grads.at[1 - core], send_hbm, store_sems.at[3])
    keep.start()
    send.start()
    stores += [keep, send]
    for store in stores:
        store.wait()


def sum_kernel(parts, result):
    total = jnp.sum(parts[...].astype(F32), axis=0, keepdims=True)
    result[...] = jnp.broadcast_to(total.astype(BF16), result.shape)


def unpack_kernel(
    place,
    mine_hbm,
    theirs_hbm,
    noise_own,
    noise_other,
    pred_own_hbm,
    pred_arrived_hbm,
    pred_hbm,
    grad_scale,
    grad_shift,
    grad_qkv,
    grad_attn_out,
    grad_dec_query,
    grad_dec_kv,
    grad_dec_out,
    grad_head,
    loss,
    grads,
    sems,
):
    member = place[0]
    core = place[3]
    channels, slots = pred_own_hbm.shape
    dim = grad_attn_out.shape[0]
    heads = dim // HEAD
    here = pl.ds(pl.multiple_of(member * slots, slots), slots)
    there = pl.ds(pl.multiple_of((1 - member) * slots, slots), slots)
    copies = [
        pltpu.make_async_copy(mine_hbm, grads.at[core], sems.at[0]),
        pltpu.make_async_copy(theirs_hbm, grads.at[1 - core], sems.at[1]),
        pltpu.make_async_copy(pred_own_hbm, pred_hbm.at[0, :, here], sems.at[2]),
        pltpu.make_async_copy(pred_arrived_hbm, pred_hbm.at[0, :, there], sems.at[3]),
    ]
    for copy in copies:
        copy.start()
    copies[0].wait()
    copies[1].wait()
    tall = HEAD * HEAD // dim
    targets = (
        (grad_qkv, 0),
        (grad_qkv, dim),
        (grad_qkv, 2 * dim),
        (grad_attn_out, 0),
        (grad_dec_query, 0),
        (grad_dec_kv, 0),
        (grad_dec_kv, dim),
        (grad_dec_out, 0),
    )
    for i, (ref, col) in enumerate(targets):
        first_chunk = i % 4 * (dim // tall)
        for c in range(dim // tall):
            for t in range(heads):
                ref[c * tall : (c + 1) * tall, col + t * HEAD : col + (t + 1) * HEAD] = grads[
                    i // 4, first_chunk + c, t * tall : (t + 1) * tall, :
                ].astype(F32)

    def extra(i):
        return jnp.concatenate(
            [grads[0, i * heads + t, HEAD:, :].astype(F32) for t in range(heads)], axis=1
        )

    head_blocks = -(-channels // 16)
    for i in range(head_blocks):
        count = min(16, channels - i * 16)
        grad_head[i * 16 : i * 16 + count] = extra(i)[:count]
    cond = extra(2 * (-(-channels // 32)))
    first = cond[0:1]
    second = cond[1:2]
    grad_scale[...] = noise_own[...] * jnp.where(member == 0, first, second) + noise_other[
        ...
    ] * jnp.where(member == 0, second, first)
    first = cond[2:3]
    second = cond[3:4]
    grad_shift[...] = noise_own[...] * jnp.where(member == 0, first, second) + noise_other[
        ...
    ] * jnp.where(member == 0, second, first)
    loss[...] = cond[4:5, :HEAD]
    copies[2].wait()
    copies[3].wait()


def whole(shape):
    return pl.BlockSpec(shape, lambda *_: (0,) * len(shape))


def per_device(
    mesh_latent,
    grid_embed,
    weather_state,
    target,
    cell_area,
    member_noise,
    mesh_nbrs,
    mesh_bias,
    grid_nbrs,
    grid_bias,
    grid_counts,
    cond_scale,
    cond_shift,
    attn_qkv,
    attn_out,
    dec_query,
    dec_kv,
    dec_out,
    head_out,
):
    rows, dim = mesh_latent.shape
    halo = rows // 2
    window = rows + 2 * halo
    outer = 2 * window
    size = lax.axis_size("space")
    grid_slots = grid_embed.shape[0]
    slots = grid_slots // 2
    channels = weather_state.shape[0]
    total = rows * size
    heads = dim // HEAD
    noise_size = member_noise.shape[1]
    entries = grid_nbrs.shape[0]
    scale_den = 2.0 * channels * grid_slots * size

    member = lax.axis_index("member")
    space = lax.axis_index("space")
    start = space * rows - halo
    place = jnp.stack([member, start, grid_counts[0], space % 2]).astype(jnp.int32)
    axes = ("member", "space")

    def permute(value, target_of):
        pairs = []
        for m in range(2):
            for k in range(size):
                to_m, to_k = target_of(m, k)
                pairs.append((m * size + k, to_m * size + to_k % size))
        return lax.ppermute(value, axes, pairs)

    smem = pl.BlockSpec(memory_space=pltpu.SMEM)
    packet, upward = pl.pallas_call(
        lambda *refs: pack_kernel(*refs, total=total),
        in_specs=[smem] + [pl.BlockSpec(memory_space=pltpu.VMEM)] * 4,
        out_shape=[
            jax.ShapeDtypeStruct((rows + mesh_nbrs.shape[0], dim), BF16),
            jax.ShapeDtypeStruct((halo + 16, dim), BF16),
        ],
        name="pack",
    )(place, mesh_latent, mesh_nbrs, mesh_bias, member_noise)
    beside = permute(packet, lambda m, k: (m, k + 1 if k % 2 else k - 1))
    below = permute(upward, lambda m, k: (1 - m, k + 2))
    above = permute(mesh_latent[:halo], lambda m, k: (m, k - 2))
    twin = permute(packet, lambda m, k: (m, k ^ 1))

    part = pl.BlockSpec((slots, dim), lambda i, place: (place[0], 0))
    lists = pl.BlockSpec((entries, slots), lambda i, place: (0, place[0]))
    square = (dim, slots)
    embed_t, norm_t, query_t, grid_logits = pl.pallas_call(
        lambda *refs: prepare_kernel(*refs, rows=rows, halo=halo, total=total),
        grid_spec=pltpu.PrefetchScalarGridSpec(
            num_scalar_prefetch=1,
            grid=(1,),
            in_specs=[part, lists, lists, whole((dim, dim))],
            out_specs=[whole(square), whole(square), whole(square), whole((window, slots))],
        ),
        out_shape=[
            jax.ShapeDtypeStruct(square, BF16),
            jax.ShapeDtypeStruct(square, BF16),
            jax.ShapeDtypeStruct(square, BF16),
            jax.ShapeDtypeStruct((window, slots), F32),
        ],
        compiler_params=pltpu.CompilerParams(vmem_limit_bytes=40 * 2**20),
        cost_estimate=pl.CostEstimate(
            flops=2 * dim * dim * slots, bytes_accessed=3 * 2**20, transcendentals=0
        ),
        name="prepare",
    )(place, grid_embed, grid_nbrs, grid_bias, dec_query)

    channel_pad = -(-channels // 32) * 32
    chunks = size
    half_shape = (chunks, HEAD + 16, HEAD)
    hbm = pl.BlockSpec(memory_space=pl.ANY)
    vmem = pl.BlockSpec(memory_space=pltpu.VMEM)
    step_in = (
        mesh_latent,
        packet[rows:],
        twin,
        beside,
        below,
        above,
        member_noise.reshape(noise_size, 1),
        embed_t,
        norm_t,
        query_t,
        grid_logits,
        weather_state,
        target,
        cell_area[None, :],
        cond_scale,
        cond_shift,
        attn_qkv,
        attn_out,
        dec_kv,
        dec_out,
        head_out,
    )
    pred_own, pred_other, keep, send, other_noise = pl.pallas_call(
        lambda *refs: step_kernel(*refs, scale_den=scale_den),
        in_specs=[smem] + [vmem] * 7 + [hbm] * 14,
        out_specs=[hbm] * 4 + [vmem],
        scratch_shapes=[
            pltpu.VMEM(square, BF16),
            pltpu.VMEM(square, BF16),
            pltpu.VMEM(square, BF16),
            pltpu.VMEM((window, slots), F32),
            pltpu.VMEM((channels, slots), F32),
            pltpu.VMEM((channels, slots), F32),
            pltpu.VMEM((1, slots), F32),
            pltpu.VMEM(cond_scale.shape, F32),
            pltpu.VMEM(cond_shift.shape, F32),
            pltpu.VMEM(attn_qkv.shape, BF16),
            pltpu.VMEM(attn_out.shape, BF16),
            pltpu.VMEM(dec_kv.shape, BF16),
            pltpu.VMEM(dec_out.shape, BF16),
            pltpu.VMEM(head_out.shape, BF16),
            pltpu.VMEM((2, channels, slots), F32),
            pltpu.VMEM((2, *half_shape), BF16),
            pltpu.VMEM((outer, dim), BF16),
            pltpu.VMEM((dim, outer), BF16),
            pltpu.VMEM((dim, window), BF16),
            pltpu.VMEM((window, window), F32),
            pltpu.VMEM((2, dim, window), BF16),
            pltpu.VMEM((2, outer, 2 * dim), BF16),
            pltpu.VMEM((2, heads, window, window), BF16),
            pltpu.VMEM((2, dim, window), BF16),
            pltpu.VMEM((2, window, dim), BF16),
            pltpu.VMEM((2, window, dim), BF16),
            pltpu.VMEM((2, window, 2 * dim), BF16),
            pltpu.VMEM((2, heads, window, slots), BF16),
            pltpu.VMEM((2, dim, slots), BF16),
            pltpu.VMEM((2, dim, slots), BF16),
            pltpu.VMEM((2, dim, slots), BF16),
            pltpu.VMEM((2, channel_pad, slots), F32),
            pltpu.VMEM((2, channel_pad, slots), BF16),
            pltpu.VMEM((channel_pad, dim), BF16),
            pltpu.VMEM((2, window, 2 * dim), BF16),
            pltpu.VMEM((outer, 2 * dim), F32),
            pltpu.SemaphoreType.DMA((14,)),
            pltpu.SemaphoreType.DMA((4,)),
        ],
        out_shape=[
            jax.ShapeDtypeStruct((channels, slots), F32),
            jax.ShapeDtypeStruct((channels, slots), F32),
            jax.ShapeDtypeStruct(half_shape, BF16),
            jax.ShapeDtypeStruct(half_shape, BF16),
            jax.ShapeDtypeStruct((noise_size, 1), F32),
        ],
        compiler_params=pltpu.CompilerParams(vmem_limit_bytes=56 * 2**20),
        cost_estimate=pl.CostEstimate(
            flops=10**10, bytes_accessed=12 * 2**20, transcendentals=2**21
        ),
        name="step",
    )(place, *step_in)

    def twin_swap(value):
        return permute(value, lambda m, k: (m, k ^ 1))

    groups = [
        [m * size + k for m in range(2) for k in range(size) if k % 2 == c] for c in range(2)
    ]

    def over_chips(value):
        return lax.all_to_all(value, axes, 0, 0, axis_index_groups=groups)

    arrived_pred = permute(pred_other, lambda m, k: (1 - m, k))
    pair = (keep.astype(F32) + twin_swap(send).astype(F32)).astype(BF16)
    parts = over_chips(pair)
    shared = pl.pallas_call(
        sum_kernel,
        in_specs=[vmem],
        out_specs=vmem,
        out_shape=jax.ShapeDtypeStruct(half_shape, BF16),
        compiler_params=pltpu.CompilerParams(vmem_limit_bytes=32 * 2**20),
        name="sum",
    )(parts)
    mine = over_chips(shared)
    theirs = twin_swap(mine)
    grad_shapes = [
        jax.ShapeDtypeStruct(shape, F32)
        for shape in (
            cond_scale.shape,
            cond_shift.shape,
            attn_qkv.shape,
            attn_out.shape,
            dec_query.shape,
            dec_kv.shape,
            dec_out.shape,
            head_out.shape,
            (1, HEAD),
        )
    ]
    outputs = pl.pallas_call(
        unpack_kernel,
        in_specs=[smem, hbm, hbm, vmem, vmem, hbm, hbm],
        out_specs=[hbm] + [vmem] * 9,
        out_shape=[jax.ShapeDtypeStruct((1, channels, grid_slots), F32)] + grad_shapes,
        scratch_shapes=[pltpu.VMEM((2, *half_shape), BF16), pltpu.SemaphoreType.DMA((4,))],
        compiler_params=pltpu.CompilerParams(vmem_limit_bytes=40 * 2**20),
        name="unpack",
    )(place, mine, theirs, step_in[6], other_noise, pred_own, arrived_pred)
    return (*outputs[:9], outputs[9][0, 0])


def solution(mesh):
    in_specs = (
        P("space", None),
        P("space", None),
        P(None, "space"),
        P(None, "space"),
        P("space"),
        P("member", None),
        P(None, "space"),
        P(None, "space"),
        P(None, "space"),
        P(None, "space"),
        P("space"),
        P(),
        P(),
        P(),
        P(),
        P(),
        P(),
        P(),
        P(),
    )
    out_specs = (P("member", None, "space"), P(), P(), P(), P(), P(), P(), P(), P(), P())
    return jax.shard_map(
        per_device, mesh=mesh, in_specs=in_specs, out_specs=out_specs, check_vma=False
    )
```

```python
import math

import jax
import jax.numpy as jnp
from jax import lax
from jax.experimental import pallas as pl
from jax.experimental.pallas import tpu as pltpu
from jax.sharding import PartitionSpec as P

HEAD = 128
EPSILON = 1e-05
LOSS_SCALE = 65536.0
SMOOTHING = 0.0625
FAR = -1e30
ALL_VMEM = 62 * 2**20

F32 = jnp.float32
BF16 = jnp.bfloat16


def nn(first, second):
    return lax.dot_general(first, second, (((1,), (0,)), ((), ())), preferred_element_type=F32)


def nt(first, second):
    return lax.dot_general(first, second, (((1,), (1,)), ((), ())), preferred_element_type=F32)


def tn(first, second):
    return lax.dot_general(first, second, (((0,), (0,)), ((), ())), preferred_element_type=F32)


def normalize(values, axis):
    center = values - jnp.mean(values, axis=axis, keepdims=True)
    spread = jnp.mean(center * center, axis=axis, keepdims=True)
    scale = lax.rsqrt(spread + EPSILON)
    return center * scale, scale


def normalize_back(values, grad_out, axis):
    unit, scale = normalize(values, axis)
    mean_grad = jnp.mean(grad_out, axis=axis, keepdims=True)
    mean_unit = jnp.mean(grad_out * unit, axis=axis, keepdims=True)
    return scale * (grad_out - mean_grad - unit * mean_unit)


def spread_bias(slots, bias, rows):
    entries, width = slots.shape
    row_ids = lax.broadcasted_iota(jnp.int32, (rows, width), 0)
    logits = jnp.full((rows, width), FAR, F32)
    for entry in range(entries):
        same = slots == slots[entry : entry + 1]
        top = jnp.max(jnp.where(same, bias, FAR), axis=0, keepdims=True)
        terms = jnp.sum(jnp.where(same, jnp.exp(bias - top), 0.0), axis=0, keepdims=True)
        logits = jnp.where(row_ids == slots[entry : entry + 1], top + jnp.log(terms), logits)
    return logits


def softmax_rows(scores):
    terms = jnp.exp(scores - jnp.max(scores, axis=0, keepdims=True))
    return terms * (1.0 / jnp.sum(terms, axis=0, keepdims=True))


def score_back(probs, grad_probs):
    probs = probs.astype(F32)
    inner = jnp.sum(probs * grad_probs, axis=0, keepdims=True)
    return (probs * (grad_probs - inner) * (1.0 / math.sqrt(HEAD))).astype(BF16)


def split_terms(values):
    high = values.astype(BF16)
    rest = values - high.astype(F32)
    middle = rest.astype(BF16)
    low = (rest - middle.astype(F32)).astype(BF16)
    return high, middle, low


def joined_terms(high, middle, low):
    return high.astype(F32) + (middle.astype(F32) + low.astype(F32))


def window_start(rows):
    return lax.axis_index("space") * rows - rows // 2


def pack_kernel(latent, nbrs, bias, noise, packet, upward, downward, *, total):
    rows = latent.shape[0]
    halo = rows // 2
    packet[:rows] = latent[...]
    downward[...] = latent[:halo]
    slots = ((nbrs[...] - window_start(rows)) & (total - 1)).astype(F32).astype(BF16)
    packet[rows:] = jnp.concatenate([slots, *split_terms(bias[...])], axis=1)
    upward[:halo] = latent[halo:]
    spare = jnp.zeros((1, rows - noise.shape[1]), F32)
    padded = jnp.concatenate([noise[...], spare], axis=1)
    padded = jnp.broadcast_to(padded, (upward.shape[0] - halo, rows))
    terms = split_terms(padded)
    upward[halo:] = jnp.concatenate([*terms, jnp.zeros_like(terms[0])], axis=1)


def prepare_kernel(
    embed_hbm,
    nbrs_hbm,
    bias_hbm,
    weight_hbm,
    embed_t,
    norm_t,
    query_t,
    logits,
    embed,
    nbrs,
    bias,
    dec_query,
    sems,
    *,
    rows,
    halo,
    total,
):
    slots = embed.shape[0]
    here = pl.ds(pl.multiple_of(lax.axis_index("member") * slots, slots), slots)
    copies = [
        pltpu.make_async_copy(embed_hbm.at[here, :], embed, sems.at[0]),
        pltpu.make_async_copy(nbrs_hbm.at[:, here], nbrs, sems.at[1]),
        pltpu.make_async_copy(bias_hbm.at[:, here], bias, sems.at[2]),
        pltpu.make_async_copy(weight_hbm, dec_query, sems.at[3]),
    ]
    for copy in copies:
        copy.start()
    copies[0].wait()
    values = embed[...].T
    embed_t[...] = values
    norm = normalize(values.astype(F32), 0)[0].astype(BF16)
    norm_t[...] = norm
    copies[1].wait()
    copies[2].wait()
    local = (nbrs[...] - window_start(rows)) & (total - 1)
    places = jnp.where(
        local < halo, local + rows, jnp.where(local < halo + rows, local - halo, local)
    )
    logits[...] = spread_bias(places, bias[...], rows + 2 * halo)
    copies[3].wait()
    query_t[...] = tn(dec_query[...], norm).astype(BF16)


def window_order(values, rows, halo):
    first = 2 * halo + halo
    return jnp.concatenate(
        [
            values[first : first + rows],
            values[first - halo : first],
            values[first + rows : first + rows + halo],
        ],
        axis=0,
    )


def step_kernel(
    counts,
    packet,
    twin,
    beside,
    below,
    above,
    noise_own,
    embed_hbm,
    norm_hbm,
    query_hbm,
    logits_hbm,
    weather_hbm,
    target_hbm,
    area_hbm,
    scale_hbm,
    shift_hbm,
    qkv_hbm,
    attn_out_hbm,
    dec_kv_hbm,
    dec_out_hbm,
    head_hbm,
    pred_own_hbm,
    pred_other_hbm,
    keep_hbm,
    send_hbm,
    noise_out,
    embed_t,
    norm_t,
    query_t,
    grid_logits,
    weather,
    target,
    area,
    cond_scale,
    cond_shift,
    attn_qkv,
    attn_out,
    dec_kv,
    dec_out,
    head_out,
    pred,
    grads,
    latent,
    unit_t,
    unit_q_t,
    mesh_logits,
    mesh_query,
    mesh_kv,
    mesh_probs,
    mesh_mixed,
    mesh_out,
    mesh_norm,
    dec_keys,
    grid_probs,
    grid_mixed,
    grid_out,
    grid_final,
    change,
    grad_change,
    head_pad,
    grad_dec,
    grad_kv,
    load_sems,
    store_sems,
    *,
    scale_den,
):
    halo, dim = above.shape
    rows = 2 * halo
    window = rows + 2 * halo
    own = packet[:rows]
    edges = packet[rows:]
    heads = dim // HEAD
    members = 2
    channels = weather.shape[0]
    slots = embed_t.shape[1]
    inv_sqrt = 1.0 / math.sqrt(HEAD)
    member = lax.axis_index("member")
    core = lax.rem(lax.axis_index("space"), 2)
    here = pl.ds(pl.multiple_of(member * slots, slots), slots)

    loads = {}

    def load(name, source, target_ref):
        loads[name] = pltpu.make_async_copy(source, target_ref, load_sems.at[len(loads)])
        loads[name].start()

    load("scale", scale_hbm, cond_scale)
    load("shift", shift_hbm, cond_shift)
    load("qkv", qkv_hbm, attn_qkv)
    load("attn_out", attn_out_hbm, attn_out)
    load("dec_kv", dec_kv_hbm, dec_kv)
    load("query", query_hbm, query_t)
    load("logits", logits_hbm, grid_logits)
    load("embed", embed_hbm, embed_t)
    load("dec_out", dec_out_hbm, dec_out)
    load("head", head_hbm, head_out)
    load("weather", weather_hbm.at[:, here], weather)
    load("target", target_hbm.at[:, here], target)
    load("area", area_hbm.at[:, here], area)
    load("norm", norm_hbm, norm_t)

    odd = core == 1
    latent[0:halo] = below[:halo]
    latent[halo : halo + rows] = jnp.where(odd, twin[:rows], beside[:rows])
    latent[halo + rows : halo + 2 * rows] = own
    latent[halo + 2 * rows : halo + 3 * rows] = jnp.where(odd, beside[:rows], twin[:rows])
    latent[halo + 3 * rows :] = above[...]
    unit = normalize(latent[...].astype(F32), 1)[0]
    unit_t[...] = unit.astype(BF16).T
    unit_q_t[...] = window_order(unit, rows, halo).astype(BF16).T

    lane = lax.broadcasted_iota(jnp.int32, (edges.shape[0], rows), 1)
    late = (lane >= halo) == odd
    ends = jnp.where(
        jnp.concatenate([late] * 4, axis=1), twin[rows:].astype(F32), beside[rows:].astype(F32)
    )
    lists = edges.astype(F32)

    def listed(part):
        return [
            lists[:, part * rows : (part + 1) * rows],
            pltpu.roll(ends[:, part * rows : (part + 1) * rows], halo, 1),
        ]

    mesh_logits[...] = spread_bias(
        jnp.concatenate(listed(0), axis=1).astype(jnp.int32),
        joined_terms(*(jnp.concatenate(listed(part), axis=1) for part in (1, 2, 3))),
        window,
    )
    noise_row = joined_terms(*(below[halo:, part * rows : (part + 1) * rows] for part in (0, 1, 2)))
    spread = cond_scale.shape[0]
    own_row = jnp.concatenate([noise_own[...], jnp.zeros((1, rows - spread), F32)], axis=1)
    noise = []
    for m, row in enumerate((own_row, noise_row[:1])):
        columns = jnp.broadcast_to(row, (rows, rows)).T[:spread]
        noise_out[m] = columns
        noise.append(columns[:, :1])
    is_before = lax.broadcasted_iota(jnp.int32, (window, rows), 1) < halo

    def split_ends(values):
        values = values.astype(F32)
        return jnp.concatenate(
            [jnp.where(is_before, values, 0.0), jnp.where(is_before, 0.0, values)], axis=0
        ).astype(BF16)

    def window_scores(keys, queries):
        mid = nn(keys[rows : rows + window], queries[:, :rows])
        ends = nn(keys, queries[:, rows:])
        return jnp.concatenate([mid, jnp.where(is_before, ends[:window], ends[window:])], axis=1)

    loads["scale"].wait()
    loads["shift"].wait()
    gains = []
    shifts = []
    for m in range(members):
        gains.append(1.0 + jnp.sum(noise[m] * cond_scale[...], axis=0, keepdims=True))
        shifts.append(jnp.sum(noise[m] * cond_shift[...], axis=0, keepdims=True))

    loads["qkv"].wait()
    for m in range(members):
        act = (unit * gains[m] + shifts[m]).astype(BF16)
        mesh_kv[m] = nn(act, attn_qkv[:, dim:]).astype(BF16)
        act_q = window_order(act, rows, halo)
        mesh_query[m] = nn(act_q, attn_qkv[:, :dim]).astype(BF16).T
        for h in range(heads):
            cols = slice(h * HEAD, (h + 1) * HEAD)
            value_cols = slice(dim + h * HEAD, dim + (h + 1) * HEAD)
            scores = window_scores(mesh_kv[m, :, cols], mesh_query[m, cols, :])
            probs = softmax_rows(scores * inv_sqrt + mesh_logits[...]).astype(BF16)
            mesh_probs[m, h] = probs
            values = mesh_kv[m, :, value_cols]
            mid = tn(values[rows : rows + window], probs[:, :rows])
            ends = tn(values, split_ends(probs[:, rows:]))
            mesh_mixed[m, cols, :] = jnp.concatenate([mid, ends], axis=1).astype(BF16)
        if m == 0:
            loads["attn_out"].wait()
            loads["dec_kv"].wait()
        residual = window_order(latent[...].astype(F32), rows, halo)
        out = (residual + nn(mesh_mixed[m].T, attn_out[...])).astype(BF16)
        mesh_out[m] = out
        norm = normalize(out.astype(F32), 1)[0].astype(BF16)
        mesh_norm[m] = norm
        dec_keys[m] = nn(norm, dec_kv[...]).astype(BF16)

    for name in ("query", "logits", "embed", "dec_out", "head"):
        loads[name].wait()
    head_pad[...] = jnp.zeros_like(head_pad)
    head_pad[:channels] = head_out[...]
    for m in range(members):
        for h in range(heads):
            cols = slice(h * HEAD, (h + 1) * HEAD)
            value_cols = slice(dim + h * HEAD, dim + (h + 1) * HEAD)
            scores = nn(dec_keys[m, :, cols], query_t[cols, :])
            probs = softmax_rows(scores * inv_sqrt + grid_logits[...]).astype(BF16)
            grid_probs[m, h] = probs
            grid_mixed[m, cols, :] = tn(dec_keys[m, :, value_cols], probs).astype(BF16)
        out = (embed_t[...].astype(F32) + tn(dec_out[...], grid_mixed[m])).astype(BF16)
        grid_out[m] = out
        final = normalize(out.astype(F32), 0)[0].astype(BF16)
        grid_final[m] = final
        change[m] = nn(head_pad[...], final)

    for name in ("weather", "target", "area", "norm"):
        loads[name].wait()
    slot = lax.broadcasted_iota(jnp.int32, (1, slots), 1) + member * slots
    live = jnp.where(slot < counts[0], 1.0, 0.0)
    weighting = live * area[...]
    first = weather[...] + live * change[0, :channels]
    second = weather[...] + live * change[1, :channels]
    pred[0] = first
    pred[1] = second
    stores = [
        pltpu.make_async_copy(pred.at[0], pred_own_hbm, store_sems.at[0]),
        pltpu.make_async_copy(pred.at[1], pred_other_hbm, store_sems.at[1]),
    ]
    for store in stores:
        store.start()

    def smooth(values):
        square = values * values + SMOOTHING
        inverse = lax.rsqrt(square)
        return square * inverse, values * inverse

    size_first, slope_first = smooth(first - target[...])
    size_second, slope_second = smooth(second - target[...])
    size_pair, slope_pair = smooth(first - second)
    loss = jnp.sum(weighting * (size_first + size_second - size_pair)) / scale_den
    factor = weighting * (LOSS_SCALE / scale_den)
    grad_change[...] = jnp.zeros_like(grad_change)
    grad_change[0, :channels] = (factor * (slope_first - slope_pair)).astype(BF16)
    grad_change[1, :channels] = (factor * (slope_second + slope_pair)).astype(BF16)

    grad_head = None
    grad_dec_out = None
    grad_query = None
    for m in range(members):
        g_change = grad_change[m]
        term = nt(g_change, grid_final[m])
        grad_head = term if m == 0 else grad_head + term
        g_final = tn(head_pad[...], g_change)
        g_out = normalize_back(grid_out[m].astype(F32), g_final, 0).astype(BF16)
        term = nt(grid_mixed[m], g_out)
        grad_dec_out = term if m == 0 else grad_dec_out + term
        g_mixed = nn(dec_out[...], g_out).astype(BF16)
        terms = []
        for h in range(heads):
            cols = slice(h * HEAD, (h + 1) * HEAD)
            value_cols = slice(dim + h * HEAD, dim + (h + 1) * HEAD)
            g_head = g_mixed[cols, :]
            probs = grid_probs[m, h]
            g_scores = score_back(probs, nn(dec_keys[m, :, value_cols], g_head))
            terms.append(tn(dec_keys[m, :, cols], g_scores))
            grad_dec[m, :, cols] = nt(g_scores, query_t[cols, :]).astype(BF16)
            grad_dec[m, :, value_cols] = nt(probs, g_head).astype(BF16)
        term = jnp.concatenate(terms, axis=0)
        grad_query = term if m == 0 else grad_query + term
    grad_dec_query = nt(norm_t[...], grad_query.astype(BF16))

    grad_dec_kv = None
    grad_attn_out = None
    grad_qkv = None
    grad_cond = None
    for m in range(members):
        g_dec = grad_dec[m]
        term = tn(mesh_norm[m], g_dec)
        grad_dec_kv = term if m == 0 else grad_dec_kv + term
        g_norm = nt(g_dec, dec_kv[...])
        g_out = normalize_back(mesh_out[m].astype(F32), g_norm, 1).astype(BF16)
        term = nn(mesh_mixed[m], g_out)
        grad_attn_out = term if m == 0 else grad_attn_out + term
        g_mixed = nt(attn_out[...], g_out).astype(BF16)
        g_queries = []
        for h in range(heads):
            cols = slice(h * HEAD, (h + 1) * HEAD)
            value_cols = slice(dim + h * HEAD, dim + (h + 1) * HEAD)
            g_head = g_mixed[cols, :]
            probs = mesh_probs[m, h]
            keys = mesh_kv[m, :, cols]
            g_scores = score_back(probs, window_scores(mesh_kv[m, :, value_cols], g_head))
            g_ends = split_ends(g_scores[:, rows:])
            mid = tn(keys[rows : rows + window], g_scores[:, :rows])
            ends = tn(keys, g_ends)
            g_queries.append(jnp.concatenate([mid, ends], axis=1))
            queries = mesh_query[m, cols, :]
            grad_kv[:, cols] = nt(g_ends, queries[:, rows:])
            grad_kv[rows : rows + window, cols] += nt(g_scores[:, :rows], queries[:, :rows])
            grad_kv[:, value_cols] = nt(split_ends(probs[:, rows:]), g_head[:, rows:])
            grad_kv[rows : rows + window, value_cols] += nt(probs[:, :rows], g_head[:, :rows])
        g_kv = grad_kv[...].astype(BF16)
        g_query = jnp.concatenate(g_queries, axis=0).astype(BF16).T
        moment = jnp.concatenate([nn(unit_q_t[...], g_query), nn(unit_t[...], g_kv)], axis=1)
        col_sum = jnp.concatenate(
            [
                jnp.sum(g_query.astype(F32), axis=0, keepdims=True),
                jnp.sum(g_kv.astype(F32), axis=0, keepdims=True),
            ],
            axis=1,
        )
        gain_col = jnp.broadcast_to(gains[m], (HEAD, dim)).T[:, :1]
        shift_col = jnp.broadcast_to(shifts[m], (HEAD, dim)).T[:, :1]
        term = gain_col * moment + shift_col * col_sum
        grad_qkv = term if m == 0 else grad_qkv + term
        weight = attn_qkv[...].astype(F32)
        g_gain = jnp.sum(weight * moment, axis=1, keepdims=True)
        g_shift = jnp.sum(weight * col_sum, axis=1, keepdims=True)
        mine = member if m == 0 else 1 - member
        row_id = lax.broadcasted_iota(jnp.int32, (8, dim), 0)
        term = jnp.where(row_id == mine, jnp.broadcast_to(g_gain, (dim, HEAD)).T[:8], 0.0)
        term += jnp.where(row_id == mine + 2, jnp.broadcast_to(g_shift, (dim, HEAD)).T[:8], 0.0)
        grad_cond = term if m == 0 else grad_cond + term

    row_id = lax.broadcasted_iota(jnp.int32, (8, dim), 0)
    grad_cond += jnp.where(row_id == 4, loss, 0.0)
    grads[:, :, HEAD:, :] = jnp.zeros((2, 64, 8, HEAD), BF16)
    blocks = (
        grad_qkv[:, :dim],
        grad_qkv[:, dim : 2 * dim],
        grad_qkv[:, 2 * dim :],
        grad_attn_out,
        grad_dec_query,
        grad_dec_kv[:, :dim],
        grad_dec_kv[:, dim:],
        grad_dec_out,
    )
    tall = HEAD * HEAD // dim
    for i, block in enumerate(blocks):
        first_chunk = i % 4 * (dim // tall)
        for c in range(dim // tall):
            for t in range(heads):
                grads[i // 4, first_chunk + c, t * tall : (t + 1) * tall, :] = block[
                    c * tall : (c + 1) * tall, t * HEAD : (t + 1) * HEAD
                ].astype(BF16)
    extras = jnp.concatenate([grad_head, grad_cond], axis=0)
    for i in range(extras.shape[0] // 8):
        for t in range(heads):
            grads[0, i * heads + t, HEAD:, :] = extras[
                i * 8 : (i + 1) * 8, t * HEAD : (t + 1) * HEAD
            ].astype(BF16)
    keep = pltpu.make_async_copy(grads.at[core], keep_hbm, store_sems.at[2])
    send = pltpu.make_async_copy(grads.at[1 - core], send_hbm, store_sems.at[3])
    keep.start()
    send.start()
    stores += [keep, send]
    for store in stores:
        store.wait()


def sum_kernel(parts, pred_own_hbm, pred_arrived_hbm, result, pred_hbm, sems):
    slots = pred_own_hbm.shape[1]
    member = lax.axis_index("member")
    here = pl.ds(pl.multiple_of(member * slots, slots), slots)
    there = pl.ds(pl.multiple_of((1 - member) * slots, slots), slots)
    copies = [
        pltpu.make_async_copy(pred_own_hbm, pred_hbm.at[0, :, here], sems.at[0]),
        pltpu.make_async_copy(pred_arrived_hbm, pred_hbm.at[0, :, there], sems.at[1]),
    ]
    for copy in copies:
        copy.start()
    total = jnp.sum(parts[...].astype(F32), axis=0, keepdims=True)
    result[...] = jnp.broadcast_to(total.astype(BF16), result.shape)
    for copy in copies:
        copy.wait()


def unpack_kernel(
    mine_hbm,
    theirs_hbm,
    noise,
    grad_scale,
    grad_shift,
    grad_qkv,
    grad_attn_out,
    grad_dec_query,
    grad_dec_kv,
    grad_dec_out,
    grad_head,
    loss,
    grads,
    sems,
):
    member = lax.axis_index("member")
    core = lax.rem(lax.axis_index("space"), 2)
    channels = grad_head.shape[0]
    dim = grad_attn_out.shape[0]
    heads = dim // HEAD
    copies = [
        pltpu.make_async_copy(mine_hbm, grads.at[core], sems.at[0]),
        pltpu.make_async_copy(theirs_hbm, grads.at[1 - core], sems.at[1]),
    ]
    for copy in copies:
        copy.start()
    for copy in copies:
        copy.wait()
    tall = HEAD * HEAD // dim
    targets = (
        (grad_qkv, 0),
        (grad_qkv, dim),
        (grad_qkv, 2 * dim),
        (grad_attn_out, 0),
        (grad_dec_query, 0),
        (grad_dec_kv, 0),
        (grad_dec_kv, dim),
        (grad_dec_out, 0),
    )
    for i, (ref, col) in enumerate(targets):
        first_chunk = i % 4 * (dim // tall)
        for c in range(dim // tall):
            for t in range(heads):
                ref[c * tall : (c + 1) * tall, col + t * HEAD : col + (t + 1) * HEAD] = grads[
                    i // 4, first_chunk + c, t * tall : (t + 1) * tall, :
                ].astype(F32)

    def extra(i):
        return jnp.concatenate(
            [grads[0, i * heads + t, HEAD:, :].astype(F32) for t in range(heads)], axis=1
        )

    for i in range(-(-channels // 8)):
        count = min(8, channels - i * 8)
        grad_head[i * 8 : i * 8 + count] = extra(i)[:count]
    cond = extra(4 * (-(-channels // 32)))
    first = cond[0:1]
    second = cond[1:2]
    grad_scale[...] = noise[0, :, :1] * jnp.where(member == 0, first, second) + noise[
        1, :, :1
    ] * jnp.where(member == 0, second, first)
    first = cond[2:3]
    second = cond[3:4]
    grad_shift[...] = noise[0, :, :1] * jnp.where(member == 0, first, second) + noise[
        1, :, :1
    ] * jnp.where(member == 0, second, first)
    loss[...] = cond[4:5, :HEAD]


def whole(shape):
    return pl.BlockSpec(shape, lambda *_: (0,) * len(shape))


def per_device(
    mesh_latent,
    grid_embed,
    weather_state,
    target,
    cell_area,
    member_noise,
    mesh_nbrs,
    mesh_bias,
    grid_nbrs,
    grid_bias,
    grid_counts,
    cond_scale,
    cond_shift,
    attn_qkv,
    attn_out,
    dec_query,
    dec_kv,
    dec_out,
    head_out,
):
    rows, dim = mesh_latent.shape
    halo = rows // 2
    window = rows + 2 * halo
    outer = 2 * window
    size = lax.axis_size("space")
    grid_slots = grid_embed.shape[0]
    slots = grid_slots // 2
    channels = weather_state.shape[0]
    total = rows * size
    heads = dim // HEAD
    noise_size = member_noise.shape[1]
    entries = grid_nbrs.shape[0]
    scale_den = 2.0 * channels * grid_slots * size

    axes = ("member", "space")

    def permute(value, target_of):
        pairs = []
        for m in range(2):
            for k in range(size):
                to_m, to_k = target_of(m, k)
                pairs.append((m * size + k, to_m * size + to_k % size))
        return lax.ppermute(value, axes, pairs)

    smem = pl.BlockSpec(memory_space=pltpu.SMEM)
    vmem = pl.BlockSpec(memory_space=pltpu.VMEM)
    hbm = pl.BlockSpec(memory_space=pltpu.HBM)
    packet, upward, downward = pl.pallas_call(
        lambda *refs: pack_kernel(*refs, total=total),
        in_specs=[vmem] * 4,
        out_shape=[
            jax.ShapeDtypeStruct((rows + mesh_nbrs.shape[0], dim), BF16),
            jax.ShapeDtypeStruct((halo + 16, dim), BF16),
            jax.ShapeDtypeStruct((halo, dim), BF16),
        ],
        compiler_params=pltpu.CompilerParams(vmem_limit_bytes=ALL_VMEM),
        name="pack",
    )(mesh_latent, mesh_nbrs, mesh_bias, member_noise)
    beside = permute(packet, lambda m, k: (m, k + 1 if k % 2 else k - 1))
    below = permute(upward, lambda m, k: (1 - m, k + 2))
    above = permute(downward, lambda m, k: (m, k - 2))
    twin = permute(packet, lambda m, k: (m, k ^ 1))

    square = (dim, slots)
    embed_t, norm_t, query_t, grid_logits = pl.pallas_call(
        lambda *refs: prepare_kernel(*refs, rows=rows, halo=halo, total=total),
        in_specs=[hbm] * 4,
        out_specs=[vmem] * 4,
        out_shape=[
            jax.ShapeDtypeStruct(square, BF16),
            jax.ShapeDtypeStruct(square, BF16),
            jax.ShapeDtypeStruct(square, BF16),
            jax.ShapeDtypeStruct((window, slots), F32),
        ],
        scratch_shapes=[
            pltpu.VMEM((slots, dim), BF16),
            pltpu.VMEM((entries, slots), jnp.int32),
            pltpu.VMEM((entries, slots), F32),
            pltpu.VMEM((dim, dim), BF16),
            pltpu.SemaphoreType.DMA((4,)),
        ],
        compiler_params=pltpu.CompilerParams(vmem_limit_bytes=ALL_VMEM),
        cost_estimate=pl.CostEstimate(
            flops=2 * dim * dim * slots, bytes_accessed=3 * 2**20, transcendentals=0
        ),
        name="prepare",
    )(grid_embed, grid_nbrs, grid_bias, dec_query)

    channel_pad = -(-channels // 32) * 32
    chunks = size
    half_shape = (chunks, HEAD + 8, HEAD)
    step_in = (
        packet,
        twin,
        beside,
        below,
        above,
        member_noise,
        embed_t,
        norm_t,
        query_t,
        grid_logits,
        weather_state,
        target,
        cell_area[None, :],
        cond_scale,
        cond_shift,
        attn_qkv,
        attn_out,
        dec_kv,
        dec_out,
        head_out,
    )
    pred_own, pred_other, keep, send, noise = pl.pallas_call(
        lambda *refs: step_kernel(*refs, scale_den=scale_den),
        in_specs=[smem] + [vmem] * 6 + [pl.BlockSpec(memory_space=pl.ANY)] * 4 + [hbm] * 10,
        out_specs=[hbm] * 4 + [vmem],
        scratch_shapes=[
            pltpu.VMEM(square, BF16),
            pltpu.VMEM(square, BF16),
            pltpu.VMEM(square, BF16),
            pltpu.VMEM((window, slots), F32),
            pltpu.VMEM((channels, slots), F32),
            pltpu.VMEM((channels, slots), F32),
            pltpu.VMEM((1, slots), F32),
            pltpu.VMEM(cond_scale.shape, F32),
            pltpu.VMEM(cond_shift.shape, F32),
            pltpu.VMEM(attn_qkv.shape, BF16),
            pltpu.VMEM(attn_out.shape, BF16),
            pltpu.VMEM(dec_kv.shape, BF16),
            pltpu.VMEM(dec_out.shape, BF16),
            pltpu.VMEM(head_out.shape, BF16),
            pltpu.VMEM((2, channels, slots), F32),
            pltpu.VMEM((2, *half_shape), BF16),
            pltpu.VMEM((outer, dim), BF16),
            pltpu.VMEM((dim, outer), BF16),
            pltpu.VMEM((dim, window), BF16),
            pltpu.VMEM((window, window), F32),
            pltpu.VMEM((2, dim, window), BF16),
            pltpu.VMEM((2, outer, 2 * dim), BF16),
            pltpu.VMEM((2, heads, window, window), BF16),
            pltpu.VMEM((2, dim, window), BF16),
            pltpu.VMEM((2, window, dim), BF16),
            pltpu.VMEM((2, window, dim), BF16),
            pltpu.VMEM((2, window, 2 * dim), BF16),
            pltpu.VMEM((2, heads, window, slots), BF16),
            pltpu.VMEM((2, dim, slots), BF16),
            pltpu.VMEM((2, dim, slots), BF16),
            pltpu.VMEM((2, dim, slots), BF16),
            pltpu.VMEM((2, channel_pad, slots), F32),
            pltpu.VMEM((2, channel_pad, slots), BF16),
            pltpu.VMEM((channel_pad, dim), BF16),
            pltpu.VMEM((2, window, 2 * dim), BF16),
            pltpu.VMEM((outer, 2 * dim), F32),
            pltpu.SemaphoreType.DMA((14,)),
            pltpu.SemaphoreType.DMA((4,)),
        ],
        out_shape=[
            jax.ShapeDtypeStruct((channels, slots), F32),
            jax.ShapeDtypeStruct((channels, slots), F32),
            jax.ShapeDtypeStruct(half_shape, BF16),
            jax.ShapeDtypeStruct(half_shape, BF16),
            jax.ShapeDtypeStruct((2, noise_size, rows), F32),
        ],
        compiler_params=pltpu.CompilerParams(vmem_limit_bytes=ALL_VMEM),
        cost_estimate=pl.CostEstimate(
            flops=10**10, bytes_accessed=12 * 2**20, transcendentals=2**21
        ),
        name="step",
    )(grid_counts, *step_in)

    def twin_swap(value):
        return permute(value, lambda m, k: (m, k ^ 1))

    groups = [
        [m * size + k for m in range(2) for k in range(size) if k % 2 == c] for c in range(2)
    ]

    def over_chips(value):
        return lax.all_to_all(value, axes, 0, 0, axis_index_groups=groups)

    arrived_pred = permute(pred_other, lambda m, k: (1 - m, k))
    pair = (keep.astype(F32) + twin_swap(send).astype(F32)).astype(BF16)
    pair, arrived_pred = lax.optimization_barrier((pair, arrived_pred))
    parts = over_chips(pair)
    shared, prediction = pl.pallas_call(
        sum_kernel,
        in_specs=[vmem, hbm, hbm],
        out_specs=[vmem, hbm],
        out_shape=[
            jax.ShapeDtypeStruct(half_shape, BF16),
            jax.ShapeDtypeStruct((1, channels, grid_slots), F32),
        ],
        scratch_shapes=[pltpu.SemaphoreType.DMA((2,))],
        compiler_params=pltpu.CompilerParams(vmem_limit_bytes=32 * 2**20),
        name="sum",
    )(parts, pred_own, arrived_pred)
    mine = over_chips(shared)
    theirs = twin_swap(mine)
    grad_shapes = [
        jax.ShapeDtypeStruct(shape, F32)
        for shape in (
            cond_scale.shape,
            cond_shift.shape,
            attn_qkv.shape,
            attn_out.shape,
            dec_query.shape,
            dec_kv.shape,
            dec_out.shape,
            head_out.shape,
            (1, HEAD),
        )
    ]
    outputs = pl.pallas_call(
        unpack_kernel,
        in_specs=[pl.BlockSpec(memory_space=pl.ANY)] * 2 + [vmem],
        out_specs=[vmem] * 9,
        out_shape=grad_shapes,
        scratch_shapes=[pltpu.VMEM((2, *half_shape), BF16), pltpu.SemaphoreType.DMA((2,))],
        compiler_params=pltpu.CompilerParams(vmem_limit_bytes=40 * 2**20),
        name="unpack",
    )(mine, theirs, noise)
    return (prediction, *outputs[:8], outputs[8][0, 0])


def solution(mesh):
    in_specs = (
        P("space", None),
        P("space", None),
        P(None, "space"),
        P(None, "space"),
        P("space"),
        P("member", None),
        P(None, "space"),
        P(None, "space"),
        P(None, "space"),
        P(None, "space"),
        P("space"),
        P(),
        P(),
        P(),
        P(),
        P(),
        P(),
        P(),
        P(),
    )
    out_specs = (P("member", None, "space"), P(), P(), P(), P(), P(), P(), P(), P(), P())
    return jax.shard_map(
        per_device, mesh=mesh, in_specs=in_specs, out_specs=out_specs, check_vma=False
    )
```

```python
import math

import jax
import jax.numpy as jnp
from jax import lax
from jax.experimental import pallas as pl
from jax.experimental.pallas import tpu as pltpu
from jax.sharding import PartitionSpec as P

HEAD = 128
EPSILON = 1e-05
LOSS_SCALE = 65536.0
SMOOTHING = 0.0625
FAR = -1e30
TILE = 256
LOG2E = math.log2(math.e)
ALL_VMEM = 62 * 2**20

F32 = jnp.float32
BF16 = jnp.bfloat16


def nn(first, second):
    return lax.dot_general(first, second, (((1,), (0,)), ((), ())), preferred_element_type=F32)


def nt(first, second):
    return lax.dot_general(first, second, (((1,), (1,)), ((), ())), preferred_element_type=F32)


def tn(first, second):
    return lax.dot_general(first, second, (((0,), (0,)), ((), ())), preferred_element_type=F32)


def normalize(values, axis):
    center = values - jnp.mean(values, axis=axis, keepdims=True)
    spread = jnp.mean(center * center, axis=axis, keepdims=True)
    scale = lax.rsqrt(spread + EPSILON)
    return center * scale, scale


def normalize_back(values, grad_out, axis):
    unit, scale = normalize(values, axis)
    mean_grad = jnp.mean(grad_out, axis=axis, keepdims=True)
    mean_unit = jnp.mean(grad_out * unit, axis=axis, keepdims=True)
    return scale * (grad_out - mean_grad - unit * mean_unit)


def spread_bias(slots, bias, rows):
    entries, width = slots.shape
    row_ids = lax.broadcasted_iota(jnp.int32, (rows, width), 0)
    logits = jnp.full((rows, width), FAR, F32)
    for entry in range(entries):
        same = slots == slots[entry : entry + 1]
        top = jnp.max(jnp.where(same, bias, FAR), axis=0, keepdims=True)
        terms = jnp.sum(jnp.where(same, jnp.exp(bias - top), 0.0), axis=0, keepdims=True)
        logits = jnp.where(row_ids == slots[entry : entry + 1], (top + jnp.log(terms)) * LOG2E, logits)
    return logits


def add_entry(slots, bias, entry, logits):
    place = slots[pl.ds(entry, 1), :]
    same = slots[...] == place
    top = jnp.max(jnp.where(same, bias[...], FAR), axis=0, keepdims=True)
    terms = jnp.sum(jnp.where(same, jnp.exp(bias[...] - top), 0.0), axis=0, keepdims=True)
    row_ids = lax.broadcasted_iota(jnp.int32, logits.shape, 0)
    logits[...] = jnp.where(row_ids == place, (top + jnp.log(terms)) * LOG2E, logits[...])


def softmax_rows(scores):
    terms = jnp.exp2(scores - jnp.max(scores, axis=0, keepdims=True))
    return terms * (1.0 / jnp.sum(terms, axis=0, keepdims=True))


def score_back(probs, grad_probs):
    probs = probs.astype(F32)
    inner = jnp.sum(probs * grad_probs, axis=0, keepdims=True)
    return probs * (grad_probs - inner) * (1.0 / math.sqrt(HEAD))


def split_terms(values):
    high = values.astype(BF16)
    rest = values - high.astype(F32)
    middle = rest.astype(BF16)
    low = (rest - middle.astype(F32)).astype(BF16)
    return high, middle, low


def joined_terms(high, middle, low):
    return high.astype(F32) + (middle.astype(F32) + low.astype(F32))


def window_start(rows):
    return lax.axis_index("space") * rows - rows // 2


def pack_kernel(latent, nbrs, bias, noise, packet, upward, downward, *, total):
    rows = latent.shape[0]
    halo = rows // 2
    packet[:rows] = latent[...]
    downward[...] = latent[:halo]
    slots = ((nbrs[...] - window_start(rows)) & (total - 1)).astype(F32).astype(BF16)
    packet[rows:] = jnp.concatenate([slots, *split_terms(bias[...])], axis=1)
    upward[:halo] = latent[halo:]
    spare = jnp.zeros((1, rows - noise.shape[1]), F32)
    padded = jnp.concatenate([noise[...], spare], axis=1)
    padded = jnp.broadcast_to(padded, (upward.shape[0] - halo, rows))
    terms = split_terms(padded)
    upward[halo:] = jnp.concatenate([*terms, jnp.zeros_like(terms[0])], axis=1)


def prepare_kernel(
    embed_hbm,
    nbrs_hbm,
    bias_hbm,
    weight_hbm,
    embed_t,
    norm_t,
    query_t,
    logits,
    embed,
    nbrs,
    bias,
    dec_query,
    weight_t,
    sems,
    *,
    rows,
    halo,
    total,
):
    slots = embed.shape[0]
    here = pl.ds(pl.multiple_of(lax.axis_index("member") * slots, slots), slots)
    copies = [
        pltpu.make_async_copy(embed_hbm.at[here, :], embed, sems.at[0]),
        pltpu.make_async_copy(nbrs_hbm.at[:, here], nbrs, sems.at[1]),
        pltpu.make_async_copy(bias_hbm.at[:, here], bias, sems.at[2]),
        pltpu.make_async_copy(weight_hbm, dec_query, sems.at[3]),
    ]
    for copy in copies:
        copy.start()
    copies[1].wait()
    copies[2].wait()
    local = (nbrs[...] - window_start(rows)) & (total - 1)
    places = jnp.where(
        local < halo, local + rows, jnp.where(local < halo + rows, local - halo, local)
    )
    logits[...] = spread_bias(places, bias[...], rows + 2 * halo)
    copies[0].wait()
    copies[3].wait()
    weight_t[...] = dec_query[...].T

    @pl.loop(0, slots // TILE)
    def _(i):
        tile = pl.ds(pl.multiple_of(i * TILE, TILE), TILE)
        values = embed[tile, :].T
        embed_t[:, tile] = values
        norm = normalize(values.astype(F32), 0)[0].astype(BF16)
        norm_t[:, tile] = norm
        query_t[:, tile] = nn(weight_t[...], norm).astype(BF16)


def window_order(values, rows, halo):
    first = 2 * halo + halo
    return jnp.concatenate(
        [
            values[first : first + rows],
            values[first - halo : first],
            values[first + rows : first + rows + halo],
        ],
        axis=0,
    )


def each(count):
    def run(body):
        for i in range(count):
            body(i)

    return run


def step_kernel(
    counts,
    packet,
    twin,
    beside,
    below,
    above,
    noise_own,
    embed_hbm,
    norm_hbm,
    query_hbm,
    logits_hbm,
    weather_hbm,
    target_hbm,
    area_hbm,
    scale_hbm,
    shift_hbm,
    qkv_hbm,
    attn_out_hbm,
    dec_kv_hbm,
    dec_out_hbm,
    head_hbm,
    pred_own_hbm,
    pred_other_hbm,
    keep_hbm,
    send_hbm,
    noise_out,
    embed_t,
    norm_t,
    query_t,
    grid_logits,
    weather,
    target,
    area,
    cond_scale,
    cond_shift,
    attn_qkv,
    attn_out,
    dec_kv,
    dec_out,
    head_out,
    pred,
    grads,
    latent,
    latent_q,
    units,
    acts,
    acts_q,
    affine,
    affine_t,
    sums,
    col_sums,
    scores,
    unit_t,
    unit_q_t,
    list_slots,
    list_bias,
    mesh_logits,
    mesh_query,
    mesh_kv,
    mesh_probs,
    mesh_grad_scores,
    mesh_mixed,
    mesh_grad_mixed,
    mesh_out,
    mesh_grad_out,
    mesh_norm,
    mesh_norm_t,
    dec_keys,
    grid_probs,
    grid_grad_scores,
    grid_mixed,
    grid_grad_out,
    grid_grad_mixed,
    grid_out,
    grid_final,
    change,
    grad_change,
    head_pad,
    head_t,
    dec_out_t,
    grad_query,
    grad_dec,
    grad_q,
    grad_kv,
    load_sems,
    store_sems,
    *,
    scale_den,
):
    halo, dim = above.shape
    rows = 2 * halo
    window = rows + 2 * halo
    outer = 2 * window
    own = packet[:rows]
    edges = packet[rows:]
    heads = dim // HEAD
    members = 2
    channels = weather.shape[0]
    slots = embed_t.shape[1]
    inv_sqrt = LOG2E / math.sqrt(HEAD)
    member = lax.axis_index("member")
    core = lax.rem(lax.axis_index("space"), 2)
    here = pl.ds(pl.multiple_of(member * slots, slots), slots)

    loads = {}

    def load(name, source, target_ref):
        loads[name] = pltpu.make_async_copy(source, target_ref, load_sems.at[len(loads)])

    def start(*group):
        for name in group:
            loads[name].start()

    load("qkv", qkv_hbm, attn_qkv)
    load("scale", scale_hbm, cond_scale)
    load("shift", shift_hbm, cond_shift)
    load("attn_out", attn_out_hbm, attn_out)
    load("dec_kv", dec_kv_hbm, dec_kv)
    load("query", query_hbm, query_t)
    load("logits", logits_hbm, grid_logits)
    load("embed", embed_hbm, embed_t)
    load("dec_out", dec_out_hbm, dec_out)
    load("head", head_hbm, head_out)
    load("weather", weather_hbm.at[:, here], weather)
    load("target", target_hbm.at[:, here], target)
    load("area", area_hbm.at[:, here], area)
    load("norm", norm_hbm, norm_t)
    start("qkv", "scale", "shift")

    odd = core == 1
    latent[0:halo] = below[:halo]
    latent[halo : halo + rows] = jnp.where(odd, twin[:rows], beside[:rows])
    latent[halo + rows : halo + 2 * rows] = own
    latent[halo + 2 * rows : halo + 3 * rows] = jnp.where(odd, beside[:rows], twin[:rows])
    latent[halo + 3 * rows :] = above[...]
    lane = lax.broadcasted_iota(jnp.int32, (edges.shape[0], rows), 1)
    late = (lane >= halo) == odd
    ends = jnp.where(
        jnp.concatenate([late] * 4, axis=1), twin[rows:].astype(F32), beside[rows:].astype(F32)
    )
    lists = edges.astype(F32)

    def listed(part):
        return [
            lists[:, part * rows : (part + 1) * rows],
            pltpu.roll(ends[:, part * rows : (part + 1) * rows], halo, 1),
        ]

    list_slots[...] = jnp.concatenate(listed(0), axis=1).astype(jnp.int32)
    list_bias[...] = joined_terms(*(jnp.concatenate(listed(part), axis=1) for part in (1, 2, 3)))
    mesh_logits[...] = jnp.full(mesh_logits.shape, FAR, F32)

    @pl.loop(0, list_slots.shape[0])
    def _(entry):
        add_entry(list_slots, list_bias, entry, mesh_logits)

    noise_row = joined_terms(*(below[halo:, part * rows : (part + 1) * rows] for part in (0, 1, 2)))
    spread = cond_scale.shape[0]
    own_row = jnp.concatenate([noise_own[...], jnp.zeros((1, rows - spread), F32)], axis=1)
    noise = []
    for m, row in enumerate((own_row, noise_row[:1])):
        columns = jnp.broadcast_to(row, (rows, rows)).T[:spread]
        noise_out[m] = columns
        noise.append(columns[:, :1])
    is_before = lax.broadcasted_iota(jnp.int32, (window, rows), 1) < halo
    inner = slice(rows, rows + window)

    def compact(full):
        return full[inner, :rows], jnp.where(is_before, full[:window, rows:], full[window:, rows:])

    def spread_out(target_ref, middle, ends):
        target_ref[inner, :rows] = middle.astype(BF16)
        target_ref[:window, rows:] = jnp.where(is_before, ends, 0.0).astype(BF16)
        target_ref[window:, rows:] = jnp.where(is_before, 0.0, ends).astype(BF16)

    def tile_of(index, size=TILE, base=0):
        if isinstance(index, int):
            return slice(base + index * size, base + (index + 1) * size)
        return pl.ds(pl.multiple_of(base + index * size, size), size)

    @each(members * heads)
    def _(i):
        mesh_probs[i, :rows, :rows] = jnp.zeros((rows, rows), BF16)
        mesh_probs[i, rows + window :, :rows] = jnp.zeros((rows, rows), BF16)
        mesh_grad_scores[i, :rows, :rows] = jnp.zeros((rows, rows), BF16)
        mesh_grad_scores[i, rows + window :, :rows] = jnp.zeros((rows, rows), BF16)

    loads["scale"].wait()
    loads["shift"].wait()
    gains = []
    shifts = []
    for m in range(members):
        gains.append(1.0 + jnp.sum(noise[m] * cond_scale[...], axis=0, keepdims=True))
        shifts.append(jnp.sum(noise[m] * cond_shift[...], axis=0, keepdims=True))
        affine[2 * m : 2 * m + 1] = gains[m]
        affine[2 * m + 1 : 2 * m + 2] = shifts[m]

    @each(outer // rows)
    def _(i):
        tile = tile_of(i, rows)
        unit = normalize(latent[tile, :].astype(F32), 1)[0]
        units[tile, :] = unit.astype(BF16)
        unit_t[:dim, tile] = unit.astype(BF16).T
        for m in range(members):
            act = unit * affine[2 * m : 2 * m + 1] + affine[2 * m + 1 : 2 * m + 2]
            acts[tile_of(i, rows, m * outer), :] = act.astype(BF16)

    latent_q[...] = window_order(latent, rows, halo)
    unit_q_t[:dim] = window_order(units, rows, halo).T
    unit_q_t[dim:] = jnp.ones((16, window), BF16)
    unit_t[dim:] = jnp.ones((16, outer), BF16)
    for m in range(members):
        acts_q[m * window : (m + 1) * window] = window_order(
            acts.at[m * outer : (m + 1) * outer], rows, halo
        )

    start("attn_out", "dec_kv")
    loads["qkv"].wait()
    start("query", "logits", "embed", "dec_out", "head", "weather", "target", "area", "norm")

    @each(dim // TILE)
    def _(i):
        part = nn(acts_q[...], attn_qkv[:, tile_of(i)]).astype(BF16)
        mesh_query[tile_of(i), :] = part.T

    @each(2 * dim // TILE)
    def _(i):
        mesh_kv[:, tile_of(i)] = nn(acts[...], attn_qkv[:, tile_of(i, TILE, dim)]).astype(BF16)

    pairs = [(m * heads + h, m, h) for m in range(members) for h in range(heads)]

    def span(index, size, base=0):
        return slice(base + index * size, base + (index + 1) * size)

    for i, m, h in pairs:
        keys = mesh_kv[span(m, outer), span(h, HEAD)]
        middle, ends = compact(nn(keys, mesh_query[span(h, HEAD), span(m, window)]))
        scores[i, :, :rows] = middle
        scores[i, :, rows:window] = ends

    @each(members * heads)
    def _(i):
        parts = [
            softmax_rows(scores[i, :, lanes] * inv_sqrt + mesh_logits[:, lanes])
            for lanes in (span(0, rows), span(1, rows))
        ]
        spread_out(mesh_probs.at[i], *parts)

    for i, m, h in pairs:
        values = mesh_kv[span(m, outer), span(h, HEAD, dim)]
        mesh_mixed[span(h, HEAD), span(m, window)] = tn(values, mesh_probs[i]).astype(BF16)

    loads["attn_out"].wait()

    @each(members)
    def _(m):
        here_q = tile_of(m, window)
        mixed = mesh_mixed[:, here_q].T
        out = (latent_q[...].astype(F32) + nn(mixed, attn_out[...])).astype(BF16)
        mesh_out[here_q, :] = out
        norm = normalize(out.astype(F32), 1)[0].astype(BF16)
        mesh_norm[here_q, :] = norm
        mesh_norm_t[:, here_q] = norm.T

    loads["dec_kv"].wait()

    @each(2 * dim // TILE)
    def _(i):
        dec_keys[:, tile_of(i)] = nn(mesh_norm[...], dec_kv[:, tile_of(i)]).astype(BF16)

    for name in ("query", "logits", "embed", "dec_out", "head"):
        loads[name].wait()
    head_pad[...] = jnp.zeros_like(head_pad)
    head_pad[:channels] = head_out[...]
    head_t[...] = head_pad[...].T
    dec_out_t[...] = dec_out[...].T

    for i, m, h in pairs:
        scores[i] = nn(dec_keys[span(m, window), span(h, HEAD)], query_t[span(h, HEAD), :])

    @each(members * heads)
    def _(i):
        for t in range(slots // HEAD):
            lanes = span(t, HEAD)
            probs = softmax_rows(scores[i, :, lanes] * inv_sqrt + grid_logits[:, lanes])
            grid_probs[i, :, lanes] = probs.astype(BF16)

    for i, m, h in pairs:
        values = dec_keys[span(m, window), span(h, HEAD, dim)]
        grid_mixed[span(h, HEAD), span(m, slots)] = tn(values, grid_probs[i]).astype(BF16)

    for m in range(members):
        out = embed_t[...].astype(F32) + nn(dec_out_t[...], grid_mixed[:, span(m, slots)])
        grid_out[:, span(m, slots)] = out.astype(BF16)

    lane_tiles = members * slots // HEAD

    @each(lane_tiles)
    def _(i):
        tile = tile_of(i, HEAD)
        final = normalize(grid_out[:, tile].astype(F32), 0)[0].astype(BF16)
        grid_final[:, tile] = final

    change[...] = nn(head_pad[...], grid_final[...])

    for name in ("weather", "target", "area", "norm"):
        loads[name].wait()
    def smooth(values):
        square = values * values + SMOOTHING
        inverse = lax.rsqrt(square)
        return square * inverse, values * inverse

    grad_change[...] = jnp.zeros_like(grad_change)

    def compare(i, loss):
        tile = tile_of(i, HEAD)
        slot = lax.broadcasted_iota(jnp.int32, (1, HEAD), 1) + (member * slots + i * HEAD)
        live = jnp.where(slot < counts[0], 1.0, 0.0)
        weighting = live * area[:, tile]
        second_tile = tile_of(i, HEAD, slots)
        first = weather[:, tile] + live * change[:channels, tile]
        second = weather[:, tile] + live * change[:channels, second_tile]
        pred[0, :, tile] = first
        pred[1, :, tile] = second
        size_first, slope_first = smooth(first - target[:, tile])
        size_second, slope_second = smooth(second - target[:, tile])
        size_pair, slope_pair = smooth(first - second)
        factor = weighting * (LOSS_SCALE / scale_den)
        grad_change[:channels, tile] = (factor * (slope_first - slope_pair)).astype(BF16)
        grad_change[:channels, second_tile] = (factor * (slope_second + slope_pair)).astype(BF16)
        terms = weighting * (size_first + size_second - size_pair)
        return loss + jnp.sum(terms, axis=0, keepdims=True)

    loss = lax.fori_loop(0, slots // HEAD, compare, jnp.zeros((1, HEAD), F32))
    loss = jnp.sum(loss) / scale_den
    stores = [
        pltpu.make_async_copy(pred.at[0], pred_own_hbm, store_sems.at[0]),
        pltpu.make_async_copy(pred.at[1], pred_other_hbm, store_sems.at[1]),
    ]
    for store in stores:
        store.start()

    tall = HEAD * HEAD // dim
    per_block = dim // tall

    def pack(index, tile, block):
        half, chunk = index // 4, index % 4 * per_block
        for c in range(per_block):
            for t in range(TILE // HEAD):
                where = tile_of(tile * (TILE // HEAD) + t, tall)
                part = block[c * tall : (c + 1) * tall, t * HEAD : (t + 1) * HEAD]
                grads[half, chunk + c, where, :] = part.astype(BF16)

    col_tiles = dim // TILE

    def pack_extras(half, chunk, values):
        for i in range(values.shape[0] // 8):
            for t in range(heads):
                grads[half, chunk + i * heads + t, HEAD:, :] = values[
                    i * 8 : (i + 1) * 8, t * HEAD : (t + 1) * HEAD
                ].astype(BF16)

    def ship(half, first, last, sem):
        source = grads.at[half, first:last]
        keep = pltpu.make_async_copy(source, keep_hbm.at[first:last], store_sems.at[sem])
        send = pltpu.make_async_copy(source, send_hbm.at[first:last], store_sems.at[sem])
        pl.when(core == half)(keep.start)
        pl.when(core != half)(send.start)
        stores.append(keep)

    grads[:, :, HEAD:, :] = jnp.zeros((2, 4 * per_block, 8, HEAD), BF16)

    pack_extras(1, 0, nt(grad_change[...], grid_final[...]))

    @each(lane_tiles)
    def _(i):
        tile = tile_of(i, HEAD)
        g_final = nn(head_t[...], grad_change[:, tile])
        g_out = normalize_back(grid_out[:, tile].astype(F32), g_final, 0).astype(BF16)
        grid_grad_out[:, tile] = g_out

    for m in range(members):
        g_mixed = nn(dec_out[...], grid_grad_out[:, span(m, slots)])
        grid_grad_mixed[:, span(m, slots)] = g_mixed.astype(BF16)

    @each(col_tiles)
    def _(i):
        pack(7, i, nt(grid_mixed[...], grid_grad_out[tile_of(i), :]))

    for i, m, h in pairs:
        values = dec_keys[span(m, window), span(h, HEAD, dim)]
        scores[i] = nn(values, grid_grad_mixed[span(h, HEAD), span(m, slots)])

    @each(members * heads)
    def _(i):
        here = tile_of(i % heads * members + i // heads, window)
        for t in range(slots // HEAD):
            lanes = span(t, HEAD)
            grid_grad_scores[here, lanes] = score_back(
                grid_probs[i, :, lanes], scores[i, :, lanes]
            ).astype(BF16)

    for i, m, h in pairs:
        g_scores = grid_grad_scores[span(h * members + m, window), :]
        g_head = grid_grad_mixed[span(h, HEAD), span(m, slots)]
        probs = grid_probs[i]
        grad_dec[span(m, window), span(h, HEAD)] = nt(g_scores, query_t[span(h, HEAD), :]).astype(BF16)
        grad_dec[span(m, window), span(h, HEAD, dim)] = nt(probs, g_head).astype(BF16)
    for h in range(heads):
        keys = dec_keys[:, span(h, HEAD)]
        g_scores = grid_grad_scores[span(h, members * window), :]
        grad_query[span(h, HEAD), :] = tn(keys, g_scores).astype(BF16)

    @each(col_tiles)
    def _(i):
        pack(4, i, nt(norm_t[...], grad_query[tile_of(i), :]))

    @each(2 * col_tiles)
    def _(i):
        block = nn(mesh_norm_t[...], grad_dec[:, tile_of(i)])
        pack(5 + i // col_tiles, i % col_tiles, block)

    ship(1, 0, 4 * per_block, 2)

    @each(members)
    def _(m):
        here_q = tile_of(m, window)
        g_norm = nt(grad_dec[here_q, :], dec_kv[...])
        g_out = normalize_back(mesh_out[here_q, :].astype(F32), g_norm, 1).astype(BF16)
        mesh_grad_out[here_q, :] = g_out
        mesh_grad_mixed[:, here_q] = nt(attn_out[...], g_out).astype(BF16)

    @each(col_tiles)
    def _(i):
        pack(3, i, nn(mesh_mixed[...], mesh_grad_out[:, tile_of(i)]))

    for i, m, h in pairs:
        values = mesh_kv[span(m, outer), span(h, HEAD, dim)]
        middle, ends = compact(nn(values, mesh_grad_mixed[span(h, HEAD), span(m, window)]))
        scores[i, :, :rows] = middle
        scores[i, :, rows:window] = ends

    @each(members * heads)
    def _(i):
        parts = [
            score_back(probs, scores[i, :, lanes])
            for probs, lanes in zip(compact(mesh_probs[i]), (span(0, rows), span(1, rows)))
        ]
        spread_out(mesh_grad_scores.at[i], *parts)

    for i, m, h in pairs:
        cols = span(h, HEAD)
        g_scores = mesh_grad_scores[i]
        g_head = mesh_grad_mixed[cols, span(m, window)]
        g_query = tn(mesh_kv[span(m, outer), cols], g_scores).astype(BF16)
        grad_q[span(m, window), cols] = g_query.T
        grad_kv[span(m, outer), cols] = nt(g_scores, mesh_query[cols, span(m, window)]).astype(BF16)
        grad_kv[span(m, outer), span(h, HEAD, dim)] = nt(mesh_probs[i], g_head).astype(BF16)

    for m in range(members):
        gain_col = jnp.broadcast_to(gains[m], (HEAD, dim)).T
        shift_col = jnp.broadcast_to(shifts[m], (HEAD, dim)).T
        affine_t[2 * m] = gain_col
        affine_t[2 * m + 1] = shift_col
    sums[...] = jnp.zeros_like(sums)
    col_sums[...] = jnp.zeros_like(col_sums)

    def project_back(index, tile, weight_tile, left, parts):
        weight = attn_qkv[:, weight_tile].astype(F32)
        total = None
        for m in range(members):
            moment = nn(left[...], parts[m])
            col_sum = moment[dim : dim + 1]
            moment = moment[:dim]
            high, middle, low = split_terms(col_sum)
            for row, value in enumerate((high, middle, low)):
                col_sums[8 * m + row : 8 * m + row + 1, weight_tile] = value.astype(F32)
            by_gain = weight * moment
            sums[m] += by_gain[:, :HEAD] + by_gain[:, HEAD:]
            terms = []
            for t in range(TILE // HEAD):
                lanes = slice(t * HEAD, (t + 1) * HEAD)
                terms.append(
                    affine_t[2 * m] * moment[:, lanes] + affine_t[2 * m + 1] * col_sum[:, lanes]
                )
            term = jnp.concatenate(terms, axis=1)
            total = term if m == 0 else total + term
        pack(index, tile, total)

    @each(2 * col_tiles)
    def _(i):
        parts = [grad_kv[m * outer : (m + 1) * outer, tile_of(i)] for m in range(members)]
        project_back(
            1 + i // col_tiles, i % col_tiles, tile_of(i, TILE, dim), unit_t, parts
        )

    ship(0, per_block, 4 * per_block, 3)

    @each(col_tiles)
    def _(i):
        parts = [grad_q[m * window : (m + 1) * window, tile_of(i)] for m in range(members)]
        project_back(0, i, tile_of(i), unit_q_t, parts)

    row_id = lax.broadcasted_iota(jnp.int32, (8, dim), 0)
    grad_cond = jnp.where(row_id == 4, loss, 0.0)
    g_shifts = nt(attn_qkv[...], col_sums[...].astype(BF16))
    for m in range(members):
        mine = member if m == 0 else 1 - member
        g_shift = g_shifts[:, 8 * m : 8 * m + 3]
        for row, lanes in ((mine, sums[m]), (mine + 2, g_shift)):
            column = jnp.sum(lanes, axis=1, keepdims=True)
            values = jnp.broadcast_to(column, (dim, HEAD)).T[:8]
            grad_cond += jnp.where(row_id == row, values, 0.0)
    pack_extras(0, 0, grad_cond)
    ship(0, 0, per_block, 4)
    for store in stores:
        store.wait()


def sum_kernel(parts, pred_own_hbm, pred_arrived_hbm, result, pred_hbm, sems):
    slots = pred_own_hbm.shape[1]
    member = lax.axis_index("member")
    here = pl.ds(pl.multiple_of(member * slots, slots), slots)
    there = pl.ds(pl.multiple_of((1 - member) * slots, slots), slots)
    copies = [
        pltpu.make_async_copy(pred_own_hbm, pred_hbm.at[0, :, here], sems.at[0]),
        pltpu.make_async_copy(pred_arrived_hbm, pred_hbm.at[0, :, there], sems.at[1]),
    ]
    for copy in copies:
        copy.start()
    total = jnp.sum(parts[...].astype(F32), axis=0, keepdims=True)
    result[...] = jnp.broadcast_to(total.astype(BF16), result.shape)
    for copy in copies:
        copy.wait()


def unpack_kernel(
    mine_hbm,
    theirs_hbm,
    noise,
    grad_scale,
    grad_shift,
    grad_qkv,
    grad_attn_out,
    grad_dec_query,
    grad_dec_kv,
    grad_dec_out,
    grad_head,
    loss,
    grads,
    sems,
):
    member = lax.axis_index("member")
    core = lax.rem(lax.axis_index("space"), 2)
    channels = grad_head.shape[0]
    dim = grad_attn_out.shape[0]
    heads = dim // HEAD
    copies = [
        pltpu.make_async_copy(mine_hbm, grads.at[core], sems.at[0]),
        pltpu.make_async_copy(theirs_hbm, grads.at[1 - core], sems.at[1]),
    ]
    for copy in copies:
        copy.start()
    for copy in copies:
        copy.wait()
    tall = HEAD * HEAD // dim
    targets = (
        (grad_qkv, 0),
        (grad_qkv, dim),
        (grad_qkv, 2 * dim),
        (grad_attn_out, 0),
        (grad_dec_query, 0),
        (grad_dec_kv, 0),
        (grad_dec_kv, dim),
        (grad_dec_out, 0),
    )
    per_block = dim // tall

    @pl.loop(0, per_block)
    def _(c):
        tile = pl.ds(pl.multiple_of(c * tall, tall), tall)
        for i, (ref, col) in enumerate(targets):
            for t in range(heads):
                ref[tile, col + t * HEAD : col + (t + 1) * HEAD] = grads[
                    i // 4, i % 4 * per_block + c, t * tall : (t + 1) * tall, :
                ].astype(F32)

    def extra(half, i):
        return jnp.concatenate(
            [grads[half, i * heads + t, HEAD:, :].astype(F32) for t in range(heads)], axis=1
        )

    for i in range(-(-channels // 8)):
        count = min(8, channels - i * 8)
        grad_head[i * 8 : i * 8 + count] = extra(1, i)[:count]
    cond = extra(0, 0)
    first = cond[0:1]
    second = cond[1:2]
    grad_scale[...] = noise[0, :, :1] * jnp.where(member == 0, first, second) + noise[
        1, :, :1
    ] * jnp.where(member == 0, second, first)
    first = cond[2:3]
    second = cond[3:4]
    grad_shift[...] = noise[0, :, :1] * jnp.where(member == 0, first, second) + noise[
        1, :, :1
    ] * jnp.where(member == 0, second, first)
    loss[...] = cond[4:5, :HEAD]


def whole(shape):
    return pl.BlockSpec(shape, lambda *_: (0,) * len(shape))


def per_device(
    mesh_latent,
    grid_embed,
    weather_state,
    target,
    cell_area,
    member_noise,
    mesh_nbrs,
    mesh_bias,
    grid_nbrs,
    grid_bias,
    grid_counts,
    cond_scale,
    cond_shift,
    attn_qkv,
    attn_out,
    dec_query,
    dec_kv,
    dec_out,
    head_out,
):
    rows, dim = mesh_latent.shape
    halo = rows // 2
    window = rows + 2 * halo
    outer = 2 * window
    size = lax.axis_size("space")
    grid_slots = grid_embed.shape[0]
    slots = grid_slots // 2
    channels = weather_state.shape[0]
    total = rows * size
    heads = dim // HEAD
    noise_size = member_noise.shape[1]
    entries = grid_nbrs.shape[0]
    scale_den = 2.0 * channels * grid_slots * size

    axes = ("member", "space")

    def permute(value, target_of):
        pairs = []
        for m in range(2):
            for k in range(size):
                to_m, to_k = target_of(m, k)
                pairs.append((m * size + k, to_m * size + to_k % size))
        return lax.ppermute(value, axes, pairs)

    smem = pl.BlockSpec(memory_space=pltpu.SMEM)
    vmem = pl.BlockSpec(memory_space=pltpu.VMEM)
    hbm = pl.BlockSpec(memory_space=pltpu.HBM)
    packet, upward, downward = pl.pallas_call(
        lambda *refs: pack_kernel(*refs, total=total),
        in_specs=[vmem] * 4,
        out_shape=[
            jax.ShapeDtypeStruct((rows + mesh_nbrs.shape[0], dim), BF16),
            jax.ShapeDtypeStruct((halo + 16, dim), BF16),
            jax.ShapeDtypeStruct((halo, dim), BF16),
        ],
        compiler_params=pltpu.CompilerParams(vmem_limit_bytes=ALL_VMEM),
        name="pack",
    )(mesh_latent, mesh_nbrs, mesh_bias, member_noise)
    twin = permute(packet, lambda m, k: (m, k ^ 1))
    beside = permute(packet, lambda m, k: (m, k + 1 if k % 2 else k - 1))
    below = permute(upward, lambda m, k: (1 - m, k + 2))
    above = permute(downward, lambda m, k: (m, k - 2))

    square = (dim, slots)
    embed_t, norm_t, query_t, grid_logits = pl.pallas_call(
        lambda *refs: prepare_kernel(*refs, rows=rows, halo=halo, total=total),
        in_specs=[hbm] * 4,
        out_specs=[vmem] * 4,
        out_shape=[
            jax.ShapeDtypeStruct(square, BF16),
            jax.ShapeDtypeStruct(square, BF16),
            jax.ShapeDtypeStruct(square, BF16),
            jax.ShapeDtypeStruct((window, slots), F32),
        ],
        scratch_shapes=[
            pltpu.VMEM((slots, dim), BF16),
            pltpu.VMEM((entries, slots), jnp.int32),
            pltpu.VMEM((entries, slots), F32),
            pltpu.VMEM((dim, dim), BF16),
            pltpu.VMEM((dim, dim), BF16),
            pltpu.SemaphoreType.DMA((4,)),
        ],
        compiler_params=pltpu.CompilerParams(vmem_limit_bytes=ALL_VMEM),
        cost_estimate=pl.CostEstimate(
            flops=2 * dim * dim * slots, bytes_accessed=3 * 2**20, transcendentals=0
        ),
        name="prepare",
    )(grid_embed, grid_nbrs, grid_bias, dec_query)

    channel_pad = -(-channels // 32) * 32
    chunks = size
    half_shape = (chunks, HEAD + 8, HEAD)
    step_in = (
        packet,
        twin,
        beside,
        below,
        above,
        member_noise,
        embed_t,
        norm_t,
        query_t,
        grid_logits,
        weather_state,
        target,
        cell_area[None, :],
        cond_scale,
        cond_shift,
        attn_qkv,
        attn_out,
        dec_kv,
        dec_out,
        head_out,
    )
    pred_own, pred_other, keep, send, noise = pl.pallas_call(
        lambda *refs: step_kernel(*refs, scale_den=scale_den),
        in_specs=[smem] + [vmem] * 6 + [pl.BlockSpec(memory_space=pl.ANY)] * 4 + [hbm] * 10,
        out_specs=[hbm] * 4 + [vmem],
        scratch_shapes=[
            pltpu.VMEM(square, BF16),
            pltpu.VMEM(square, BF16),
            pltpu.VMEM(square, BF16),
            pltpu.VMEM((window, slots), F32),
            pltpu.VMEM((channels, slots), F32),
            pltpu.VMEM((channels, slots), F32),
            pltpu.VMEM((1, slots), F32),
            pltpu.VMEM(cond_scale.shape, F32),
            pltpu.VMEM(cond_shift.shape, F32),
            pltpu.VMEM(attn_qkv.shape, BF16),
            pltpu.VMEM(attn_out.shape, BF16),
            pltpu.VMEM(dec_kv.shape, BF16),
            pltpu.VMEM(dec_out.shape, BF16),
            pltpu.VMEM(head_out.shape, BF16),
            pltpu.VMEM((2, channels, slots), F32),
            pltpu.VMEM((2, *half_shape), BF16),
            pltpu.VMEM((outer, dim), BF16),
            pltpu.VMEM((window, dim), BF16),
            pltpu.VMEM((outer, dim), BF16),
            pltpu.VMEM((2 * outer, dim), BF16),
            pltpu.VMEM((2 * window, dim), BF16),
            pltpu.VMEM((8, dim), F32),
            pltpu.VMEM((4, dim, HEAD), F32),
            pltpu.VMEM((2, dim, HEAD), F32),
            pltpu.VMEM((16, 3 * dim), F32),
            pltpu.VMEM((2 * heads, window, slots), F32),
            pltpu.VMEM((dim + 16, outer), BF16),
            pltpu.VMEM((dim + 16, window), BF16),
            pltpu.VMEM((mesh_nbrs.shape[0], window), jnp.int32),
            pltpu.VMEM((mesh_nbrs.shape[0], window), F32),
            pltpu.VMEM((window, window), F32),
            pltpu.VMEM((dim, 2 * window), BF16),
            pltpu.VMEM((2 * outer, 2 * dim), BF16),
            pltpu.VMEM((2 * heads, outer, window), BF16),
            pltpu.VMEM((2 * heads, outer, window), BF16),
            pltpu.VMEM((dim, 2 * window), BF16),
            pltpu.VMEM((dim, 2 * window), BF16),
            pltpu.VMEM((2 * window, dim), BF16),
            pltpu.VMEM((2 * window, dim), BF16),
            pltpu.VMEM((2 * window, dim), BF16),
            pltpu.VMEM((dim, 2 * window), BF16),
            pltpu.VMEM((2 * window, 2 * dim), BF16),
            pltpu.VMEM((2 * heads, window, slots), BF16),
            pltpu.VMEM((2 * heads * window, slots), BF16),
            pltpu.VMEM((dim, 2 * slots), BF16),
            pltpu.VMEM((dim, 2 * slots), BF16),
            pltpu.VMEM((dim, 2 * slots), BF16),
            pltpu.VMEM((dim, 2 * slots), BF16),
            pltpu.VMEM((dim, 2 * slots), BF16),
            pltpu.VMEM((channel_pad, 2 * slots), F32),
            pltpu.VMEM((channel_pad, 2 * slots), BF16),
            pltpu.VMEM((channel_pad, dim), BF16),
            pltpu.VMEM((dim, channel_pad), BF16),
            pltpu.VMEM((dim, dim), BF16),
            pltpu.VMEM((dim, slots), BF16),
            pltpu.VMEM((2 * window, 2 * dim), BF16),
            pltpu.VMEM((2 * window, dim), BF16),
            pltpu.VMEM((2 * outer, 2 * dim), BF16),
            pltpu.SemaphoreType.DMA((14,)),
            pltpu.SemaphoreType.DMA((5,)),
        ],
        out_shape=[
            jax.ShapeDtypeStruct((channels, slots), F32),
            jax.ShapeDtypeStruct((channels, slots), F32),
            jax.ShapeDtypeStruct(half_shape, BF16),
            jax.ShapeDtypeStruct(half_shape, BF16),
            jax.ShapeDtypeStruct((2, noise_size, rows), F32),
        ],
        compiler_params=pltpu.CompilerParams(vmem_limit_bytes=ALL_VMEM),
        cost_estimate=pl.CostEstimate(
            flops=10**10, bytes_accessed=12 * 2**20, transcendentals=2**21
        ),
        name="step",
    )(grid_counts, *step_in)

    def twin_swap(value):
        return permute(value, lambda m, k: (m, k ^ 1))

    groups = [
        [m * size + k for m in range(2) for k in range(size) if k % 2 == c] for c in range(2)
    ]

    def over_chips(value):
        return lax.all_to_all(value, axes, 0, 0, axis_index_groups=groups)

    arrived_pred = permute(pred_other, lambda m, k: (1 - m, k))
    pair = (keep.astype(F32) + twin_swap(send).astype(F32)).astype(BF16)
    pair, arrived_pred = lax.optimization_barrier((pair, arrived_pred))
    parts = over_chips(pair)
    shared, prediction = pl.pallas_call(
        sum_kernel,
        in_specs=[vmem, hbm, hbm],
        out_specs=[vmem, hbm],
        out_shape=[
            jax.ShapeDtypeStruct(half_shape, BF16),
            jax.ShapeDtypeStruct((1, channels, grid_slots), F32),
        ],
        scratch_shapes=[pltpu.SemaphoreType.DMA((2,))],
        compiler_params=pltpu.CompilerParams(vmem_limit_bytes=32 * 2**20),
        name="sum",
    )(parts, pred_own, arrived_pred)
    mine = over_chips(shared)
    theirs = twin_swap(mine)
    grad_shapes = [
        jax.ShapeDtypeStruct(shape, F32)
        for shape in (
            cond_scale.shape,
            cond_shift.shape,
            attn_qkv.shape,
            attn_out.shape,
            dec_query.shape,
            dec_kv.shape,
            dec_out.shape,
            head_out.shape,
            (1, HEAD),
        )
    ]
    outputs = pl.pallas_call(
        unpack_kernel,
        in_specs=[pl.BlockSpec(memory_space=pl.ANY)] * 2 + [vmem],
        out_specs=[vmem] * 9,
        out_shape=grad_shapes,
        scratch_shapes=[pltpu.VMEM((2, *half_shape), BF16), pltpu.SemaphoreType.DMA((2,))],
        compiler_params=pltpu.CompilerParams(vmem_limit_bytes=40 * 2**20),
        name="unpack",
    )(mine, theirs, noise)
    return (prediction, *outputs[:8], outputs[8][0, 0])


def solution(mesh):
    in_specs = (
        P("space", None),
        P("space", None),
        P(None, "space"),
        P(None, "space"),
        P("space"),
        P("member", None),
        P(None, "space"),
        P(None, "space"),
        P(None, "space"),
        P(None, "space"),
        P("space"),
        P(),
        P(),
        P(),
        P(),
        P(),
        P(),
        P(),
        P(),
    )
    out_specs = (P("member", None, "space"), P(), P(), P(), P(), P(), P(), P(), P(), P())
    return jax.shard_map(
        per_device, mesh=mesh, in_specs=in_specs, out_specs=out_specs, check_vma=False
    )
```

```python
import math

import jax
import jax.numpy as jnp
from jax import lax
from jax.experimental import pallas as pl
from jax.experimental.pallas import tpu as pltpu
from jax.sharding import PartitionSpec as P

HEAD = 128
EPSILON = 1e-05
LOSS_SCALE = 65536.0
SMOOTHING = 0.0625
FAR = -1e30
TILE = 256
LOG2E = math.log2(math.e)
ALL_VMEM = 62 * 2**20

F32 = jnp.float32
BF16 = jnp.bfloat16


def nn(first, second):
    return lax.dot_general(first, second, (((1,), (0,)), ((), ())), preferred_element_type=F32)


def nt(first, second):
    return lax.dot_general(first, second, (((1,), (1,)), ((), ())), preferred_element_type=F32)


def tn(first, second):
    return lax.dot_general(first, second, (((0,), (0,)), ((), ())), preferred_element_type=F32)


def normalize(values, axis):
    center = values - jnp.mean(values, axis=axis, keepdims=True)
    spread = jnp.mean(center * center, axis=axis, keepdims=True)
    scale = lax.rsqrt(spread + EPSILON)
    return center * scale, scale


def normalize_back(values, grad_out, axis):
    unit, scale = normalize(values, axis)
    mean_grad = jnp.mean(grad_out, axis=axis, keepdims=True)
    mean_unit = jnp.mean(grad_out * unit, axis=axis, keepdims=True)
    return scale * (grad_out - mean_grad - unit * mean_unit)


def spread_bias(slots, bias, rows):
    entries, width = slots.shape
    row_ids = lax.broadcasted_iota(jnp.int32, (rows, width), 0)
    logits = jnp.full((rows, width), FAR, F32)
    for entry in range(entries):
        same = slots == slots[entry : entry + 1]
        top = jnp.max(jnp.where(same, bias, FAR), axis=0, keepdims=True)
        terms = jnp.sum(jnp.where(same, jnp.exp(bias - top), 0.0), axis=0, keepdims=True)
        logits = jnp.where(row_ids == slots[entry : entry + 1], (top + jnp.log(terms)) * LOG2E, logits)
    return logits


def add_entry(slots, bias, entry, logits):
    place = slots[pl.ds(entry, 1), :]
    same = slots[...] == place
    top = jnp.max(jnp.where(same, bias[...], FAR), axis=0, keepdims=True)
    terms = jnp.sum(jnp.where(same, jnp.exp(bias[...] - top), 0.0), axis=0, keepdims=True)
    row_ids = lax.broadcasted_iota(jnp.int32, logits.shape, 0)
    logits[...] = jnp.where(row_ids == place, (top + jnp.log(terms)) * LOG2E, logits[...])


def softmax_rows(scores):
    terms = jnp.exp2(scores - jnp.max(scores, axis=0, keepdims=True))
    return terms * (1.0 / jnp.sum(terms, axis=0, keepdims=True))


def score_back(probs, grad_probs):
    probs = probs.astype(F32)
    inner = jnp.sum(probs * grad_probs, axis=0, keepdims=True)
    return probs * (grad_probs - inner) * (1.0 / math.sqrt(HEAD))


def split_terms(values):
    high = values.astype(BF16)
    rest = values - high.astype(F32)
    middle = rest.astype(BF16)
    low = (rest - middle.astype(F32)).astype(BF16)
    return high, middle, low


def joined_terms(high, middle, low):
    return high.astype(F32) + (middle.astype(F32) + low.astype(F32))


def window_start(rows):
    return lax.axis_index("space") * rows - rows // 2


def pack_kernel(latent, nbrs, bias, noise, packet, upward, downward, *, total):
    rows = latent.shape[0]
    halo = rows // 2
    packet[:rows] = latent[...]
    downward[...] = latent[:halo]
    slots = ((nbrs[...] - window_start(rows)) & (total - 1)).astype(F32).astype(BF16)
    packet[rows:] = jnp.concatenate([slots, *split_terms(bias[...])], axis=1)
    upward[:halo] = latent[halo:]
    spare = jnp.zeros((1, rows - noise.shape[1]), F32)
    padded = jnp.concatenate([noise[...], spare], axis=1)
    padded = jnp.broadcast_to(padded, (upward.shape[0] - halo, rows))
    terms = split_terms(padded)
    upward[halo:] = jnp.concatenate([*terms, jnp.zeros_like(terms[0])], axis=1)


def prepare_kernel(
    embed_hbm,
    nbrs_hbm,
    bias_hbm,
    weight_hbm,
    embed_t,
    norm_t,
    query_t,
    logits,
    embed,
    nbrs,
    bias,
    dec_query,
    weight_t,
    sems,
    *,
    rows,
    halo,
    total,
):
    slots = embed.shape[0]
    here = pl.ds(pl.multiple_of(lax.axis_index("member") * slots, slots), slots)
    copies = [
        pltpu.make_async_copy(embed_hbm.at[here, :], embed, sems.at[0]),
        pltpu.make_async_copy(nbrs_hbm.at[:, here], nbrs, sems.at[1]),
        pltpu.make_async_copy(bias_hbm.at[:, here], bias, sems.at[2]),
        pltpu.make_async_copy(weight_hbm, dec_query, sems.at[3]),
    ]
    for copy in copies:
        copy.start()
    copies[1].wait()
    copies[2].wait()
    local = (nbrs[...] - window_start(rows)) & (total - 1)
    places = jnp.where(
        local < halo, local + rows, jnp.where(local < halo + rows, local - halo, local)
    )
    logits[...] = spread_bias(places, bias[...], rows + 2 * halo)
    copies[0].wait()
    copies[3].wait()
    weight_t[...] = dec_query[...].T

    @pl.loop(0, slots // TILE)
    def _(i):
        tile = pl.ds(pl.multiple_of(i * TILE, TILE), TILE)
        values = embed[tile, :].T
        embed_t[:, tile] = values
        norm = normalize(values.astype(F32), 0)[0].astype(BF16)
        norm_t[:, tile] = norm
        query_t[:, tile] = nn(weight_t[...], norm).astype(BF16)


def window_order(values, rows, halo):
    first = 2 * halo + halo
    return jnp.concatenate(
        [
            values[first : first + rows],
            values[first - halo : first],
            values[first + rows : first + rows + halo],
        ],
        axis=0,
    )


def each(count):
    def run(body):
        for i in range(count):
            body(i)

    return run


def step_kernel(
    counts,
    packet,
    twin,
    beside,
    below,
    above,
    noise_own,
    embed_hbm,
    norm_hbm,
    query_hbm,
    logits_hbm,
    weather_hbm,
    target_hbm,
    area_hbm,
    scale_hbm,
    shift_hbm,
    qkv_hbm,
    attn_out_hbm,
    dec_kv_hbm,
    dec_out_hbm,
    head_hbm,
    pred_own_hbm,
    pred_other_hbm,
    keep_hbm,
    send_hbm,
    noise_out,
    embed_t,
    norm_t,
    query_t,
    grid_logits,
    weather,
    target,
    area,
    cond_scale,
    cond_shift,
    attn_qkv,
    attn_out,
    dec_kv,
    dec_out,
    head_out,
    pred,
    grads,
    latent,
    latent_q,
    units,
    acts,
    acts_q,
    affine,
    affine_t,
    sums,
    col_sums,
    scores,
    unit_t,
    unit_q_t,
    list_slots,
    list_bias,
    mesh_logits,
    mesh_query,
    mesh_kv,
    mesh_probs,
    mesh_grad_scores,
    mesh_mixed,
    mesh_grad_mixed,
    mesh_out,
    mesh_grad_out,
    mesh_norm,
    mesh_norm_t,
    dec_keys,
    grid_probs,
    grid_grad_scores,
    grid_mixed,
    grid_grad_out,
    grid_grad_mixed,
    grid_out,
    grid_final,
    change,
    grad_change,
    head_pad,
    head_t,
    dec_out_t,
    grad_query,
    grad_dec,
    grad_q,
    grad_kv,
    load_sems,
    store_sems,
    *,
    scale_den,
):
    halo, dim = above.shape
    rows = 2 * halo
    window = rows + 2 * halo
    outer = 2 * window
    own = packet[:rows]
    edges = packet[rows:]
    heads = dim // HEAD
    members = 2
    channels = weather.shape[0]
    slots = embed_t.shape[1]
    inv_sqrt = LOG2E / math.sqrt(HEAD)
    member = lax.axis_index("member")
    core = lax.rem(lax.axis_index("space"), 2)
    here = pl.ds(pl.multiple_of(member * slots, slots), slots)

    loads = {}

    def load(name, source, target_ref):
        loads[name] = pltpu.make_async_copy(source, target_ref, load_sems.at[len(loads)])

    def start(*group):
        for name in group:
            loads[name].start()

    load("qkv", qkv_hbm, attn_qkv)
    load("scale", scale_hbm, cond_scale)
    load("shift", shift_hbm, cond_shift)
    load("attn_out", attn_out_hbm, attn_out)
    load("dec_kv", dec_kv_hbm, dec_kv)
    load("query", query_hbm, query_t)
    load("logits", logits_hbm, grid_logits)
    load("embed", embed_hbm, embed_t)
    load("dec_out", dec_out_hbm, dec_out)
    load("head", head_hbm, head_out)
    load("weather", weather_hbm.at[:, here], weather)
    load("target", target_hbm.at[:, here], target)
    load("area", area_hbm.at[:, here], area)
    load("norm", norm_hbm, norm_t)
    start("qkv", "scale", "shift")

    odd = core == 1
    latent[0:halo] = below[:halo]
    latent[halo : halo + rows] = jnp.where(odd, twin[:rows], beside[:rows])
    latent[halo + rows : halo + 2 * rows] = own
    latent[halo + 2 * rows : halo + 3 * rows] = jnp.where(odd, beside[:rows], twin[:rows])
    latent[halo + 3 * rows :] = above[...]
    lane = lax.broadcasted_iota(jnp.int32, (edges.shape[0], rows), 1)
    late = (lane >= halo) == odd
    ends = jnp.where(
        jnp.concatenate([late] * 4, axis=1), twin[rows:].astype(F32), beside[rows:].astype(F32)
    )
    lists = edges.astype(F32)

    def listed(part):
        return [
            lists[:, part * rows : (part + 1) * rows],
            pltpu.roll(ends[:, part * rows : (part + 1) * rows], halo, 1),
        ]

    list_slots[...] = jnp.concatenate(listed(0), axis=1).astype(jnp.int32)
    list_bias[...] = joined_terms(*(jnp.concatenate(listed(part), axis=1) for part in (1, 2, 3)))
    mesh_logits[...] = jnp.full(mesh_logits.shape, FAR, F32)

    @pl.loop(0, list_slots.shape[0])
    def _(entry):
        add_entry(list_slots, list_bias, entry, mesh_logits)

    noise_row = joined_terms(*(below[halo:, part * rows : (part + 1) * rows] for part in (0, 1, 2)))
    spread = cond_scale.shape[0]
    own_row = jnp.concatenate([noise_own[...], jnp.zeros((1, rows - spread), F32)], axis=1)
    noise = []
    for m, row in enumerate((own_row, noise_row[:1])):
        columns = jnp.broadcast_to(row, (rows, rows)).T[:spread]
        noise_out[m] = columns
        noise.append(columns[:, :1])
    is_before = lax.broadcasted_iota(jnp.int32, (window, rows), 1) < halo
    inner = slice(rows, rows + window)

    def compact(full):
        return full[inner, :rows], jnp.where(is_before, full[:window, rows:], full[window:, rows:])

    def spread_out(target_ref, middle, ends):
        target_ref[inner, :rows] = middle.astype(BF16)
        target_ref[:window, rows:] = jnp.where(is_before, ends, 0.0).astype(BF16)
        target_ref[window:, rows:] = jnp.where(is_before, 0.0, ends).astype(BF16)

    def tile_of(index, size=TILE, base=0):
        if isinstance(index, int):
            return slice(base + index * size, base + (index + 1) * size)
        return pl.ds(pl.multiple_of(base + index * size, size), size)

    @each(members * heads)
    def _(i):
        mesh_probs[i, :rows, :rows] = jnp.zeros((rows, rows), BF16)
        mesh_probs[i, rows + window :, :rows] = jnp.zeros((rows, rows), BF16)
        mesh_grad_scores[i, :rows, :rows] = jnp.zeros((rows, rows), BF16)
        mesh_grad_scores[i, rows + window :, :rows] = jnp.zeros((rows, rows), BF16)

    loads["scale"].wait()
    loads["shift"].wait()
    gains = []
    shifts = []
    for m in range(members):
        gains.append(1.0 + jnp.sum(noise[m] * cond_scale[...], axis=0, keepdims=True))
        shifts.append(jnp.sum(noise[m] * cond_shift[...], axis=0, keepdims=True))
        affine[2 * m : 2 * m + 1] = gains[m]
        affine[2 * m + 1 : 2 * m + 2] = shifts[m]

    @each(outer // rows)
    def _(i):
        tile = tile_of(i, rows)
        unit = normalize(latent[tile, :].astype(F32), 1)[0]
        units[tile, :] = unit.astype(BF16)
        unit_t[:dim, tile] = unit.astype(BF16).T
        for m in range(members):
            act = unit * affine[2 * m : 2 * m + 1] + affine[2 * m + 1 : 2 * m + 2]
            acts[tile_of(i, rows, m * outer), :] = act.astype(BF16)

    latent_q[...] = window_order(latent, rows, halo)
    unit_q_t[:dim] = window_order(units, rows, halo).T
    unit_q_t[dim:] = jnp.ones((16, window), BF16)
    unit_t[dim:] = jnp.ones((16, outer), BF16)
    for m in range(members):
        acts_q[m * window : (m + 1) * window] = window_order(
            acts.at[m * outer : (m + 1) * outer], rows, halo
        )

    start("attn_out", "dec_kv")
    loads["qkv"].wait()
    start("query", "logits", "embed", "dec_out", "head", "weather", "target", "area", "norm")

    @each(dim // TILE)
    def _(i):
        part = nn(acts_q[...], attn_qkv[:, tile_of(i)]).astype(BF16)
        mesh_query[tile_of(i), :] = part.T

    @each(2 * dim // TILE)
    def _(i):
        mesh_kv[:, tile_of(i)] = nn(acts[...], attn_qkv[:, tile_of(i, TILE, dim)]).astype(BF16)

    pairs = [(m * heads + h, m, h) for m in range(members) for h in range(heads)]

    def span(index, size, base=0):
        return slice(base + index * size, base + (index + 1) * size)

    for i, m, h in pairs:
        keys = mesh_kv[span(m, outer), span(h, HEAD)]
        middle, ends = compact(nn(keys, mesh_query[span(h, HEAD), span(m, window)]))
        scores[i, :, :rows] = middle
        scores[i, :, rows:window] = ends

    @each(members * heads)
    def _(i):
        parts = [
            softmax_rows(scores[i, :, lanes] * inv_sqrt + mesh_logits[:, lanes])
            for lanes in (span(0, rows), span(1, rows))
        ]
        spread_out(mesh_probs.at[i], *parts)

    for i, m, h in pairs:
        values = mesh_kv[span(m, outer), span(h, HEAD, dim)]
        mesh_mixed[span(h, HEAD), span(m, window)] = tn(values, mesh_probs[i]).astype(BF16)

    loads["attn_out"].wait()

    @each(members)
    def _(m):
        here_q = tile_of(m, window)
        mixed = mesh_mixed[:, here_q].T
        out = (latent_q[...].astype(F32) + nn(mixed, attn_out[...])).astype(BF16)
        mesh_out[here_q, :] = out
        norm = normalize(out.astype(F32), 1)[0].astype(BF16)
        mesh_norm[here_q, :] = norm
        mesh_norm_t[:, here_q] = norm.T

    loads["dec_kv"].wait()

    @each(2 * dim // TILE)
    def _(i):
        dec_keys[:, tile_of(i)] = nn(mesh_norm[...], dec_kv[:, tile_of(i)]).astype(BF16)

    for name in ("query", "logits", "embed", "dec_out", "head"):
        loads[name].wait()
    head_pad[...] = jnp.zeros_like(head_pad)
    head_pad[:channels] = head_out[...]
    head_t[...] = head_pad[...].T
    dec_out_t[...] = dec_out[...].T

    for i, m, h in pairs:
        scores[i] = nn(dec_keys[span(m, window), span(h, HEAD)], query_t[span(h, HEAD), :])

    @each(members * heads)
    def _(i):
        for t in range(slots // HEAD):
            lanes = span(t, HEAD)
            probs = softmax_rows(scores[i, :, lanes] * inv_sqrt + grid_logits[:, lanes])
            grid_probs[i, :, lanes] = probs.astype(BF16)

    for i, m, h in pairs:
        values = dec_keys[span(m, window), span(h, HEAD, dim)]
        grid_mixed[span(h, HEAD), span(m, slots)] = tn(values, grid_probs[i]).astype(BF16)

    for m in range(members):
        out = embed_t[...].astype(F32) + nn(dec_out_t[...], grid_mixed[:, span(m, slots)])
        grid_out[:, span(m, slots)] = out.astype(BF16)

    lane_tiles = members * slots // HEAD

    @each(lane_tiles)
    def _(i):
        tile = tile_of(i, HEAD)
        final = normalize(grid_out[:, tile].astype(F32), 0)[0].astype(BF16)
        grid_final[:, tile] = final

    change[...] = nn(head_pad[...], grid_final[...])

    for name in ("weather", "target", "area", "norm"):
        loads[name].wait()
    def smooth(values):
        square = values * values + SMOOTHING
        inverse = lax.rsqrt(square)
        return square * inverse, values * inverse

    grad_change[...] = jnp.zeros_like(grad_change)

    def compare(i, loss):
        tile = tile_of(i, HEAD)
        slot = lax.broadcasted_iota(jnp.int32, (1, HEAD), 1) + (member * slots + i * HEAD)
        live = jnp.where(slot < counts[0], 1.0, 0.0)
        weighting = live * area[:, tile]
        second_tile = tile_of(i, HEAD, slots)
        first = weather[:, tile] + live * change[:channels, tile]
        second = weather[:, tile] + live * change[:channels, second_tile]
        pred[0, :, tile] = first
        pred[1, :, tile] = second
        size_first, slope_first = smooth(first - target[:, tile])
        size_second, slope_second = smooth(second - target[:, tile])
        size_pair, slope_pair = smooth(first - second)
        factor = weighting * (LOSS_SCALE / scale_den)
        grad_change[:channels, tile] = (factor * (slope_first - slope_pair)).astype(BF16)
        grad_change[:channels, second_tile] = (factor * (slope_second + slope_pair)).astype(BF16)
        terms = weighting * (size_first + size_second - size_pair)
        return loss + jnp.sum(terms, axis=0, keepdims=True)

    loss = lax.fori_loop(0, slots // HEAD, compare, jnp.zeros((1, HEAD), F32))
    loss = jnp.sum(loss) / scale_den
    stores = [
        pltpu.make_async_copy(pred.at[0], pred_own_hbm, store_sems.at[0]),
        pltpu.make_async_copy(pred.at[1], pred_other_hbm, store_sems.at[1]),
    ]
    for store in stores:
        store.start()

    tall = HEAD * HEAD // dim
    per_block = dim // tall

    def pack(index, tile, block):
        half, chunk = index // 4, index % 4 * per_block
        for c in range(per_block):
            for t in range(TILE // HEAD):
                where = tile_of(tile * (TILE // HEAD) + t, tall)
                part = block[c * tall : (c + 1) * tall, t * HEAD : (t + 1) * HEAD]
                grads[half, chunk + c, where, :] = part.astype(BF16)

    col_tiles = dim // TILE

    def pack_extras(half, chunk, values):
        for i in range(values.shape[0] // 8):
            for t in range(heads):
                grads[half, chunk + i * heads + t, HEAD:, :] = values[
                    i * 8 : (i + 1) * 8, t * HEAD : (t + 1) * HEAD
                ].astype(BF16)

    def ship(half, first, last, sem):
        source = grads.at[half, first:last]
        keep = pltpu.make_async_copy(source, keep_hbm.at[first:last], store_sems.at[sem])
        send = pltpu.make_async_copy(source, send_hbm.at[first:last], store_sems.at[sem])
        pl.when(core == half)(keep.start)
        pl.when(core != half)(send.start)
        stores.append(keep)

    grads[:, :, HEAD:, :] = jnp.zeros((2, 4 * per_block, 8, HEAD), BF16)

    pack_extras(1, 0, nt(grad_change[...], grid_final[...]))

    @each(lane_tiles)
    def _(i):
        tile = tile_of(i, HEAD)
        g_final = nn(head_t[...], grad_change[:, tile])
        g_out = normalize_back(grid_out[:, tile].astype(F32), g_final, 0).astype(BF16)
        grid_grad_out[:, tile] = g_out

    for m in range(members):
        g_mixed = nn(dec_out[...], grid_grad_out[:, span(m, slots)])
        grid_grad_mixed[:, span(m, slots)] = g_mixed.astype(BF16)

    @each(col_tiles)
    def _(i):
        pack(7, i, nt(grid_mixed[...], grid_grad_out[tile_of(i), :]))

    for i, m, h in pairs:
        values = dec_keys[span(m, window), span(h, HEAD, dim)]
        scores[i] = nn(values, grid_grad_mixed[span(h, HEAD), span(m, slots)])

    @each(members * heads)
    def _(i):
        here = tile_of(i % heads * members + i // heads, window)
        for t in range(slots // HEAD):
            lanes = span(t, HEAD)
            grid_grad_scores[here, lanes] = score_back(
                grid_probs[i, :, lanes], scores[i, :, lanes]
            ).astype(BF16)

    for i, m, h in pairs:
        g_scores = grid_grad_scores[span(h * members + m, window), :]
        g_head = grid_grad_mixed[span(h, HEAD), span(m, slots)]
        probs = grid_probs[i]
        grad_dec[span(m, window), span(h, HEAD)] = nt(g_scores, query_t[span(h, HEAD), :]).astype(BF16)
        grad_dec[span(m, window), span(h, HEAD, dim)] = nt(probs, g_head).astype(BF16)
    for h in range(heads):
        keys = dec_keys[:, span(h, HEAD)]
        g_scores = grid_grad_scores[span(h, members * window), :]
        grad_query[span(h, HEAD), :] = tn(keys, g_scores).astype(BF16)

    @each(col_tiles)
    def _(i):
        pack(4, i, nt(norm_t[...], grad_query[tile_of(i), :]))

    @each(2 * col_tiles)
    def _(i):
        block = nn(mesh_norm_t[...], grad_dec[:, tile_of(i)])
        pack(5 + i // col_tiles, i % col_tiles, block)

    ship(1, 0, 4 * per_block, 2)

    @each(members)
    def _(m):
        here_q = tile_of(m, window)
        g_norm = nt(grad_dec[here_q, :], dec_kv[...])
        g_out = normalize_back(mesh_out[here_q, :].astype(F32), g_norm, 1).astype(BF16)
        mesh_grad_out[here_q, :] = g_out
        mesh_grad_mixed[:, here_q] = nt(attn_out[...], g_out).astype(BF16)

    @each(col_tiles)
    def _(i):
        pack(3, i, nn(mesh_mixed[...], mesh_grad_out[:, tile_of(i)]))

    for i, m, h in pairs:
        values = mesh_kv[span(m, outer), span(h, HEAD, dim)]
        middle, ends = compact(nn(values, mesh_grad_mixed[span(h, HEAD), span(m, window)]))
        scores[i, :, :rows] = middle
        scores[i, :, rows:window] = ends

    @each(members * heads)
    def _(i):
        parts = [
            score_back(probs, scores[i, :, lanes])
            for probs, lanes in zip(compact(mesh_probs[i]), (span(0, rows), span(1, rows)))
        ]
        spread_out(mesh_grad_scores.at[i], *parts)

    for i, m, h in pairs:
        cols = span(h, HEAD)
        g_scores = mesh_grad_scores[i]
        g_head = mesh_grad_mixed[cols, span(m, window)]
        g_query = tn(mesh_kv[span(m, outer), cols], g_scores).astype(BF16)
        grad_q[span(m, window), cols] = g_query.T
        grad_kv[span(m, outer), cols] = nt(g_scores, mesh_query[cols, span(m, window)]).astype(BF16)
        grad_kv[span(m, outer), span(h, HEAD, dim)] = nt(mesh_probs[i], g_head).astype(BF16)

    for m in range(members):
        gain_col = jnp.broadcast_to(gains[m], (HEAD, dim)).T
        shift_col = jnp.broadcast_to(shifts[m], (HEAD, dim)).T
        affine_t[2 * m] = gain_col
        affine_t[2 * m + 1] = shift_col
    sums[...] = jnp.zeros_like(sums)
    col_sums[...] = jnp.zeros_like(col_sums)

    def project_back(index, tile, weight_tile, left, parts):
        weight = attn_qkv[:, weight_tile].astype(F32)
        total = None
        for m in range(members):
            moment = nn(left[...], parts[m])
            col_sum = moment[dim : dim + 1]
            moment = moment[:dim]
            high, middle, low = split_terms(col_sum)
            for row, value in enumerate((high, middle, low)):
                col_sums[8 * m + row : 8 * m + row + 1, weight_tile] = value.astype(F32)
            by_gain = weight * moment
            sums[m] += by_gain[:, :HEAD] + by_gain[:, HEAD:]
            terms = []
            for t in range(TILE // HEAD):
                lanes = slice(t * HEAD, (t + 1) * HEAD)
                terms.append(
                    affine_t[2 * m] * moment[:, lanes] + affine_t[2 * m + 1] * col_sum[:, lanes]
                )
            term = jnp.concatenate(terms, axis=1)
            total = term if m == 0 else total + term
        pack(index, tile, total)

    @each(2 * col_tiles)
    def _(i):
        parts = [grad_kv[m * outer : (m + 1) * outer, tile_of(i)] for m in range(members)]
        project_back(
            1 + i // col_tiles, i % col_tiles, tile_of(i, TILE, dim), unit_t, parts
        )

    ship(0, per_block, 4 * per_block, 3)

    @each(col_tiles)
    def _(i):
        parts = [grad_q[m * window : (m + 1) * window, tile_of(i)] for m in range(members)]
        project_back(0, i, tile_of(i), unit_q_t, parts)

    row_id = lax.broadcasted_iota(jnp.int32, (8, dim), 0)
    grad_cond = jnp.where(row_id == 4, loss, 0.0)
    g_shifts = nt(attn_qkv[...], col_sums[...].astype(BF16))
    for m in range(members):
        mine = member if m == 0 else 1 - member
        g_shift = g_shifts[:, 8 * m : 8 * m + 3]
        for row, lanes in ((mine, sums[m]), (mine + 2, g_shift)):
            column = jnp.sum(lanes, axis=1, keepdims=True)
            values = jnp.broadcast_to(column, (dim, HEAD)).T[:8]
            grad_cond += jnp.where(row_id == row, values, 0.0)
    pack_extras(0, 0, grad_cond)
    ship(0, 0, per_block, 4)
    for store in stores:
        store.wait()


def sum_kernel(parts, pred_own_hbm, pred_arrived_hbm, result, pred_hbm, sems):
    slots = pred_own_hbm.shape[1]
    member = lax.axis_index("member")
    here = pl.ds(pl.multiple_of(member * slots, slots), slots)
    there = pl.ds(pl.multiple_of((1 - member) * slots, slots), slots)
    copies = [
        pltpu.make_async_copy(pred_own_hbm, pred_hbm.at[0, :, here], sems.at[0]),
        pltpu.make_async_copy(pred_arrived_hbm, pred_hbm.at[0, :, there], sems.at[1]),
    ]
    for copy in copies:
        copy.start()
    total = jnp.sum(parts[...].astype(F32), axis=0, keepdims=True)
    result[...] = jnp.broadcast_to(total.astype(BF16), result.shape)
    for copy in copies:
        copy.wait()


def unpack_kernel(*refs, own_half):
    data, noise = refs[:2]
    outputs, scratch = (refs[2:11], refs[11:]) if own_half else (refs[11:20], refs[20:])
    grad_scale, grad_shift, grad_qkv, grad_attn_out = outputs[:4]
    grad_dec_query, grad_dec_kv, grad_dec_out, grad_head, loss = outputs[4:]
    blocks, cond, head, tail, sems = scratch
    member = lax.axis_index("member")
    core = lax.rem(lax.axis_index("space"), 2)
    half = core if own_half else 1 - core
    channels, dim = grad_head.shape
    heads = dim // HEAD
    tall = HEAD * HEAD // dim
    per_block = dim // tall
    targets = (
        (
            grad_qkv.at[:, :dim],
            grad_qkv.at[:, dim : 2 * dim],
            grad_qkv.at[:, 2 * dim :],
            grad_attn_out,
        ),
        (grad_dec_query, grad_dec_kv.at[:, :dim], grad_dec_kv.at[:, dim:], grad_dec_out),
    )

    def block_copy(which, i):
        return pltpu.make_async_copy(blocks.at[i], targets[which][i], sems.at[i])

    for i in range(4):

        @pl.loop(0, per_block, unroll=2)
        def _(c):
            tile = pl.ds(pl.multiple_of(c * tall, tall), tall)
            for t in range(heads):
                blocks[i, tile, t * HEAD : (t + 1) * HEAD] = data[
                    i * per_block + c, t * tall : (t + 1) * tall, :
                ].astype(F32)

        for which in range(2):
            pl.when(half == which)(block_copy(which, i).start)

    def extra(i):
        return jnp.concatenate(
            [data[i * heads + t, HEAD:, :].astype(F32) for t in range(heads)], axis=1
        )

    @pl.when(half == 0)
    def _():
        sums = extra(0)
        for k in range(2):
            first = sums[2 * k : 2 * k + 1]
            second = sums[2 * k + 1 : 2 * k + 2]
            mine = jnp.where(member == 0, first, second)
            other = jnp.where(member == 0, second, first)
            cond[k] = noise[0, :, :1] * mine + noise[1, :, :1] * other
        tail[...] = sums[4:5, :HEAD]
        copies = [
            pltpu.make_async_copy(cond.at[0], grad_scale, sems.at[4]),
            pltpu.make_async_copy(cond.at[1], grad_shift, sems.at[5]),
            pltpu.make_async_copy(tail, loss, sems.at[6]),
        ]
        for copy in copies:
            copy.start()
        for copy in copies:
            copy.wait()

    @pl.when(half == 1)
    def _():
        for i in range(-(-channels // 8)):
            count = min(8, channels - i * 8)
            head[i * 8 : i * 8 + count] = extra(i)[:count]
        copy = pltpu.make_async_copy(head, grad_head, sems.at[4])
        copy.start()
        copy.wait()

    for i in range(4):
        for which in range(2):
            pl.when(half == which)(block_copy(which, i).wait)


def whole(shape):
    return pl.BlockSpec(shape, lambda *_: (0,) * len(shape))


def per_device(
    mesh_latent,
    grid_embed,
    weather_state,
    target,
    cell_area,
    member_noise,
    mesh_nbrs,
    mesh_bias,
    grid_nbrs,
    grid_bias,
    grid_counts,
    cond_scale,
    cond_shift,
    attn_qkv,
    attn_out,
    dec_query,
    dec_kv,
    dec_out,
    head_out,
):
    rows, dim = mesh_latent.shape
    halo = rows // 2
    window = rows + 2 * halo
    outer = 2 * window
    size = lax.axis_size("space")
    grid_slots = grid_embed.shape[0]
    slots = grid_slots // 2
    channels = weather_state.shape[0]
    total = rows * size
    heads = dim // HEAD
    noise_size = member_noise.shape[1]
    entries = grid_nbrs.shape[0]
    scale_den = 2.0 * channels * grid_slots * size

    axes = ("member", "space")

    def permute(value, target_of):
        pairs = []
        for m in range(2):
            for k in range(size):
                to_m, to_k = target_of(m, k)
                pairs.append((m * size + k, to_m * size + to_k % size))
        return lax.ppermute(value, axes, pairs)

    smem = pl.BlockSpec(memory_space=pltpu.SMEM)
    vmem = pl.BlockSpec(memory_space=pltpu.VMEM)
    hbm = pl.BlockSpec(memory_space=pltpu.HBM)
    packet, upward, downward = pl.pallas_call(
        lambda *refs: pack_kernel(*refs, total=total),
        in_specs=[vmem] * 4,
        out_shape=[
            jax.ShapeDtypeStruct((rows + mesh_nbrs.shape[0], dim), BF16),
            jax.ShapeDtypeStruct((halo + 16, dim), BF16),
            jax.ShapeDtypeStruct((halo, dim), BF16),
        ],
        compiler_params=pltpu.CompilerParams(vmem_limit_bytes=ALL_VMEM),
        name="pack",
    )(mesh_latent, mesh_nbrs, mesh_bias, member_noise)
    twin = permute(packet, lambda m, k: (m, k ^ 1))
    beside = permute(packet, lambda m, k: (m, k + 1 if k % 2 else k - 1))
    below = permute(upward, lambda m, k: (1 - m, k + 2))
    above = permute(downward, lambda m, k: (m, k - 2))

    square = (dim, slots)
    embed_t, norm_t, query_t, grid_logits = pl.pallas_call(
        lambda *refs: prepare_kernel(*refs, rows=rows, halo=halo, total=total),
        in_specs=[hbm] * 4,
        out_specs=[vmem] * 4,
        out_shape=[
            jax.ShapeDtypeStruct(square, BF16),
            jax.ShapeDtypeStruct(square, BF16),
            jax.ShapeDtypeStruct(square, BF16),
            jax.ShapeDtypeStruct((window, slots), F32),
        ],
        scratch_shapes=[
            pltpu.VMEM((slots, dim), BF16),
            pltpu.VMEM((entries, slots), jnp.int32),
            pltpu.VMEM((entries, slots), F32),
            pltpu.VMEM((dim, dim), BF16),
            pltpu.VMEM((dim, dim), BF16),
            pltpu.SemaphoreType.DMA((4,)),
        ],
        compiler_params=pltpu.CompilerParams(vmem_limit_bytes=ALL_VMEM),
        cost_estimate=pl.CostEstimate(
            flops=2 * dim * dim * slots, bytes_accessed=3 * 2**20, transcendentals=0
        ),
        name="prepare",
    )(grid_embed, grid_nbrs, grid_bias, dec_query)

    channel_pad = -(-channels // 32) * 32
    chunks = size
    half_shape = (chunks, HEAD + 8, HEAD)
    step_in = (
        packet,
        twin,
        beside,
        below,
        above,
        member_noise,
        embed_t,
        norm_t,
        query_t,
        grid_logits,
        weather_state,
        target,
        cell_area[None, :],
        cond_scale,
        cond_shift,
        attn_qkv,
        attn_out,
        dec_kv,
        dec_out,
        head_out,
    )
    pred_own, pred_other, keep, send, noise = pl.pallas_call(
        lambda *refs: step_kernel(*refs, scale_den=scale_den),
        in_specs=[smem] + [vmem] * 6 + [pl.BlockSpec(memory_space=pl.ANY)] * 4 + [hbm] * 10,
        out_specs=[hbm] * 4 + [vmem],
        scratch_shapes=[
            pltpu.VMEM(square, BF16),
            pltpu.VMEM(square, BF16),
            pltpu.VMEM(square, BF16),
            pltpu.VMEM((window, slots), F32),
            pltpu.VMEM((channels, slots), F32),
            pltpu.VMEM((channels, slots), F32),
            pltpu.VMEM((1, slots), F32),
            pltpu.VMEM(cond_scale.shape, F32),
            pltpu.VMEM(cond_shift.shape, F32),
            pltpu.VMEM(attn_qkv.shape, BF16),
            pltpu.VMEM(attn_out.shape, BF16),
            pltpu.VMEM(dec_kv.shape, BF16),
            pltpu.VMEM(dec_out.shape, BF16),
            pltpu.VMEM(head_out.shape, BF16),
            pltpu.VMEM((2, channels, slots), F32),
            pltpu.VMEM((2, *half_shape), BF16),
            pltpu.VMEM((outer, dim), BF16),
            pltpu.VMEM((window, dim), BF16),
            pltpu.VMEM((outer, dim), BF16),
            pltpu.VMEM((2 * outer, dim), BF16),
            pltpu.VMEM((2 * window, dim), BF16),
            pltpu.VMEM((8, dim), F32),
            pltpu.VMEM((4, dim, HEAD), F32),
            pltpu.VMEM((2, dim, HEAD), F32),
            pltpu.VMEM((16, 3 * dim), F32),
            pltpu.VMEM((2 * heads, window, slots), F32),
            pltpu.VMEM((dim + 16, outer), BF16),
            pltpu.VMEM((dim + 16, window), BF16),
            pltpu.VMEM((mesh_nbrs.shape[0], window), jnp.int32),
            pltpu.VMEM((mesh_nbrs.shape[0], window), F32),
            pltpu.VMEM((window, window), F32),
            pltpu.VMEM((dim, 2 * window), BF16),
            pltpu.VMEM((2 * outer, 2 * dim), BF16),
            pltpu.VMEM((2 * heads, outer, window), BF16),
            pltpu.VMEM((2 * heads, outer, window), BF16),
            pltpu.VMEM((dim, 2 * window), BF16),
            pltpu.VMEM((dim, 2 * window), BF16),
            pltpu.VMEM((2 * window, dim), BF16),
            pltpu.VMEM((2 * window, dim), BF16),
            pltpu.VMEM((2 * window, dim), BF16),
            pltpu.VMEM((dim, 2 * window), BF16),
            pltpu.VMEM((2 * window, 2 * dim), BF16),
            pltpu.VMEM((2 * heads, window, slots), BF16),
            pltpu.VMEM((2 * heads * window, slots), BF16),
            pltpu.VMEM((dim, 2 * slots), BF16),
            pltpu.VMEM((dim, 2 * slots), BF16),
            pltpu.VMEM((dim, 2 * slots), BF16),
            pltpu.VMEM((dim, 2 * slots), BF16),
            pltpu.VMEM((dim, 2 * slots), BF16),
            pltpu.VMEM((channel_pad, 2 * slots), F32),
            pltpu.VMEM((channel_pad, 2 * slots), BF16),
            pltpu.VMEM((channel_pad, dim), BF16),
            pltpu.VMEM((dim, channel_pad), BF16),
            pltpu.VMEM((dim, dim), BF16),
            pltpu.VMEM((dim, slots), BF16),
            pltpu.VMEM((2 * window, 2 * dim), BF16),
            pltpu.VMEM((2 * window, dim), BF16),
            pltpu.VMEM((2 * outer, 2 * dim), BF16),
            pltpu.SemaphoreType.DMA((14,)),
            pltpu.SemaphoreType.DMA((5,)),
        ],
        out_shape=[
            jax.ShapeDtypeStruct((channels, slots), F32),
            jax.ShapeDtypeStruct((channels, slots), F32),
            jax.ShapeDtypeStruct(half_shape, BF16),
            jax.ShapeDtypeStruct(half_shape, BF16),
            jax.ShapeDtypeStruct((2, noise_size, rows), F32),
        ],
        compiler_params=pltpu.CompilerParams(vmem_limit_bytes=ALL_VMEM),
        cost_estimate=pl.CostEstimate(
            flops=10**10, bytes_accessed=12 * 2**20, transcendentals=2**21
        ),
        name="step",
    )(grid_counts, *step_in)

    def twin_swap(value):
        return permute(value, lambda m, k: (m, k ^ 1))

    groups = [
        [m * size + k for m in range(2) for k in range(size) if k % 2 == c] for c in range(2)
    ]

    def over_chips(value):
        return lax.all_to_all(value, axes, 0, 0, axis_index_groups=groups)

    arrived_pred = permute(pred_other, lambda m, k: (1 - m, k))
    pair = (keep.astype(F32) + twin_swap(send).astype(F32)).astype(BF16)
    pair, arrived_pred = lax.optimization_barrier((pair, arrived_pred))
    parts = over_chips(pair)
    shared, prediction = pl.pallas_call(
        sum_kernel,
        in_specs=[vmem, hbm, hbm],
        out_specs=[vmem, hbm],
        out_shape=[
            jax.ShapeDtypeStruct(half_shape, BF16),
            jax.ShapeDtypeStruct((1, channels, grid_slots), F32),
        ],
        scratch_shapes=[pltpu.SemaphoreType.DMA((2,))],
        compiler_params=pltpu.CompilerParams(vmem_limit_bytes=32 * 2**20),
        name="sum",
    )(parts, pred_own, arrived_pred)
    mine = over_chips(shared)
    theirs = twin_swap(mine)
    grad_shapes = [
        jax.ShapeDtypeStruct(shape, F32)
        for shape in (
            cond_scale.shape,
            cond_shift.shape,
            attn_qkv.shape,
            attn_out.shape,
            dec_query.shape,
            dec_kv.shape,
            dec_out.shape,
            head_out.shape,
            (1, HEAD),
        )
    ]
    anywhere = pl.BlockSpec(memory_space=pl.ANY)

    def unpack(own_half, data, outputs):
        return pl.pallas_call(
            lambda *refs: unpack_kernel(*refs, own_half=own_half),
            in_specs=[vmem, vmem] + [anywhere] * len(outputs),
            out_specs=[anywhere] * 9,
            out_shape=grad_shapes,
            scratch_shapes=[
                pltpu.VMEM((4, dim, dim), F32),
                pltpu.VMEM((2, *cond_scale.shape), F32),
                pltpu.VMEM(head_out.shape, F32),
                pltpu.VMEM((1, HEAD), F32),
                pltpu.SemaphoreType.DMA((7,)),
            ],
            input_output_aliases={2 + i: i for i in range(len(outputs))},
            compiler_params=pltpu.CompilerParams(vmem_limit_bytes=32 * 2**20),
            cost_estimate=pl.CostEstimate(
                flops=0, bytes_accessed=7 * 2**20, transcendentals=0
            ),
            name="unpack_mine" if own_half else "unpack_theirs",
        )(data, noise, *outputs)

    outputs = unpack(True, mine, ())
    outputs = unpack(False, theirs, tuple(outputs))
    return (prediction, *outputs[:8], outputs[8][0, 0])


def solution(mesh):
    in_specs = (
        P("space", None),
        P("space", None),
        P(None, "space"),
        P(None, "space"),
        P("space"),
        P("member", None),
        P(None, "space"),
        P(None, "space"),
        P(None, "space"),
        P(None, "space"),
        P("space"),
        P(),
        P(),
        P(),
        P(),
        P(),
        P(),
        P(),
        P(),
    )
    out_specs = (P("member", None, "space"), P(), P(), P(), P(), P(), P(), P(), P(), P())
    return jax.shard_map(
        per_device, mesh=mesh, in_specs=in_specs, out_specs=out_specs, check_vma=False
    )
```

```python
import math

import jax
import jax.numpy as jnp
from jax import lax
from jax.experimental import pallas as pl
from jax.experimental.pallas import tpu as pltpu
from jax.sharding import PartitionSpec as P

HEAD = 128
EPSILON = 1e-05
LOSS_SCALE = 65536.0
SMOOTHING = 0.0625
FAR = -1e30
TILE = 256
LOG2E = math.log2(math.e)
ALL_VMEM = 62 * 2**20

F32 = jnp.float32
BF16 = jnp.bfloat16


def nn(first, second):
    return lax.dot_general(first, second, (((1,), (0,)), ((), ())), preferred_element_type=F32)


def nt(first, second):
    return lax.dot_general(first, second, (((1,), (1,)), ((), ())), preferred_element_type=F32)


def tn(first, second):
    return lax.dot_general(first, second, (((0,), (0,)), ((), ())), preferred_element_type=F32)


def normalize(values, axis):
    center = values - jnp.mean(values, axis=axis, keepdims=True)
    spread = jnp.mean(center * center, axis=axis, keepdims=True)
    scale = lax.rsqrt(spread + EPSILON)
    return center * scale, scale


def normalize_back(values, grad_out, axis):
    unit, scale = normalize(values, axis)
    mean_grad = jnp.mean(grad_out, axis=axis, keepdims=True)
    mean_unit = jnp.mean(grad_out * unit, axis=axis, keepdims=True)
    return scale * (grad_out - mean_grad - unit * mean_unit)


def spread_bias(slots, bias, rows):
    entries, width = slots.shape
    row_ids = lax.broadcasted_iota(jnp.int32, (rows, width), 0)
    logits = jnp.full((rows, width), FAR, F32)
    for entry in range(entries):
        same = slots == slots[entry : entry + 1]
        top = jnp.max(jnp.where(same, bias, FAR), axis=0, keepdims=True)
        terms = jnp.sum(jnp.where(same, jnp.exp(bias - top), 0.0), axis=0, keepdims=True)
        logits = jnp.where(row_ids == slots[entry : entry + 1], (top + jnp.log(terms)) * LOG2E, logits)
    return logits


def softmax_rows(scores):
    terms = jnp.exp2(scores - jnp.max(scores, axis=0, keepdims=True))
    return terms * (1.0 / jnp.sum(terms, axis=0, keepdims=True))


def score_back(probs, grad_probs):
    probs = probs.astype(F32)
    inner = jnp.sum(probs * grad_probs, axis=0, keepdims=True)
    return probs * (grad_probs - inner) * (1.0 / math.sqrt(HEAD))


def split_terms(values):
    high = values.astype(BF16)
    rest = values - high.astype(F32)
    middle = rest.astype(BF16)
    low = (rest - middle.astype(F32)).astype(BF16)
    return high, middle, low


def joined_terms(high, middle, low):
    return high.astype(F32) + (middle.astype(F32) + low.astype(F32))


def window_start(rows):
    return lax.axis_index("space") * rows - rows // 2


def pack_kernel(latent, nbrs, bias, packet, *, total):
    rows = latent.shape[0]
    packet[:rows] = latent[...]
    slots = ((nbrs[...] - window_start(rows)) & (total - 1)).astype(F32).astype(BF16)
    packet[rows:] = jnp.concatenate([slots, *split_terms(bias[...])], axis=1)


def is_odd():
    return lax.rem(lax.axis_index("space"), 2) == 1


def outward_kernel(packet, twin, noise, outward, *, rows):
    halo = rows // 2
    size = packet.shape[0]
    outward[:size] = packet[...]
    outward[size : size + halo] = jnp.where(is_odd(), twin[halo:rows], twin[:halo])
    spare = jnp.zeros((1, rows - noise.shape[1]), F32)
    padded = jnp.concatenate([noise[...], spare], axis=1)
    padded = jnp.broadcast_to(padded, (outward.shape[0] - size - halo, rows))
    terms = split_terms(padded)
    outward[size + halo :] = jnp.concatenate([*terms, jnp.zeros_like(terms[0])], axis=1)


def prepare_kernel(
    embed_hbm,
    nbrs_hbm,
    bias_hbm,
    weight_hbm,
    _,
    embed_t,
    norm_t,
    query_t,
    logits,
    embed,
    nbrs,
    bias,
    dec_query,
    weight_t,
    sems,
    *,
    rows,
    halo,
    total,
):
    slots = embed.shape[0]
    here = pl.ds(pl.multiple_of(lax.axis_index("member") * slots, slots), slots)
    copies = [
        pltpu.make_async_copy(embed_hbm.at[here, :], embed, sems.at[0]),
        pltpu.make_async_copy(nbrs_hbm.at[:, here], nbrs, sems.at[1]),
        pltpu.make_async_copy(bias_hbm.at[:, here], bias, sems.at[2]),
        pltpu.make_async_copy(weight_hbm, dec_query, sems.at[3]),
    ]
    for copy in copies:
        copy.start()
    copies[1].wait()
    copies[2].wait()
    local = (nbrs[...] - window_start(rows)) & (total - 1)
    places = jnp.where(
        local < halo, local + rows, jnp.where(local < halo + rows, local - halo, local)
    )
    for part in range(slots // HEAD):
        lanes = slice(part * HEAD, (part + 1) * HEAD)
        logits[:, lanes] = spread_bias(places[:, lanes], bias[:, lanes], rows + 2 * halo)
    copies[0].wait()
    copies[3].wait()
    weight_t[...] = dec_query[...].T

    @pl.loop(0, slots // TILE)
    def _(i):
        tile = pl.ds(pl.multiple_of(i * TILE, TILE), TILE)
        values = embed[tile, :].T
        embed_t[:, tile] = values
        norm = normalize(values.astype(F32), 0)[0].astype(BF16)
        norm_t[:, tile] = norm
        query_t[:, tile] = nn(weight_t[...], norm).astype(BF16)


def window_order(values, rows, halo):
    first = 2 * halo + halo
    return jnp.concatenate(
        [
            values[first : first + rows],
            values[first - halo : first],
            values[first + rows : first + rows + halo],
        ],
        axis=0,
    )


def each(count):
    def run(body):
        for i in range(count):
            body(i)

    return run


def step_kernel(
    counts,
    packet,
    twin,
    beside,
    relay,
    noise_own,
    embed_hbm,
    norm_hbm,
    query_hbm,
    logits_hbm,
    weather_hbm,
    target_hbm,
    area_hbm,
    scale_hbm,
    shift_hbm,
    qkv_hbm,
    attn_out_hbm,
    dec_kv_hbm,
    dec_out_hbm,
    head_hbm,
    pred_own_hbm,
    pred_other_hbm,
    keep_hbm,
    send_hbm,
    noise_out,
    embed_t,
    norm_t,
    query_t,
    grid_logits,
    weather,
    target,
    area,
    cond_scale,
    cond_shift,
    attn_qkv,
    attn_out,
    dec_kv,
    dec_out,
    head_out,
    pred,
    grads,
    latent,
    latent_q,
    units,
    acts,
    acts_q,
    affine,
    affine_t,
    sums,
    col_sums,
    scores,
    unit_t,
    unit_q_t,
    list_slots,
    list_bias,
    mesh_logits,
    mesh_query,
    mesh_kv,
    mesh_probs,
    mesh_grad_scores,
    mesh_mixed,
    mesh_grad_mixed,
    mesh_out,
    mesh_grad_out,
    mesh_norm,
    mesh_norm_t,
    dec_keys,
    grid_probs,
    grid_grad_scores,
    grid_mixed,
    grid_grad_out,
    grid_grad_mixed,
    grid_out,
    grid_final,
    change,
    grad_change,
    head_pad,
    head_t,
    dec_out_t,
    grad_query,
    grad_dec,
    grad_q,
    grad_kv,
    load_sems,
    store_sems,
    *,
    rows,
    scale_den,
):
    size, dim = packet.shape
    halo = rows // 2
    window = rows + 2 * halo
    outer = 2 * window
    own = packet[:rows]
    edges = packet[rows:]
    heads = dim // HEAD
    members = 2
    channels = weather.shape[0]
    slots = embed_t.shape[1]
    inv_sqrt = LOG2E / math.sqrt(HEAD)
    member = lax.axis_index("member")
    core = lax.rem(lax.axis_index("space"), 2)
    here = pl.ds(pl.multiple_of(member * slots, slots), slots)

    loads = {}

    def load(name, source, target_ref):
        loads[name] = pltpu.make_async_copy(source, target_ref, load_sems.at[len(loads)])

    def start(*group):
        for name in group:
            loads[name].start()

    load("qkv", qkv_hbm, attn_qkv)
    load("scale", scale_hbm, cond_scale)
    load("shift", shift_hbm, cond_shift)
    load("attn_out", attn_out_hbm, attn_out)
    load("dec_kv", dec_kv_hbm, dec_kv)
    load("query", query_hbm, query_t)
    load("logits", logits_hbm, grid_logits)
    load("embed", embed_hbm, embed_t)
    load("dec_out", dec_out_hbm, dec_out)
    load("head", head_hbm, head_out)
    load("weather", weather_hbm.at[:, here], weather)
    load("target", target_hbm.at[:, here], target)
    load("area", area_hbm.at[:, here], area)
    load("norm", norm_hbm, norm_t)
    start("qkv", "scale", "shift")

    odd = is_odd()
    far = slice(size, size + halo)
    latent[0:halo] = jnp.where(odd, relay[halo:rows], beside[far])
    latent[halo : halo + rows] = jnp.where(odd, twin[:rows], beside[:rows])
    latent[halo + rows : halo + 2 * rows] = own
    latent[halo + 2 * rows : halo + 3 * rows] = jnp.where(odd, beside[:rows], twin[:rows])
    latent[halo + 3 * rows :] = jnp.where(odd, beside[far], relay[:halo])
    lane = lax.broadcasted_iota(jnp.int32, (edges.shape[0], rows), 1)
    late = (lane >= halo) == odd
    ends = jnp.where(
        jnp.concatenate([late] * 4, axis=1),
        twin[rows:size].astype(F32),
        beside[rows:size].astype(F32),
    )
    lists = edges.astype(F32)

    def listed(part):
        return [
            lists[:, part * rows : (part + 1) * rows],
            pltpu.roll(ends[:, part * rows : (part + 1) * rows], halo, 1),
        ]

    list_slots[...] = jnp.concatenate(listed(0), axis=1).astype(jnp.int32)
    list_bias[...] = joined_terms(*(jnp.concatenate(listed(part), axis=1) for part in (1, 2, 3)))
    for part in range(2):
        lanes = slice(part * rows, (part + 1) * rows)
        mesh_logits[:, lanes] = spread_bias(list_slots[:, lanes], list_bias[:, lanes], window)

    noise_rows = jnp.where(odd, relay[size + halo :], beside[size + halo :])
    noise_row = joined_terms(
        *(noise_rows[:, part * rows : (part + 1) * rows] for part in (0, 1, 2))
    )
    spread = cond_scale.shape[0]
    own_row = jnp.concatenate([noise_own[...], jnp.zeros((1, rows - spread), F32)], axis=1)
    noise = []
    for m, row in enumerate((own_row, noise_row[:1])):
        columns = jnp.broadcast_to(row, (rows, rows)).T[:spread]
        noise_out[m] = columns
        noise.append(columns[:, :1])
    is_before = lax.broadcasted_iota(jnp.int32, (window, rows), 1) < halo
    inner = slice(rows, rows + window)

    def compact(full):
        return full[inner, :rows], jnp.where(is_before, full[:window, rows:], full[window:, rows:])

    def spread_out(target_ref, middle, ends):
        target_ref[inner, :rows] = middle.astype(BF16)
        target_ref[:window, rows:] = jnp.where(is_before, ends, 0.0).astype(BF16)
        target_ref[window:, rows:] = jnp.where(is_before, 0.0, ends).astype(BF16)

    def tile_of(index, size=TILE, base=0):
        if isinstance(index, int):
            return slice(base + index * size, base + (index + 1) * size)
        return pl.ds(pl.multiple_of(base + index * size, size), size)

    @each(members * heads)
    def _(i):
        mesh_probs[i, :rows, :rows] = jnp.zeros((rows, rows), BF16)
        mesh_probs[i, rows + window :, :rows] = jnp.zeros((rows, rows), BF16)
        mesh_grad_scores[i, :rows, :rows] = jnp.zeros((rows, rows), BF16)
        mesh_grad_scores[i, rows + window :, :rows] = jnp.zeros((rows, rows), BF16)

    loads["scale"].wait()
    loads["shift"].wait()
    gains = []
    shifts = []
    for m in range(members):
        gains.append(1.0 + jnp.sum(noise[m] * cond_scale[...], axis=0, keepdims=True))
        shifts.append(jnp.sum(noise[m] * cond_shift[...], axis=0, keepdims=True))
        affine[2 * m : 2 * m + 1] = gains[m]
        affine[2 * m + 1 : 2 * m + 2] = shifts[m]

    @each(outer // rows)
    def _(i):
        tile = tile_of(i, rows)
        unit = normalize(latent[tile, :].astype(F32), 1)[0]
        units[tile, :] = unit.astype(BF16)
        unit_t[:dim, tile] = unit.astype(BF16).T
        for m in range(members):
            act = unit * affine[2 * m : 2 * m + 1] + affine[2 * m + 1 : 2 * m + 2]
            acts[tile_of(i, rows, m * outer), :] = act.astype(BF16)

    latent_q[...] = window_order(latent, rows, halo)
    unit_q_t[:dim] = window_order(units, rows, halo).T
    unit_q_t[dim:] = jnp.ones((16, window), BF16)
    unit_t[dim:] = jnp.ones((16, outer), BF16)
    for m in range(members):
        acts_q[m * window : (m + 1) * window] = window_order(
            acts.at[m * outer : (m + 1) * outer], rows, halo
        )

    start("attn_out", "dec_kv")
    loads["qkv"].wait()
    start("query", "logits", "embed", "dec_out", "head", "weather", "target", "area", "norm")

    @each(dim // TILE)
    def _(i):
        part = nn(acts_q[...], attn_qkv[:, tile_of(i)]).astype(BF16)
        mesh_query[tile_of(i), :] = part.T

    @each(2 * dim // TILE)
    def _(i):
        mesh_kv[:, tile_of(i)] = nn(acts[...], attn_qkv[:, tile_of(i, TILE, dim)]).astype(BF16)

    pairs = [(m * heads + h, m, h) for m in range(members) for h in range(heads)]

    def span(index, size, base=0):
        return slice(base + index * size, base + (index + 1) * size)

    for i, m, h in pairs:
        keys = mesh_kv[span(m, outer), span(h, HEAD)]
        middle, ends = compact(nn(keys, mesh_query[span(h, HEAD), span(m, window)]))
        scores[i, :, :rows] = middle
        scores[i, :, rows:window] = ends

    @each(members * heads)
    def _(i):
        parts = [
            softmax_rows(scores[i, :, lanes] * inv_sqrt + mesh_logits[:, lanes])
            for lanes in (span(0, rows), span(1, rows))
        ]
        spread_out(mesh_probs.at[i], *parts)

    for i, m, h in pairs:
        values = mesh_kv[span(m, outer), span(h, HEAD, dim)]
        mesh_mixed[span(h, HEAD), span(m, window)] = tn(values, mesh_probs[i]).astype(BF16)

    loads["attn_out"].wait()

    @each(members)
    def _(m):
        here_q = tile_of(m, window)
        mixed = mesh_mixed[:, here_q].T
        out = (latent_q[...].astype(F32) + nn(mixed, attn_out[...])).astype(BF16)
        mesh_out[here_q, :] = out
        norm = normalize(out.astype(F32), 1)[0].astype(BF16)
        mesh_norm[here_q, :] = norm
        mesh_norm_t[:, here_q] = norm.T

    loads["dec_kv"].wait()

    @each(2 * dim // TILE)
    def _(i):
        dec_keys[:, tile_of(i)] = nn(mesh_norm[...], dec_kv[:, tile_of(i)]).astype(BF16)

    for name in ("query", "logits", "embed", "dec_out", "head"):
        loads[name].wait()
    head_pad[...] = jnp.zeros_like(head_pad)
    head_pad[:channels] = head_out[...]
    head_t[...] = head_pad[...].T
    dec_out_t[...] = dec_out[...].T

    for i, m, h in pairs:
        scores[i] = nn(dec_keys[span(m, window), span(h, HEAD)], query_t[span(h, HEAD), :])

    @each(members * heads)
    def _(i):
        for t in range(slots // HEAD):
            lanes = span(t, HEAD)
            probs = softmax_rows(scores[i, :, lanes] * inv_sqrt + grid_logits[:, lanes])
            grid_probs[i, :, lanes] = probs.astype(BF16)

    for i, m, h in pairs:
        values = dec_keys[span(m, window), span(h, HEAD, dim)]
        grid_mixed[span(h, HEAD), span(m, slots)] = tn(values, grid_probs[i]).astype(BF16)

    for m in range(members):
        out = embed_t[...].astype(F32) + nn(dec_out_t[...], grid_mixed[:, span(m, slots)])
        grid_out[:, span(m, slots)] = out.astype(BF16)

    lane_tiles = members * slots // HEAD

    @each(lane_tiles)
    def _(i):
        tile = tile_of(i, HEAD)
        final = normalize(grid_out[:, tile].astype(F32), 0)[0].astype(BF16)
        grid_final[:, tile] = final

    change[...] = nn(head_pad[...], grid_final[...])

    for name in ("weather", "target", "area", "norm"):
        loads[name].wait()
    def smooth(values):
        square = values * values + SMOOTHING
        inverse = lax.rsqrt(square)
        return square * inverse, values * inverse

    grad_change[...] = jnp.zeros_like(grad_change)

    def compare(i, loss):
        tile = tile_of(i, HEAD)
        slot = lax.broadcasted_iota(jnp.int32, (1, HEAD), 1) + (member * slots + i * HEAD)
        live = jnp.where(slot < counts[0], 1.0, 0.0)
        weighting = live * area[:, tile]
        second_tile = tile_of(i, HEAD, slots)
        first = weather[:, tile] + live * change[:channels, tile]
        second = weather[:, tile] + live * change[:channels, second_tile]
        pred[0, :, tile] = first
        pred[1, :, tile] = second
        size_first, slope_first = smooth(first - target[:, tile])
        size_second, slope_second = smooth(second - target[:, tile])
        size_pair, slope_pair = smooth(first - second)
        factor = weighting * (LOSS_SCALE / scale_den)
        grad_change[:channels, tile] = (factor * (slope_first - slope_pair)).astype(BF16)
        grad_change[:channels, second_tile] = (factor * (slope_second + slope_pair)).astype(BF16)
        terms = weighting * (size_first + size_second - size_pair)
        return loss + jnp.sum(terms, axis=0, keepdims=True)

    loss = lax.fori_loop(0, slots // HEAD, compare, jnp.zeros((1, HEAD), F32))
    loss = jnp.sum(loss) / scale_den
    stores = [
        pltpu.make_async_copy(pred.at[0], pred_own_hbm, store_sems.at[0]),
        pltpu.make_async_copy(pred.at[1], pred_other_hbm, store_sems.at[1]),
    ]
    for store in stores:
        store.start()

    tall = HEAD * HEAD // dim
    per_block = dim // tall

    def pack(index, tile, block):
        half, chunk = index // 4, index % 4 * per_block
        for c in range(per_block):
            for t in range(TILE // HEAD):
                where = tile_of(tile * (TILE // HEAD) + t, tall)
                part = block[c * tall : (c + 1) * tall, t * HEAD : (t + 1) * HEAD]
                grads[half, chunk + c, where, :] = part.astype(BF16)

    col_tiles = dim // TILE

    def pack_extras(half, chunk, values):
        for i in range(values.shape[0] // 8):
            for t in range(heads):
                grads[half, chunk + i * heads + t, HEAD:, :] = values[
                    i * 8 : (i + 1) * 8, t * HEAD : (t + 1) * HEAD
                ].astype(BF16)

    def ship(half, first, last, sem):
        source = grads.at[half, first:last]
        keep = pltpu.make_async_copy(source, keep_hbm.at[first:last], store_sems.at[sem])
        send = pltpu.make_async_copy(source, send_hbm.at[first:last], store_sems.at[sem])
        pl.when(core == half)(keep.start)
        pl.when(core != half)(send.start)
        stores.append(keep)

    grads[:, :, HEAD:, :] = jnp.zeros((2, 4 * per_block, 8, HEAD), BF16)

    pack_extras(1, 0, nt(grad_change[...], grid_final[...]))

    @each(lane_tiles)
    def _(i):
        tile = tile_of(i, HEAD)
        g_final = nn(head_t[...], grad_change[:, tile])
        g_out = normalize_back(grid_out[:, tile].astype(F32), g_final, 0).astype(BF16)
        grid_grad_out[:, tile] = g_out

    for m in range(members):
        g_mixed = nn(dec_out[...], grid_grad_out[:, span(m, slots)])
        grid_grad_mixed[:, span(m, slots)] = g_mixed.astype(BF16)

    @each(col_tiles)
    def _(i):
        pack(7, i, nt(grid_mixed[...], grid_grad_out[tile_of(i), :]))

    for i, m, h in pairs:
        values = dec_keys[span(m, window), span(h, HEAD, dim)]
        scores[i] = nn(values, grid_grad_mixed[span(h, HEAD), span(m, slots)])

    @each(members * heads)
    def _(i):
        here = tile_of(i % heads * members + i // heads, window)
        for t in range(slots // HEAD):
            lanes = span(t, HEAD)
            grid_grad_scores[here, lanes] = score_back(
                grid_probs[i, :, lanes], scores[i, :, lanes]
            ).astype(BF16)

    for i, m, h in pairs:
        g_scores = grid_grad_scores[span(h * members + m, window), :]
        g_head = grid_grad_mixed[span(h, HEAD), span(m, slots)]
        probs = grid_probs[i]
        grad_dec[span(m, window), span(h, HEAD)] = nt(g_scores, query_t[span(h, HEAD), :]).astype(BF16)
        grad_dec[span(m, window), span(h, HEAD, dim)] = nt(probs, g_head).astype(BF16)
    for h in range(heads):
        keys = dec_keys[:, span(h, HEAD)]
        g_scores = grid_grad_scores[span(h, members * window), :]
        grad_query[span(h, HEAD), :] = tn(keys, g_scores).astype(BF16)

    @each(col_tiles)
    def _(i):
        pack(4, i, nt(norm_t[...], grad_query[tile_of(i), :]))

    @each(2 * col_tiles)
    def _(i):
        block = nn(mesh_norm_t[...], grad_dec[:, tile_of(i)])
        pack(5 + i // col_tiles, i % col_tiles, block)

    ship(1, 0, 4 * per_block, 2)

    @each(members)
    def _(m):
        here_q = tile_of(m, window)
        g_norm = nt(grad_dec[here_q, :], dec_kv[...])
        g_out = normalize_back(mesh_out[here_q, :].astype(F32), g_norm, 1).astype(BF16)
        mesh_grad_out[here_q, :] = g_out
        mesh_grad_mixed[:, here_q] = nt(attn_out[...], g_out).astype(BF16)

    @each(col_tiles)
    def _(i):
        pack(3, i, nn(mesh_mixed[...], mesh_grad_out[:, tile_of(i)]))

    for i, m, h in pairs:
        values = mesh_kv[span(m, outer), span(h, HEAD, dim)]
        middle, ends = compact(nn(values, mesh_grad_mixed[span(h, HEAD), span(m, window)]))
        scores[i, :, :rows] = middle
        scores[i, :, rows:window] = ends

    @each(members * heads)
    def _(i):
        parts = [
            score_back(probs, scores[i, :, lanes])
            for probs, lanes in zip(compact(mesh_probs[i]), (span(0, rows), span(1, rows)))
        ]
        spread_out(mesh_grad_scores.at[i], *parts)

    for i, m, h in pairs:
        cols = span(h, HEAD)
        g_scores = mesh_grad_scores[i]
        g_head = mesh_grad_mixed[cols, span(m, window)]
        g_query = tn(mesh_kv[span(m, outer), cols], g_scores).astype(BF16)
        grad_q[span(m, window), cols] = g_query.T
        grad_kv[span(m, outer), cols] = nt(g_scores, mesh_query[cols, span(m, window)]).astype(BF16)
        grad_kv[span(m, outer), span(h, HEAD, dim)] = nt(mesh_probs[i], g_head).astype(BF16)

    for m in range(members):
        gain_col = jnp.broadcast_to(gains[m], (HEAD, dim)).T
        shift_col = jnp.broadcast_to(shifts[m], (HEAD, dim)).T
        affine_t[2 * m] = gain_col
        affine_t[2 * m + 1] = shift_col
    sums[...] = jnp.zeros_like(sums)
    col_sums[...] = jnp.zeros_like(col_sums)

    def project_back(index, tile, weight_tile, left, parts):
        weight = attn_qkv[:, weight_tile].astype(F32)
        total = None
        for m in range(members):
            moment = nn(left[...], parts[m])
            col_sum = moment[dim : dim + 1]
            moment = moment[:dim]
            high, middle, low = split_terms(col_sum)
            for row, value in enumerate((high, middle, low)):
                col_sums[8 * m + row : 8 * m + row + 1, weight_tile] = value.astype(F32)
            by_gain = weight * moment
            sums[m] += by_gain[:, :HEAD] + by_gain[:, HEAD:]
            terms = []
            for t in range(TILE // HEAD):
                lanes = slice(t * HEAD, (t + 1) * HEAD)
                terms.append(
                    affine_t[2 * m] * moment[:, lanes] + affine_t[2 * m + 1] * col_sum[:, lanes]
                )
            term = jnp.concatenate(terms, axis=1)
            total = term if m == 0 else total + term
        pack(index, tile, total)

    @each(2 * col_tiles)
    def _(i):
        parts = [grad_kv[m * outer : (m + 1) * outer, tile_of(i)] for m in range(members)]
        project_back(
            1 + i // col_tiles, i % col_tiles, tile_of(i, TILE, dim), unit_t, parts
        )

    ship(0, per_block, 4 * per_block, 3)

    @each(col_tiles)
    def _(i):
        parts = [grad_q[m * window : (m + 1) * window, tile_of(i)] for m in range(members)]
        project_back(0, i, tile_of(i), unit_q_t, parts)

    row_id = lax.broadcasted_iota(jnp.int32, (8, dim), 0)
    grad_cond = jnp.where(row_id == 4, loss, 0.0)
    g_shifts = nt(attn_qkv[...], col_sums[...].astype(BF16))
    for m in range(members):
        mine = member if m == 0 else 1 - member
        g_shift = g_shifts[:, 8 * m : 8 * m + 3]
        for row, lanes in ((mine, sums[m]), (mine + 2, g_shift)):
            column = jnp.sum(lanes, axis=1, keepdims=True)
            values = jnp.broadcast_to(column, (dim, HEAD)).T[:8]
            grad_cond += jnp.where(row_id == row, values, 0.0)
    pack_extras(0, 0, grad_cond)
    ship(0, 0, per_block, 4)
    for store in stores:
        store.wait()


def sum_kernel(parts, pred_own_hbm, pred_arrived_hbm, result, pred_hbm, sems):
    slots = pred_own_hbm.shape[1]
    member = lax.axis_index("member")
    here = pl.ds(pl.multiple_of(member * slots, slots), slots)
    there = pl.ds(pl.multiple_of((1 - member) * slots, slots), slots)
    copies = [
        pltpu.make_async_copy(pred_own_hbm, pred_hbm.at[0, :, here], sems.at[0]),
        pltpu.make_async_copy(pred_arrived_hbm, pred_hbm.at[0, :, there], sems.at[1]),
    ]
    for copy in copies:
        copy.start()
    total = jnp.sum(parts[...].astype(F32), axis=0, keepdims=True)
    result[...] = jnp.broadcast_to(total.astype(BF16), result.shape)
    for copy in copies:
        copy.wait()


def unpack_kernel(*refs, own_half):
    data, noise = refs[:2]
    outputs, scratch = (refs[2:11], refs[11:]) if own_half else (refs[11:20], refs[20:])
    grad_scale, grad_shift, grad_qkv, grad_attn_out = outputs[:4]
    grad_dec_query, grad_dec_kv, grad_dec_out, grad_head, loss = outputs[4:]
    blocks, cond, head, tail, sems = scratch
    member = lax.axis_index("member")
    core = lax.rem(lax.axis_index("space"), 2)
    half = core if own_half else 1 - core
    channels, dim = grad_head.shape
    heads = dim // HEAD
    tall = HEAD * HEAD // dim
    per_block = dim // tall
    targets = (
        (
            grad_qkv.at[:, :dim],
            grad_qkv.at[:, dim : 2 * dim],
            grad_qkv.at[:, 2 * dim :],
            grad_attn_out,
        ),
        (grad_dec_query, grad_dec_kv.at[:, :dim], grad_dec_kv.at[:, dim:], grad_dec_out),
    )

    def block_copy(which, i):
        return pltpu.make_async_copy(blocks.at[i], targets[which][i], sems.at[i])

    for i in range(4):

        @pl.loop(0, per_block, unroll=2)
        def _(c):
            tile = pl.ds(pl.multiple_of(c * tall, tall), tall)
            for t in range(heads):
                blocks[i, tile, t * HEAD : (t + 1) * HEAD] = data[
                    i * per_block + c, t * tall : (t + 1) * tall, :
                ].astype(F32)

        for which in range(2):
            pl.when(half == which)(block_copy(which, i).start)

    def extra(i):
        return jnp.concatenate(
            [data[i * heads + t, HEAD:, :].astype(F32) for t in range(heads)], axis=1
        )

    @pl.when(half == 0)
    def _():
        sums = extra(0)
        for k in range(2):
            first = sums[2 * k : 2 * k + 1]
            second = sums[2 * k + 1 : 2 * k + 2]
            mine = jnp.where(member == 0, first, second)
            other = jnp.where(member == 0, second, first)
            cond[k] = noise[0, :, :1] * mine + noise[1, :, :1] * other
        tail[...] = sums[4:5, :HEAD]
        copies = [
            pltpu.make_async_copy(cond.at[0], grad_scale, sems.at[4]),
            pltpu.make_async_copy(cond.at[1], grad_shift, sems.at[5]),
            pltpu.make_async_copy(tail, loss, sems.at[6]),
        ]
        for copy in copies:
            copy.start()
        for copy in copies:
            copy.wait()

    @pl.when(half == 1)
    def _():
        for i in range(-(-channels // 8)):
            count = min(8, channels - i * 8)
            head[i * 8 : i * 8 + count] = extra(i)[:count]
        copy = pltpu.make_async_copy(head, grad_head, sems.at[4])
        copy.start()
        copy.wait()

    for i in range(4):
        for which in range(2):
            pl.when(half == which)(block_copy(which, i).wait)


def whole(shape):
    return pl.BlockSpec(shape, lambda *_: (0,) * len(shape))


def per_device(
    mesh_latent,
    grid_embed,
    weather_state,
    target,
    cell_area,
    member_noise,
    mesh_nbrs,
    mesh_bias,
    grid_nbrs,
    grid_bias,
    grid_counts,
    cond_scale,
    cond_shift,
    attn_qkv,
    attn_out,
    dec_query,
    dec_kv,
    dec_out,
    head_out,
):
    rows, dim = mesh_latent.shape
    halo = rows // 2
    window = rows + 2 * halo
    outer = 2 * window
    size = lax.axis_size("space")
    grid_slots = grid_embed.shape[0]
    slots = grid_slots // 2
    channels = weather_state.shape[0]
    total = rows * size
    heads = dim // HEAD
    noise_size = member_noise.shape[1]
    entries = grid_nbrs.shape[0]
    scale_den = 2.0 * channels * grid_slots * size

    axes = ("member", "space")

    def permute(value, target_of):
        pairs = []
        for m in range(2):
            for k in range(size):
                to_m, to_k = target_of(m, k)
                pairs.append((m * size + k, to_m * size + to_k % size))
        return lax.ppermute(value, axes, pairs)

    smem = pl.BlockSpec(memory_space=pltpu.SMEM)
    vmem = pl.BlockSpec(memory_space=pltpu.VMEM)
    hbm = pl.BlockSpec(memory_space=pltpu.HBM)
    packet = pl.pallas_call(
        lambda *refs: pack_kernel(*refs, total=total),
        in_specs=[vmem] * 3,
        out_shape=jax.ShapeDtypeStruct((rows + mesh_nbrs.shape[0], dim), BF16),
        compiler_params=pltpu.CompilerParams(vmem_limit_bytes=ALL_VMEM),
        name="pack",
    )(mesh_latent, mesh_nbrs, mesh_bias)
    twin = permute(packet, lambda m, k: (m, k ^ 1))
    outward = pl.pallas_call(
        lambda *refs: outward_kernel(*refs, rows=rows),
        in_specs=[vmem] * 3,
        out_shape=jax.ShapeDtypeStruct((packet.shape[0] + halo + 16, dim), BF16),
        compiler_params=pltpu.CompilerParams(vmem_limit_bytes=32 * 2**20),
        name="outward",
    )(packet, twin, member_noise)
    beside = permute(outward, lambda m, k: (1 - m, k + 1) if k % 2 else (m, k - 1))

    square = (dim, slots)
    embed_t, norm_t, query_t, grid_logits = pl.pallas_call(
        lambda *refs: prepare_kernel(*refs, rows=rows, halo=halo, total=total),
        in_specs=[hbm] * 5,
        out_specs=[vmem] * 4,
        out_shape=[
            jax.ShapeDtypeStruct(square, BF16),
            jax.ShapeDtypeStruct(square, BF16),
            jax.ShapeDtypeStruct(square, BF16),
            jax.ShapeDtypeStruct((window, slots), F32),
        ],
        scratch_shapes=[
            pltpu.VMEM((slots, dim), BF16),
            pltpu.VMEM((entries, slots), jnp.int32),
            pltpu.VMEM((entries, slots), F32),
            pltpu.VMEM((dim, dim), BF16),
            pltpu.VMEM((dim, dim), BF16),
            pltpu.SemaphoreType.DMA((4,)),
        ],
        compiler_params=pltpu.CompilerParams(vmem_limit_bytes=ALL_VMEM),
        cost_estimate=pl.CostEstimate(
            flops=2 * dim * dim * slots, bytes_accessed=3 * 2**20, transcendentals=0
        ),
        name="prepare",
    )(grid_embed, grid_nbrs, grid_bias, dec_query, outward)
    beside, embed_t = lax.optimization_barrier((beside, embed_t))
    relay = permute(beside, lambda m, k: (m, k ^ 1))

    channel_pad = -(-channels // 32) * 32
    chunks = size
    half_shape = (chunks, HEAD + 8, HEAD)
    step_in = (
        packet,
        twin,
        beside,
        relay,
        member_noise,
        embed_t,
        norm_t,
        query_t,
        grid_logits,
        weather_state,
        target,
        cell_area[None, :],
        cond_scale,
        cond_shift,
        attn_qkv,
        attn_out,
        dec_kv,
        dec_out,
        head_out,
    )
    pred_own, pred_other, keep, send, noise = pl.pallas_call(
        lambda *refs: step_kernel(*refs, rows=rows, scale_den=scale_den),
        in_specs=[smem] + [vmem] * 5 + [pl.BlockSpec(memory_space=pl.ANY)] * 4 + [hbm] * 10,
        out_specs=[hbm] * 4 + [vmem],
        scratch_shapes=[
            pltpu.VMEM(square, BF16),
            pltpu.VMEM(square, BF16),
            pltpu.VMEM(square, BF16),
            pltpu.VMEM((window, slots), F32),
            pltpu.VMEM((channels, slots), F32),
            pltpu.VMEM((channels, slots), F32),
            pltpu.VMEM((1, slots), F32),
            pltpu.VMEM(cond_scale.shape, F32),
            pltpu.VMEM(cond_shift.shape, F32),
            pltpu.VMEM(attn_qkv.shape, BF16),
            pltpu.VMEM(attn_out.shape, BF16),
            pltpu.VMEM(dec_kv.shape, BF16),
            pltpu.VMEM(dec_out.shape, BF16),
            pltpu.VMEM(head_out.shape, BF16),
            pltpu.VMEM((2, channels, slots), F32),
            pltpu.VMEM((2, *half_shape), BF16),
            pltpu.VMEM((outer, dim), BF16),
            pltpu.VMEM((window, dim), BF16),
            pltpu.VMEM((outer, dim), BF16),
            pltpu.VMEM((2 * outer, dim), BF16),
            pltpu.VMEM((2 * window, dim), BF16),
            pltpu.VMEM((8, dim), F32),
            pltpu.VMEM((4, dim, HEAD), F32),
            pltpu.VMEM((2, dim, HEAD), F32),
            pltpu.VMEM((16, 3 * dim), F32),
            pltpu.VMEM((2 * heads, window, slots), F32),
            pltpu.VMEM((dim + 16, outer), BF16),
            pltpu.VMEM((dim + 16, window), BF16),
            pltpu.VMEM((mesh_nbrs.shape[0], window), jnp.int32),
            pltpu.VMEM((mesh_nbrs.shape[0], window), F32),
            pltpu.VMEM((window, window), F32),
            pltpu.VMEM((dim, 2 * window), BF16),
            pltpu.VMEM((2 * outer, 2 * dim), BF16),
            pltpu.VMEM((2 * heads, outer, window), BF16),
            pltpu.VMEM((2 * heads, outer, window), BF16),
            pltpu.VMEM((dim, 2 * window), BF16),
            pltpu.VMEM((dim, 2 * window), BF16),
            pltpu.VMEM((2 * window, dim), BF16),
            pltpu.VMEM((2 * window, dim), BF16),
            pltpu.VMEM((2 * window, dim), BF16),
            pltpu.VMEM((dim, 2 * window), BF16),
            pltpu.VMEM((2 * window, 2 * dim), BF16),
            pltpu.VMEM((2 * heads, window, slots), BF16),
            pltpu.VMEM((2 * heads * window, slots), BF16),
            pltpu.VMEM((dim, 2 * slots), BF16),
            pltpu.VMEM((dim, 2 * slots), BF16),
            pltpu.VMEM((dim, 2 * slots), BF16),
            pltpu.VMEM((dim, 2 * slots), BF16),
            pltpu.VMEM((dim, 2 * slots), BF16),
            pltpu.VMEM((channel_pad, 2 * slots), F32),
            pltpu.VMEM((channel_pad, 2 * slots), BF16),
            pltpu.VMEM((channel_pad, dim), BF16),
            pltpu.VMEM((dim, channel_pad), BF16),
            pltpu.VMEM((dim, dim), BF16),
            pltpu.VMEM((dim, slots), BF16),
            pltpu.VMEM((2 * window, 2 * dim), BF16),
            pltpu.VMEM((2 * window, dim), BF16),
            pltpu.VMEM((2 * outer, 2 * dim), BF16),
            pltpu.SemaphoreType.DMA((14,)),
            pltpu.SemaphoreType.DMA((5,)),
        ],
        out_shape=[
            jax.ShapeDtypeStruct((channels, slots), F32),
            jax.ShapeDtypeStruct((channels, slots), F32),
            jax.ShapeDtypeStruct(half_shape, BF16),
            jax.ShapeDtypeStruct(half_shape, BF16),
            jax.ShapeDtypeStruct((2, noise_size, rows), F32),
        ],
        compiler_params=pltpu.CompilerParams(vmem_limit_bytes=ALL_VMEM),
        cost_estimate=pl.CostEstimate(
            flops=10**10, bytes_accessed=12 * 2**20, transcendentals=2**21
        ),
        name="step",
    )(grid_counts, *step_in)

    def twin_swap(value):
        return permute(value, lambda m, k: (m, k ^ 1))

    groups = [
        [m * size + k for m in range(2) for k in range(size) if k % 2 == c] for c in range(2)
    ]

    def over_chips(value):
        return lax.all_to_all(value, axes, 0, 0, axis_index_groups=groups)

    arrived_pred = permute(pred_other, lambda m, k: (1 - m, k))
    pair = (keep.astype(F32) + twin_swap(send).astype(F32)).astype(BF16)
    pair, arrived_pred = lax.optimization_barrier((pair, arrived_pred))
    parts = over_chips(pair)
    shared, prediction = pl.pallas_call(
        sum_kernel,
        in_specs=[vmem, hbm, hbm],
        out_specs=[vmem, hbm],
        out_shape=[
            jax.ShapeDtypeStruct(half_shape, BF16),
            jax.ShapeDtypeStruct((1, channels, grid_slots), F32),
        ],
        scratch_shapes=[pltpu.SemaphoreType.DMA((2,))],
        compiler_params=pltpu.CompilerParams(vmem_limit_bytes=32 * 2**20),
        name="sum",
    )(parts, pred_own, arrived_pred)
    mine = over_chips(shared)
    theirs = twin_swap(mine)
    grad_shapes = [
        jax.ShapeDtypeStruct(shape, F32)
        for shape in (
            cond_scale.shape,
            cond_shift.shape,
            attn_qkv.shape,
            attn_out.shape,
            dec_query.shape,
            dec_kv.shape,
            dec_out.shape,
            head_out.shape,
            (1, HEAD),
        )
    ]
    anywhere = pl.BlockSpec(memory_space=pl.ANY)

    def unpack(own_half, data, outputs):
        return pl.pallas_call(
            lambda *refs: unpack_kernel(*refs, own_half=own_half),
            in_specs=[vmem, vmem] + [anywhere] * len(outputs),
            out_specs=[anywhere] * 9,
            out_shape=grad_shapes,
            scratch_shapes=[
                pltpu.VMEM((4, dim, dim), F32),
                pltpu.VMEM((2, *cond_scale.shape), F32),
                pltpu.VMEM(head_out.shape, F32),
                pltpu.VMEM((1, HEAD), F32),
                pltpu.SemaphoreType.DMA((7,)),
            ],
            input_output_aliases={2 + i: i for i in range(len(outputs))},
            compiler_params=pltpu.CompilerParams(vmem_limit_bytes=32 * 2**20),
            cost_estimate=pl.CostEstimate(
                flops=0, bytes_accessed=7 * 2**20, transcendentals=0
            ),
            name="unpack_mine" if own_half else "unpack_theirs",
        )(data, noise, *outputs)

    outputs = unpack(True, mine, ())
    outputs = unpack(False, theirs, tuple(outputs))
    return (prediction, *outputs[:8], outputs[8][0, 0])


def solution(mesh):
    in_specs = (
        P("space", None),
        P("space", None),
        P(None, "space"),
        P(None, "space"),
        P("space"),
        P("member", None),
        P(None, "space"),
        P(None, "space"),
        P(None, "space"),
        P(None, "space"),
        P("space"),
        P(),
        P(),
        P(),
        P(),
        P(),
        P(),
        P(),
        P(),
    )
    out_specs = (P("member", None, "space"), P(), P(), P(), P(), P(), P(), P(), P(), P())
    return jax.shard_map(
        per_device, mesh=mesh, in_specs=in_specs, out_specs=out_specs, check_vma=False
    )
```
